32 devices in a mesh: doc: 4 (over z), fsdp: 8 (over y, x, core).
Axes of the slice: x: 2, y: 2, z: 4, core: 2. Of those that a mesh axis runs over, the one named last changes fastest.
Arguments:
- tokens_in: bfloat16 [4, 256, 4096], P('doc'), may hold values from -6 to 6
- mix_in: bfloat16 [4, 256, 8192], P('doc', None, 'fsdp'), may hold values from -6 to 6
- step_size: float32 [4, 256, 128], P('doc', None, 'fsdp'), may hold values from 0.0025 to 0.03
- doc_ids: int32 [4, 256], P('doc'), may hold values from 0 to 3, never falling along the last dimension, each value on 1 to 128 neighbouring positions
- out_grad: bfloat16 [4, 256, 8192], P('doc', None, 'fsdp'), may hold values from -6 to 6
- proj_weight: bfloat16 [4096, 256], P('fsdp'), may hold values from -0.046875 to 0.046875
- conv_weight: float32 [4, 8192], P(None, 'fsdp'), may hold values from -3 to 3
- decay_rate: float32 [128], P('fsdp'), may hold values from 0.02 to 2.5
- carried_state: bfloat16 [4, 128, 64, 128], P(None, 'fsdp', 'doc'), may hold values from -3 to 3
- carried_conv: bfloat16 [4, 3, 128, 64], P(None, None, 'fsdp', 'doc'), may hold values from -6 to 6
- carry_from: int32 [4], replicated, may hold values from -1 to 3, as said below
Outputs:
- grad_proj: float32 [4096, 256], P(('doc', 'fsdp'))
- grad_state: bfloat16 [4, 128, 64, 128], P(None, 'fsdp', 'doc')
- grad_conv: bfloat16 [4, 3, 128, 64], P(None, None, 'fsdp', 'doc')
The draws below stay inside these ranges and needn't reach their ends.
Inputs may be any that keep to these rules, and one draw needn't show every extreme that they name: `carry_from`: each row names the slot of the previous window that its first document continues, or -1 if it starts fresh; no slot is named by two rows.
All inputs are finite; a program needn't handle non-finite values.
Results may differ from the reference program's by a relative error of at most 0.007.
Values may be sent and summed in bfloat16 or wider, within the bound.
A program may use at most 64 MiB of HBM per device.

```python
import math
import jax
import jax.numpy as jnp
import numpy as np
from jax import lax

D = 4096
LOCAL_HEADS = 128
P_SIZE = 64
N = 128
K = 4
ROW_TOKENS = 256
PACKED_ROWS = 4
DI = 8192


def draw_step_size(key, part):
    row_random_key, token_random_key = jax.random.split(key, 2)
    row_factor_scale = jnp.exp(jax.random.uniform(row_random_key, (PACKED_ROWS, 1, 1), jnp.float32, math.log(0.5), math.log(2.0)))
    token_factor_scale = jax.random.uniform(token_random_key, (PACKED_ROWS, ROW_TOKENS, LOCAL_HEADS), jnp.float32, 0.5, 1.5)
    return (0.01 * row_factor_scale * token_factor_scale).astype(jnp.float32)


def draw_decay_rate(key, part):
    key_base = jax.random.fold_in(key, 0)
    base_rate = jnp.exp(jax.random.uniform(key_base, (LOCAL_HEADS,), jnp.float32, math.log(0.08), math.log(2.5)))
    return base_rate.astype(jnp.float32)


def draw_carry_from(key, part):
    ordering = jax.random.permutation(key, PACKED_ROWS).astype(jnp.int32)
    coin_flip = jax.random.randint(jax.random.fold_in(key, 7), (PACKED_ROWS,), 0, 4)
    position = jnp.arange(PACKED_ROWS, dtype=jnp.int32)
    target = jnp.where(ordering[0] == PACKED_ROWS - 1, 1, 0)
    dropped = ((coin_flip == 0) | (position == target)) & (ordering != PACKED_ROWS - 1)
    return jnp.where(dropped, -1, ordering).astype(jnp.int32)


def spiked(values, key, source, target, shards_of, factor):
    owner, partner = [(jnp.arange(values.shape[axis_at]) // (values.shape[axis_at] // shards_of)).reshape([-1 if axis == axis_at else 1 for axis in range(values.ndim)]) for axis_at in (source, target)]
    chosen = jax.random.permutation(key, shards_of)[partner]
    strong = (owner == chosen) | (owner == (partner + shards_of // 2) % shards_of)
    return jnp.where(strong, factor * values, values)


def block_scale(rng, shape, cuts, low, top_value):
    factor_of = 1.0
    for dim, blocks in cuts:
        heights = jax.random.uniform(jax.random.fold_in(jax.random.fold_in(rng, 6), dim), (blocks,), jnp.float32, low / len(cuts), top_value / len(cuts))
        factor_of = factor_of * jnp.repeat(jnp.exp(heights), shape[dim] // blocks).reshape((-1,) + (1,) * (len(shape) - 1 - dim))
    return factor_of


def profile(amount, total, reach, lean):
    loads = [(1 << 20) // math.isqrt(standing ** lean) + 1 for standing in range(2, amount + 1)]
    surplus, counts = total - reach - (amount - 1), [1] * (amount - 1)
    while surplus > 0:
        movable = [i for i in range(amount - 1) if counts[i] < reach]
        mass, left = sum([loads[i] for i in movable]), surplus
        for i in movable:
            addition = min(reach - counts[i], max(1, left * loads[i] // mass), surplus)
            counts[i] = counts[i] + addition
            surplus = surplus - addition
    return np.array([reach] + counts)


def ragged(own_key, amount, total, limit, skew):
    if amount == 2:
        one = jax.random.randint(own_key, (), max(1, total - limit), min(limit, total - 1) + 1)
        return jnp.stack([one, total - one])
    sizes = jnp.asarray(profile(amount, total, limit, skew), jnp.int32)
    pairs = (amount - 1) // 2
    giver, taker = sizes[1:1 + 2 * pairs:2], sizes[2:2 + 2 * pairs:2]
    margin = jnp.minimum(giver - 1, limit - taker)
    moved = jax.random.randint(jax.random.fold_in(own_key, 1), (pairs,), 0, 1 << 20) % (margin + 1)
    sizes = sizes.at[1:1 + 2 * pairs:2].set(giver - moved).at[2:2 + 2 * pairs:2].set(taker + moved)
    return sizes[jax.random.permutation(jax.random.fold_in(own_key, 2), amount)]


def normal_values(stream_key, shape, scale, most, pieces=(), kind=jnp.bfloat16):
    result = jax.random.normal(stream_key, shape, jnp.float32) * scale
    if len(pieces) > 0:
        result = block_scale(stream_key, shape, pieces, -0.22, 0.18) * result
    return jnp.clip(result, min=-most, max=most).astype(kind)


def noise_with(own_key, extent, scale, bound, shards, heavy, kind=jnp.bfloat16):
    result = scale * jax.random.normal(own_key, extent, jnp.float32)
    if shards:
        result = result * block_scale(own_key, extent, shards, -0.22, 0.18)
    return jnp.clip(spiked(result, jax.random.fold_in(own_key, 3), *heavy), -bound, bound).astype(kind)


def setup_inputs(seed: int = 0) -> dict:
    splits = jax.random.split(jax.random.key(seed), 12)
    tokens_in = noise_with(splits[0], (PACKED_ROWS, ROW_TOKENS, D), 1.0, 6.0, ((0, 4),), (0, 2, 4, 2.0))
    mix_in = normal_values(splits[1], (PACKED_ROWS, ROW_TOKENS, DI), 1.0, 6.0, ((0, 4), (2, 8)))
    step_size = draw_step_size(jax.random.fold_in(splits[11], 71), 0)
    doc_ids = jax.vmap(lambda own: jnp.searchsorted(jnp.cumsum(ragged(own, 4, ROW_TOKENS, ROW_TOKENS // 2, 0)), jnp.arange(ROW_TOKENS), side="right"))(jax.random.split(splits[3], PACKED_ROWS)).reshape((PACKED_ROWS, ROW_TOKENS)).astype(jnp.int32)
    out_grad = normal_values(splits[4], (PACKED_ROWS, ROW_TOKENS, DI), 1.0, 6.0, ((0, 4), (2, 8)))
    proj_weight = normal_values(splits[5], (D, 2 * N), (4 * D) ** -0.5, 0.046875, ((0, 8),))
    conv_weight = normal_values(splits[6], (K, DI), 0.5, 3.0, ((1, 8),), jnp.float32)
    decay_rate = draw_decay_rate(jax.random.fold_in(splits[11], 71), 0)
    carried_state = normal_values(splits[8], (PACKED_ROWS, LOCAL_HEADS, P_SIZE, N), 0.5, 3.0, ((1, 8), (2, 4)))
    carried_conv = normal_values(splits[9], (PACKED_ROWS, K - 1, LOCAL_HEADS, P_SIZE), 1.0, 6.0, ((2, 8), (3, 4)))
    carry_from = draw_carry_from(jax.random.fold_in(splits[11], 71), 0)
    return dict(tokens_in=tokens_in, mix_in=mix_in, step_size=step_size, doc_ids=doc_ids, out_grad=out_grad, proj_weight=proj_weight, conv_weight=conv_weight, decay_rate=decay_rate, carried_state=carried_state, carried_conv=carried_conv, carry_from=carry_from)


def silu_slope(value):
    sigmoid_value = jax.nn.sigmoid(value)
    return sigmoid_value * (1.0 + value * (1.0 - sigmoid_value))


def conv_masks(seg_row, tap_count):
    length = seg_row.shape[0]
    opening = seg_row == seg_row[0]
    tap_masks = []
    for offset in range(tap_count):
        earlier = jnp.concatenate([jnp.full((offset,), -1, jnp.int32), seg_row[: length - offset].astype(jnp.int32)])
        inside = jnp.arange(length) >= offset
        tap_masks.append(jnp.where(inside, earlier == seg_row, opening))
    return opening, tap_masks


def row_pass(coeff, mix_row, step_row, seg_row, grad_rows, state_zero, conv_zero, conv_weight, decay_rate):
    length, channels = mix_row.shape
    head_count = step_row.shape[1]
    head_dim = channels // head_count
    tap_count = conv_weight.shape[0]
    nstate = coeff.shape[1] // 2
    opening, tap_masks = conv_masks(seg_row, tap_count)
    extended = jnp.concatenate([conv_zero, mix_row], axis=0).astype(jnp.float32)
    preact = jnp.zeros((length, channels), jnp.float32)
    for offset in range(tap_count):
        window = extended[tap_count - 1 - offset: tap_count - 1 - offset + length]
        preact = preact + jnp.where(tap_masks[offset][:, None], conv_weight[offset][None, :] * window, 0.0)
    mixed_rows = jax.nn.silu(preact).astype(jnp.bfloat16)
    values = (step_row[:, :, None] * mixed_rows.reshape(length, head_count, head_dim).astype(jnp.float32)).astype(jnp.bfloat16)
    write_coeff = coeff[:, :nstate]
    read_coeff = coeff[:, nstate:]
    scores = jnp.dot(read_coeff, write_coeff.T, preferred_element_type=jnp.float32)
    log_decay = jnp.cumsum(-(decay_rate[None, :] * step_row), axis=0).T
    lower = jnp.arange(length)[:, None] >= jnp.arange(length)[None, :]
    allowed = lower & (seg_row[:, None] == seg_row[None, :])
    spread = log_decay[:, :, None] - log_decay[:, None, :]
    decays = jnp.where(allowed[None], jnp.exp(jnp.where(allowed[None], spread, 0.0)), 0.0)
    edge_weight = jnp.where(opening[None, :], jnp.exp(log_decay), 0.0)
    weighted = (decays * scores[None]).astype(jnp.bfloat16)
    grad_heads = grad_rows.reshape(length, head_count, head_dim)
    values_grad = jnp.einsum("hts,thp->shp", weighted.astype(jnp.float32), grad_heads.astype(jnp.float32))
    products = jnp.einsum("thp,shp->hts", grad_heads.astype(jnp.float32), values.astype(jnp.float32))
    score_grad = jnp.sum(decays * products, axis=0)
    carried = jnp.einsum("thp,hpn->thn", grad_heads.astype(jnp.float32), state_zero.astype(jnp.float32))
    read_grad = jnp.dot(score_grad, write_coeff.astype(jnp.float32), precision=lax.Precision.HIGHEST)
    read_grad = read_grad + jnp.sum(edge_weight.T[:, :, None] * carried, axis=1)
    write_grad = jnp.dot(score_grad.T, read_coeff.astype(jnp.float32), precision=lax.Precision.HIGHEST)
    scaled = edge_weight.T[:, :, None] * grad_heads.astype(jnp.float32)
    state_grad = jnp.einsum("thp,tn->hpn", scaled, read_coeff.astype(jnp.float32), precision=lax.Precision.HIGHEST)
    mixed_grad = (values_grad * step_row[:, :, None]).reshape(length, channels)
    preact_grad = mixed_grad * silu_slope(preact)
    conv_rows = []
    for index_row in range(tap_count - 1):
        running = jnp.zeros((channels,), jnp.float32)
        for offset in range(tap_count - 1 - index_row, tap_count):
            position = index_row - (tap_count - 1) + offset
            running = running + jnp.where(opening[position], conv_weight[offset] * preact_grad[position], 0.0)
        conv_rows.append(running)
    conv_grad = jnp.stack(conv_rows)
    return jnp.concatenate([write_grad, read_grad], axis=1), state_grad, conv_grad


def reference(tokens_in, mix_in, step_size, doc_ids, out_grad, proj_weight, conv_weight, decay_rate, carried_state, carried_conv, carry_from):
    slot_count = carried_state.shape[0]
    row_total = tokens_in.shape[0]
    model_width = tokens_in.shape[2]
    channels = mix_in.shape[2]
    tap_count = conv_weight.shape[0]

    def one_row(running, index_row):
        source = carry_from[index_row]
        usable = source >= 0
        clipped = jnp.maximum(source, 0).astype(jnp.int32)
        state_zero = jnp.where(usable, carried_state[clipped], jnp.zeros_like(carried_state[0]))
        conv_zero = jnp.where(usable, carried_conv[clipped], jnp.zeros_like(carried_conv[0])).reshape(tap_count - 1, channels)
        coeff = jnp.dot(tokens_in[index_row], proj_weight, preferred_element_type=jnp.float32).astype(jnp.bfloat16)
        coeff_grad, state_grad, conv_grad = row_pass(coeff, mix_in[index_row], step_size[index_row], doc_ids[index_row], out_grad[index_row], state_zero, conv_zero, conv_weight, decay_rate)
        running = running + jnp.einsum("tj,tn->jn", tokens_in[index_row].astype(jnp.float32), coeff_grad, precision=lax.Precision.HIGHEST)
        return running, (state_grad.astype(jnp.bfloat16), conv_grad.astype(jnp.bfloat16))

    grad_proj, (state_grads, conv_grads) = lax.scan(one_row, jnp.zeros((model_width, proj_weight.shape[1]), jnp.float32), jnp.arange(row_total, dtype=jnp.int32))
    picker = (carry_from[:, None] == jnp.arange(slot_count, dtype=jnp.int32)[None, :]).astype(jnp.float32)
    grad_state = jnp.dot(picker.T, state_grads.reshape(row_total, -1).astype(jnp.float32), precision=lax.Precision.HIGHEST)
    grad_state = grad_state.astype(jnp.bfloat16).reshape(carried_state.shape)
    grad_conv = jnp.dot(picker.T, conv_grads.reshape(row_total, -1).astype(jnp.float32), precision=lax.Precision.HIGHEST)
    grad_conv = grad_conv.astype(jnp.bfloat16).reshape(carried_conv.shape)
    return grad_proj, grad_state, grad_conv
```

```python
import functools

import jax
import jax.numpy as jnp
from jax import lax
from jax.experimental import pallas as pl
from jax.experimental.pallas import tpu as pltpu
from jax.sharding import PartitionSpec as P


def silu_slope(value):
    sigmoid_value = jax.nn.sigmoid(value)
    return sigmoid_value * (1.0 + value * (1.0 - sigmoid_value))


def conv_masks(seg_row, tap_count):
    length = seg_row.shape[0]
    opening = seg_row == seg_row[0]
    tap_masks = []
    for offset in range(tap_count):
        earlier = jnp.concatenate([jnp.full((offset,), -1, jnp.int32), seg_row[: length - offset]])
        inside = jnp.arange(length) >= offset
        tap_masks.append(jnp.where(inside, earlier == seg_row, opening))
    return (opening, tap_masks)


def row_pass(
    coeff, mix_row, step_row, seg_row, grad_rows, state_zero, conv_zero, conv_weight, decay_rate
):
    length, channels = mix_row.shape
    head_count = step_row.shape[1]
    head_dim = channels // head_count
    tap_count = conv_weight.shape[0]
    nstate = coeff.shape[1] // 2
    opening, tap_masks = conv_masks(seg_row, tap_count)
    extended = jnp.concatenate([conv_zero, mix_row], axis=0).astype(jnp.float32)
    preact = jnp.zeros((length, channels), jnp.float32)
    for offset in range(tap_count):
        window = extended[tap_count - 1 - offset : tap_count - 1 - offset + length]
        preact = preact + jnp.where(
            tap_masks[offset][:, None], conv_weight[offset][None, :] * window, 0.0
        )
    mixed_rows = jax.nn.silu(preact).astype(jnp.bfloat16)
    values = (
        step_row[:, :, None] * mixed_rows.reshape(length, head_count, head_dim).astype(jnp.float32)
    ).astype(jnp.bfloat16)
    write_coeff = coeff[:, :nstate]
    read_coeff = coeff[:, nstate:]
    scores = jnp.dot(read_coeff, write_coeff.T, preferred_element_type=jnp.float32)
    log_decay = jnp.cumsum(-(decay_rate[None, :] * step_row), axis=0).T
    lower = jnp.arange(length)[:, None] >= jnp.arange(length)[None, :]
    allowed = lower & (seg_row[:, None] == seg_row[None, :])
    spread = log_decay[:, :, None] - log_decay[:, None, :]
    decays = jnp.where(allowed[None], jnp.exp(jnp.where(allowed[None], spread, 0.0)), 0.0)
    edge_weight = jnp.where(opening[None, :], jnp.exp(log_decay), 0.0)
    weighted = (decays * scores[None]).astype(jnp.bfloat16)
    grad_heads = grad_rows.reshape(length, head_count, head_dim)
    values_grad = jnp.einsum(
        "hts,thp->shp", weighted, grad_heads, preferred_element_type=jnp.float32
    )
    products = jnp.einsum("thp,shp->hts", grad_heads, values, preferred_element_type=jnp.float32)
    score_grad = jnp.sum(decays * products, axis=0)
    carried = jnp.einsum("thp,hpn->thn", grad_heads, state_zero, preferred_element_type=jnp.float32)
    read_grad = jnp.dot(
        score_grad, write_coeff.astype(jnp.float32), precision=lax.Precision.HIGHEST
    )
    read_grad = read_grad + jnp.sum(edge_weight.T[:, :, None] * carried, axis=1)
    write_grad = jnp.dot(
        score_grad.T, read_coeff.astype(jnp.float32), precision=lax.Precision.HIGHEST
    )
    scaled = edge_weight.T[:, :, None] * grad_heads.astype(jnp.float32)
    state_grad = jnp.einsum(
        "thp,tn->hpn", scaled, read_coeff.astype(jnp.float32), precision=lax.Precision.HIGHEST
    )
    mixed_grad = (values_grad * step_row[:, :, None]).reshape(length, channels)
    preact_grad = mixed_grad * silu_slope(preact)
    conv_rows = []
    for index_row in range(tap_count - 1):
        running = jnp.zeros((channels,), jnp.float32)
        for offset in range(tap_count - 1 - index_row, tap_count):
            position = index_row - (tap_count - 1) + offset
            running = running + jnp.where(
                opening[position], conv_weight[offset] * preact_grad[position], 0.0
            )
        conv_rows.append(running)
    conv_grad = jnp.stack(conv_rows)
    return (jnp.concatenate([write_grad, read_grad], axis=1), state_grad, conv_grad)


def shards(
    tokens_in,
    mix_in,
    step_size,
    doc_ids,
    out_grad,
    proj_weight,
    conv_weight,
    decay_rate,
    carried_state,
    carried_conv,
    carry_from,
):
    rows_dev, length, model_width = tokens_in.shape
    head_count = step_size.shape[2]
    slot_count = carried_state.shape[0]
    part_p = carried_state.shape[2]
    nstate = carried_state.shape[3]
    tap_count = conv_weight.shape[0]
    doc_count = lax.axis_size("doc")
    head_dim = part_p * doc_count
    channels = head_count * head_dim
    picker = (carry_from[:, None] == jnp.arange(slot_count, dtype=jnp.int32)[None, :]).astype(
        jnp.bfloat16
    )
    chosen_state = jnp.einsum(
        "rs,shpn->rhpn", picker, carried_state, preferred_element_type=jnp.float32
    ).astype(jnp.bfloat16)
    chosen_conv = jnp.einsum(
        "rs,skhp->rkhp", picker, carried_conv, preferred_element_type=jnp.float32
    ).astype(jnp.bfloat16)
    chosen_state = chosen_state.reshape(slot_count, head_count, part_p * nstate)
    chosen_conv = chosen_conv.reshape(slot_count, (tap_count - 1) * head_count, part_p)
    start_state, start_conv = (
        lax.all_to_all(chosen_state, "doc", split_axis=0, concat_axis=2, tiled=True),
        lax.all_to_all(chosen_conv, "doc", split_axis=0, concat_axis=2, tiled=True),
    )
    start_state = start_state.reshape(rows_dev, head_count, head_dim, nstate)
    start_conv = start_conv.reshape(rows_dev, tap_count - 1, channels)
    flattened = tokens_in.reshape(rows_dev * length, model_width)
    coeff_sum = jnp.dot(
        flattened,
        lax.all_gather(proj_weight, "fsdp", axis=0, tiled=True),
        preferred_element_type=jnp.float32,
    )
    coeff = coeff_sum.astype(jnp.bfloat16).reshape(rows_dev, length, proj_weight.shape[1])
    coeff_grad, state_grad, conv_grad = row_pass(
        coeff[0],
        mix_in[0],
        step_size[0],
        doc_ids[0],
        out_grad[0],
        start_state[0],
        start_conv[0],
        conv_weight,
        decay_rate,
    )
    coeff_grads = [coeff_grad]
    state_grads = [state_grad]
    conv_grads = [conv_grad]
    back_state = (
        jnp.stack(state_grads).astype(jnp.bfloat16).reshape(rows_dev, head_count, head_dim * nstate)
    )
    back_conv = (
        jnp.stack(conv_grads)
        .astype(jnp.bfloat16)
        .reshape(rows_dev, (tap_count - 1) * head_count, head_dim)
    )
    got_state, got_conv = (
        lax.all_to_all(back_state, "doc", split_axis=2, concat_axis=0, tiled=True),
        lax.all_to_all(back_conv, "doc", split_axis=2, concat_axis=0, tiled=True),
    )
    grad_state = jnp.einsum(
        "rs,rx->sx", picker, got_state.reshape(slot_count, -1), preferred_element_type=jnp.float32
    )
    grad_state = grad_state.astype(jnp.bfloat16).reshape(carried_state.shape)
    grad_conv = jnp.einsum(
        "rs,rx->sx", picker, got_conv.reshape(slot_count, -1), preferred_element_type=jnp.float32
    )
    grad_conv = grad_conv.astype(jnp.bfloat16).reshape(carried_conv.shape)
    coeff_flat = jnp.stack(coeff_grads).reshape(rows_dev * length, -1)
    share = lax.psum_scatter(coeff_flat, "fsdp", scatter_dimension=1, tiled=True)
    partial_cols = jnp.einsum(
        "tj,tn->jn", flattened.astype(jnp.float32), share, precision=lax.Precision.HIGHEST
    )
    summed_cols = lax.psum_scatter(partial_cols, "doc", scatter_dimension=0, tiled=True)
    grad_proj = lax.all_to_all(summed_cols, "fsdp", split_axis=0, concat_axis=1, tiled=True)
    return (grad_proj, grad_state, grad_conv)


F32 = jnp.float32
BF16 = jnp.bfloat16
MESH = pl.DeviceIdType.MESH


def dot_nn(a, b, precision=None):
    return lax.dot_general(
        a, b, (((1,), (0,)), ((), ())), precision=precision, preferred_element_type=F32
    )


def dot_nt(a, b):
    return lax.dot_general(a, b, (((1,), (1,)), ((), ())), preferred_element_type=F32)


def dot_tn(a, b):
    return lax.dot_general(a, b, (((0,), (0,)), ((), ())), preferred_element_type=F32)


def iota(shape, axis):
    return lax.broadcasted_iota(jnp.int32, shape, axis)


def layer_kernel(
    docs,
    parts,
    carry_ref,
    tokens_ref,
    mix_ref,
    step_ref,
    seg_ref,
    grad_ref,
    weight_ref,
    taps_ref,
    rate_ref,
    state_ref,
    conv_ref,
    proj_out,
    state_out,
    conv_out,
    tok_part,
    tok_cols,
    coeff_partial,
    coeff_recv,
    coeff,
    cg_partial,
    cg_recv,
    cg,
    state_send,
    state_recv,
    conv_send,
    conv_recv,
    sgrad_send,
    sgrad_recv,
    cgrad_send,
    cgrad_recv,
    fin_own,
    fin_send,
    fin_recv,
    ext,
    seg_ext,
    og_scaled,
    val_scaled,
    first_pre,
    first_scale,
    load_sem,
    part_send_sem,
    part_recv_sem,
    doc_send_sem,
    doc_recv_sem,
):
    d = lax.axis_index("doc")
    f = lax.axis_index("fsdp")
    length, channels = mix_ref.shape[1], mix_ref.shape[2]
    heads = step_ref.shape[2]
    head_dim = channels // heads
    part_p = head_dim // docs
    width = weight_ref.shape[1]
    nstate = width // 2
    slots = state_ref.shape[0]
    depth = weight_ref.shape[0]
    block = length // parts
    out_rows = proj_out.shape[0]
    taps = taps_ref.shape[0]

    loads = [
        pltpu.make_async_copy(
            tokens_ref.at[0, :, pl.ds(pl.multiple_of(f * depth, 128), depth)],
            tok_part,
            load_sem.at[0],
        )
    ]
    for q in range(docs):
        loads.append(
            pltpu.make_async_copy(
                tokens_ref.at[
                    0, :, pl.ds(pl.multiple_of((q * parts + f) * out_rows, 128), out_rows)
                ],
                tok_cols.at[:, pl.ds(q * out_rows, out_rows)],
                load_sem.at[1 + q],
            )
        )
    for load in loads:
        load.start()

    barrier = pltpu.get_barrier_semaphore()
    for j in range(1, parts):
        pl.semaphore_signal(
            barrier, inc=1, device_id=(d, lax.rem(f + j, parts)), device_id_type=MESH
        )
    for j in range(1, docs):
        pl.semaphore_signal(
            barrier, inc=1, device_id=(lax.rem(d + j, docs), f), device_id_type=MESH
        )

    def part_copy(phase, j, src, dst):
        return pltpu.make_async_remote_copy(
            src_ref=src,
            dst_ref=dst,
            send_sem=part_send_sem.at[phase, j],
            recv_sem=part_recv_sem.at[phase, j],
            device_id=(d, lax.rem(f + j, parts)),
            device_id_type=MESH,
        )

    def doc_copy(phase, j, src, dst):
        return pltpu.make_async_remote_copy(
            src_ref=src,
            dst_ref=dst,
            send_sem=doc_send_sem.at[phase, j],
            recv_sem=doc_recv_sem.at[phase, j],
            device_id=(lax.rem(d + j, docs), f),
            device_id_type=MESH,
        )

    def rows_of(owner):
        return pl.ds(pl.multiple_of(owner * block, block), block)

    for r in range(slots):
        source = carry_ref[r]
        usable = jnp.where(source >= 0, 1.0, 0.0)
        index = jnp.maximum(source, 0)
        state_send[r] = (state_ref[index].astype(F32) * usable).astype(BF16)
        conv_send[r] = (conv_ref[index].astype(F32) * usable).astype(BF16)

    loads[0].wait()
    coeff_partial[...] = dot_nn(tok_part[...], weight_ref[...])

    pl.semaphore_wait(barrier, parts - 1 + docs - 1)

    conv_copies = [
        doc_copy(0, j, conv_send.at[lax.rem(d + j, docs)], conv_recv.at[d]) for j in range(1, docs)
    ]
    coeff_copies = [
        part_copy(0, j, coeff_partial.at[rows_of(lax.rem(f + j, parts))], coeff_recv.at[j])
        for j in range(1, parts)
    ]
    state_copies = [
        doc_copy(1, j, state_send.at[lax.rem(d + j, docs)], state_recv.at[:, d])
        for j in range(1, docs)
    ]
    for copy in conv_copies + coeff_copies + state_copies:
        copy.start()
    conv_recv[d] = conv_send[d]
    state_recv[:, d] = state_send[d]

    lower = iota((length, length), 0) >= iota((length, length), 1)
    steps = step_ref[0]
    log_decay = dot_nn(
        jnp.where(lower, 1.0, 0.0), -(rate_ref[...] * steps), precision=lax.Precision.HIGHEST
    )

    def halves(x):
        top = x.astype(BF16)
        return top, (x - top.astype(F32)).astype(BF16)

    grow = halves(jnp.exp(log_decay))
    shrink = halves(jnp.exp(-log_decay))
    step_halves = halves(steps)

    seg_row = seg_ref[...].astype(F32)
    seg_cols = jnp.broadcast_to(seg_row, (128, length)).T
    seg_ext[8:, :] = seg_cols
    seg_ext[:8, :] = jnp.broadcast_to(seg_cols[:1], (8, 128))
    allowed = lower & (seg_cols[:, :1] == seg_row)
    opening = seg_cols == seg_cols[:1]

    for copy in conv_copies:
        copy.wait_recv()

    def place(q):
        lane = iota((part_p, channels), 1)
        return jnp.where(
            lax.rem(lane, head_dim) == iota((part_p, channels), 0) + q * part_p, 1.0, 0.0
        ).astype(BF16)

    places = [place(q) for q in range(docs)]
    head_rows = (taps - 1) * heads
    own_head = (
        lax.div(iota((taps - 1, heads, channels), 2), head_dim)
        == iota((taps - 1, heads, channels), 1)
    )
    spread = jnp.zeros((head_rows, channels), F32)
    for q in range(docs):
        spread = spread + dot_nn(conv_recv[q].reshape(head_rows, part_p), places[q])
    carried_rows = jnp.sum(
        jnp.where(own_head, spread.reshape(taps - 1, heads, channels), 0.0), axis=1
    )
    ext[:8, :] = jnp.zeros((8, channels), F32)
    ext[8 - (taps - 1) : 8, :] = carried_rows
    ext[8:, :] = mix_ref[0].astype(F32)

    for copy in coeff_copies:
        copy.wait_recv()
    total = coeff_partial[rows_of(f)]
    for j in range(1, parts):
        total = total + coeff_recv[j]
    coeff[rows_of(f)] = total.astype(BF16)
    gather_copies = [
        part_copy(1, j, coeff.at[rows_of(f)], coeff.at[rows_of(f)]) for j in range(1, parts)
    ]
    for copy in gather_copies:
        copy.start()

    def chunk(c, carry):
        lanes = pl.ds(pl.multiple_of(c * 128, 128), 128)
        expand = jnp.where(
            iota((heads, 128), 0) == lax.div(iota((heads, 128), 1) + c * 128, head_dim), 1.0, 0.0
        ).astype(BF16)

        def per_channel(pair):
            return dot_nn(pair[0], expand) + dot_nn(pair[1], expand)

        preact = jnp.zeros((length, 128), F32)
        for k in range(taps):
            same = seg_ext[8 - k : 8 - k + length, :] == seg_cols
            window = ext[8 - k : 8 - k + length, lanes]
            preact = preact + jnp.where(same, taps_ref[k : k + 1, lanes] * window, 0.0)
        step_c = per_channel(step_halves)
        shrink_c = per_channel(shrink)
        mixed = (preact / (1.0 + jnp.exp(-preact))).astype(BF16).astype(F32)
        values = (step_c * mixed).astype(BF16).astype(F32)
        val_scaled[:, lanes] = (values * shrink_c).astype(BF16)
        og_scaled[:, lanes] = (grad_ref[0, :, lanes].astype(F32) * per_channel(grow)).astype(BF16)
        first_pre[:, lanes] = preact[:8]
        first_scale[:, lanes] = (step_c * shrink_c)[:8]
        return carry

    lax.fori_loop(0, channels // 128, chunk, 0)
    score_grad = jnp.where(allowed, dot_nt(og_scaled[...], val_scaled[...]), 0.0).astype(BF16)

    for copy in state_copies:
        copy.wait_recv()
    from_state = jnp.where(
        opening, dot_nn(og_scaled[...], state_recv[...].reshape(channels, nstate)), 0.0
    )

    for copy in gather_copies:
        copy.wait_recv()
    write_coeff = coeff[:, :nstate]
    read_coeff = coeff[:, nstate:]
    cg_partial[:, :nstate] = dot_tn(score_grad, read_coeff)
    cg_partial[:, nstate:] = dot_nn(score_grad, write_coeff) + from_state
    sum_copies = [
        part_copy(2, j, cg_partial.at[rows_of(lax.rem(f + j, parts))], cg_recv.at[j])
        for j in range(1, parts)
    ]
    for copy in sum_copies:
        copy.start()

    open_read = jnp.where(opening, read_coeff.astype(F32), 0.0).astype(BF16)
    sgrad_send[...] = (
        dot_tn(og_scaled[...], open_read).astype(BF16).reshape(heads, docs, part_p, nstate)
    )
    sgrad_copies = [
        doc_copy(2, j, sgrad_send.at[:, lax.rem(d + j, docs)], sgrad_recv.at[d])
        for j in range(1, docs)
    ]
    for copy in sgrad_copies:
        copy.start()
    first_scores = dot_nt(write_coeff[:16], read_coeff)
    first_seg = jnp.broadcast_to(seg_row, (16, length)) == seg_cols[:16, :1]
    first_allowed = first_seg & (iota((16, length), 1) >= iota((16, length), 0))
    first_scores = jnp.where(first_allowed, first_scores, 0.0).astype(BF16)
    first_grad = dot_nn(first_scores, og_scaled[...])[:8]
    pre = first_pre[...]
    gate = 1.0 / (1.0 + jnp.exp(-pre))
    pre_grad = first_grad * first_scale[...] * gate * (1.0 + pre * (1.0 - gate))
    pre_grad = jnp.where(seg_cols[:8, :1] == seg_cols[:1, :1], pre_grad, 0.0)
    conv_rows = []
    for row in range(taps - 1):
        running = jnp.zeros((1, channels), F32)
        for k in range(taps - 1 - row, taps):
            position = row - (taps - 1) + k
            running = running + taps_ref[k : k + 1, :] * pre_grad[position : position + 1]
        conv_rows.append(
            jnp.where(own_head[0], jnp.broadcast_to(running, (heads, channels)), 0.0).astype(BF16)
        )
    for q in range(docs):
        for row in range(taps - 1):
            cgrad_send[q, row] = dot_nt(conv_rows[row], places[q]).astype(BF16)
    cgrad_copies = [
        doc_copy(3, j, cgrad_send.at[lax.rem(d + j, docs)], cgrad_recv.at[d])
        for j in range(1, docs)
    ]
    for copy in cgrad_copies:
        copy.start()
    sgrad_recv[d] = sgrad_send[:, d]
    cgrad_recv[d] = cgrad_send[d]

    for copy in sum_copies:
        copy.wait_recv()
    total = cg_partial[rows_of(f)]
    for j in range(1, parts):
        total = total + cg_recv[j]
    cg[rows_of(f)] = total.astype(BF16)
    cg_copies = [part_copy(3, j, cg.at[rows_of(f)], cg.at[rows_of(f)]) for j in range(1, parts)]
    for copy in cg_copies:
        copy.start()
    for load in loads[1:]:
        load.wait()

    for copy in cg_copies:
        copy.wait_recv()
    product = dot_tn(tok_cols[...], cg[...])
    fin_own[...] = product.reshape(docs, out_rows, width)
    fin_send[...] = product.astype(BF16).reshape(docs, out_rows, width)
    fin_copies = [
        doc_copy(4, j, fin_send.at[lax.rem(d + j, docs)], fin_recv.at[j]) for j in range(1, docs)
    ]
    for copy in fin_copies:
        copy.start()

    for copy in sgrad_copies + cgrad_copies:
        copy.wait_recv()
    for s in range(slots):
        row_of = jnp.int32(0)
        found = jnp.float32(0.0)
        for r in range(slots):
            hit = carry_ref[r] == s
            row_of = jnp.where(hit, r, row_of)
            found = jnp.where(hit, 1.0, found)
        state_out[s] = (sgrad_recv[row_of].astype(F32) * found).astype(BF16)
        conv_out[s] = (cgrad_recv[row_of].astype(F32) * found).astype(BF16)

    for copy in fin_copies:
        copy.wait_recv()
    result = fin_own[d]
    for j in range(1, docs):
        result = result + fin_recv[j].astype(F32)
    proj_out[...] = result

    for copies in (
        conv_copies,
        coeff_copies,
        state_copies,
        gather_copies,
        sum_copies,
        sgrad_copies,
        cgrad_copies,
        cg_copies,
        fin_copies,
    ):
        for copy in copies:
            copy.wait_send()


def device_part(docs, parts, *args):
    (
        tokens_in,
        mix_in,
        step_size,
        doc_ids,
        out_grad,
        proj_weight,
        conv_weight,
        decay_rate,
        carried_state,
        carried_conv,
        carry_from,
    ) = args
    rows_dev, length, model_width = tokens_in.shape
    channels = mix_in.shape[2]
    heads = step_size.shape[2]
    depth, width = proj_weight.shape
    slots, _, part_p, nstate = carried_state.shape
    taps = conv_weight.shape[0]
    out_rows = model_width // (docs * parts)
    block = length // parts
    aligned = (
        rows_dev == 1
        and slots == docs
        and part_p % 16 == 0
        and heads % 16 == 0
        and block % 16 == 0
        and out_rows % 128 == 0
        and depth % 128 == 0
        and nstate == 128
        and channels % 128 == 0
        and taps <= 8
    )
    if not aligned:
        return shards(*args)
    vmem = pl.BlockSpec(memory_space=pltpu.VMEM)
    return pl.pallas_call(
        functools.partial(layer_kernel, docs, parts),
        out_shape=(
            jax.ShapeDtypeStruct((out_rows, width), F32),
            jax.ShapeDtypeStruct(carried_state.shape, BF16),
            jax.ShapeDtypeStruct(carried_conv.shape, BF16),
        ),
        in_specs=[
            pl.BlockSpec(memory_space=pltpu.SMEM),
            pl.BlockSpec(memory_space=pl.ANY),
        ]
        + [vmem] * 9,
        out_specs=(vmem, vmem, vmem),
        scratch_shapes=[
            pltpu.VMEM((length, depth), BF16),
            pltpu.VMEM((length, docs * out_rows), BF16),
            pltpu.VMEM((length, width), F32),
            pltpu.VMEM((parts, block, width), F32),
            pltpu.VMEM((length, width), BF16),
            pltpu.VMEM((length, width), F32),
            pltpu.VMEM((parts, block, width), F32),
            pltpu.VMEM((length, width), BF16),
            pltpu.VMEM((slots, heads, part_p, nstate), BF16),
            pltpu.VMEM((heads, docs, part_p, nstate), BF16),
            pltpu.VMEM((slots, taps - 1, heads, part_p), BF16),
            pltpu.VMEM((docs, taps - 1, heads, part_p), BF16),
            pltpu.VMEM((heads, docs, part_p, nstate), BF16),
            pltpu.VMEM((docs, heads, part_p, nstate), BF16),
            pltpu.VMEM((docs, taps - 1, heads, part_p), BF16),
            pltpu.VMEM((docs, taps - 1, heads, part_p), BF16),
            pltpu.VMEM((docs, out_rows, width), F32),
            pltpu.VMEM((docs, out_rows, width), BF16),
            pltpu.VMEM((docs, out_rows, width), BF16),
            pltpu.VMEM((length + 8, channels), F32),
            pltpu.VMEM((length + 8, 128), F32),
            pltpu.VMEM((length, channels), BF16),
            pltpu.VMEM((length, channels), BF16),
            pltpu.VMEM((8, channels), F32),
            pltpu.VMEM((8, channels), F32),
            pltpu.SemaphoreType.DMA((1 + docs,)),
            pltpu.SemaphoreType.DMA((4, parts)),
            pltpu.SemaphoreType.DMA((4, parts)),
            pltpu.SemaphoreType.DMA((5, docs)),
            pltpu.SemaphoreType.DMA((5, docs)),
        ],
        compiler_params=pltpu.CompilerParams(
            collective_id=0, has_side_effects=True, vmem_limit_bytes=40 * 1024 * 1024
        ),
        cost_estimate=pl.CostEstimate(
            flops=2 * length * channels * length * 4, bytes_accessed=4 << 20, transcendentals=0
        ),
    )(
        carry_from,
        tokens_in,
        mix_in,
        step_size,
        doc_ids,
        out_grad,
        proj_weight,
        conv_weight,
        decay_rate.reshape(1, heads),
        carried_state,
        carried_conv,
    )


def solution(mesh):
    return jax.shard_map(
        functools.partial(device_part, mesh.shape["doc"], mesh.shape["fsdp"]),
        mesh=mesh,
        in_specs=(
            P("doc", None, None),
            P("doc", None, "fsdp"),
            P("doc", None, "fsdp"),
            P("doc", None),
            P("doc", None, "fsdp"),
            P("fsdp", None),
            P(None, "fsdp"),
            P("fsdp"),
            P(None, "fsdp", "doc", None),
            P(None, None, "fsdp", "doc"),
            P(),
        ),
        out_specs=(
            P(("doc", "fsdp"), None),
            P(None, "fsdp", "doc", None),
            P(None, None, "fsdp", "doc"),
        ),
        check_vma=False,
    )
```

```python
import functools

import jax
import jax.numpy as jnp
from jax import lax
from jax.experimental import pallas as pl
from jax.experimental.pallas import tpu as pltpu
from jax.sharding import PartitionSpec as P


def silu_slope(value):
    sigmoid_value = jax.nn.sigmoid(value)
    return sigmoid_value * (1.0 + value * (1.0 - sigmoid_value))


def conv_masks(seg_row, tap_count):
    length = seg_row.shape[0]
    opening = seg_row == seg_row[0]
    tap_masks = []
    for offset in range(tap_count):
        earlier = jnp.concatenate([jnp.full((offset,), -1, jnp.int32), seg_row[: length - offset]])
        inside = jnp.arange(length) >= offset
        tap_masks.append(jnp.where(inside, earlier == seg_row, opening))
    return (opening, tap_masks)


def row_pass(
    coeff, mix_row, step_row, seg_row, grad_rows, state_zero, conv_zero, conv_weight, decay_rate
):
    length, channels = mix_row.shape
    head_count = step_row.shape[1]
    head_dim = channels // head_count
    tap_count = conv_weight.shape[0]
    nstate = coeff.shape[1] // 2
    opening, tap_masks = conv_masks(seg_row, tap_count)
    extended = jnp.concatenate([conv_zero, mix_row], axis=0).astype(jnp.float32)
    preact = jnp.zeros((length, channels), jnp.float32)
    for offset in range(tap_count):
        window = extended[tap_count - 1 - offset : tap_count - 1 - offset + length]
        preact = preact + jnp.where(
            tap_masks[offset][:, None], conv_weight[offset][None, :] * window, 0.0
        )
    mixed_rows = jax.nn.silu(preact).astype(jnp.bfloat16)
    values = (
        step_row[:, :, None] * mixed_rows.reshape(length, head_count, head_dim).astype(jnp.float32)
    ).astype(jnp.bfloat16)
    write_coeff = coeff[:, :nstate]
    read_coeff = coeff[:, nstate:]
    scores = jnp.dot(read_coeff, write_coeff.T, preferred_element_type=jnp.float32)
    log_decay = jnp.cumsum(-(decay_rate[None, :] * step_row), axis=0).T
    lower = jnp.arange(length)[:, None] >= jnp.arange(length)[None, :]
    allowed = lower & (seg_row[:, None] == seg_row[None, :])
    spread = log_decay[:, :, None] - log_decay[:, None, :]
    decays = jnp.where(allowed[None], jnp.exp(jnp.where(allowed[None], spread, 0.0)), 0.0)
    edge_weight = jnp.where(opening[None, :], jnp.exp(log_decay), 0.0)
    weighted = (decays * scores[None]).astype(jnp.bfloat16)
    grad_heads = grad_rows.reshape(length, head_count, head_dim)
    values_grad = jnp.einsum(
        "hts,thp->shp", weighted, grad_heads, preferred_element_type=jnp.float32
    )
    products = jnp.einsum("thp,shp->hts", grad_heads, values, preferred_element_type=jnp.float32)
    score_grad = jnp.sum(decays * products, axis=0)
    carried = jnp.einsum("thp,hpn->thn", grad_heads, state_zero, preferred_element_type=jnp.float32)
    read_grad = jnp.dot(
        score_grad, write_coeff.astype(jnp.float32), precision=lax.Precision.HIGHEST
    )
    read_grad = read_grad + jnp.sum(edge_weight.T[:, :, None] * carried, axis=1)
    write_grad = jnp.dot(
        score_grad.T, read_coeff.astype(jnp.float32), precision=lax.Precision.HIGHEST
    )
    scaled = edge_weight.T[:, :, None] * grad_heads.astype(jnp.float32)
    state_grad = jnp.einsum(
        "thp,tn->hpn", scaled, read_coeff.astype(jnp.float32), precision=lax.Precision.HIGHEST
    )
    mixed_grad = (values_grad * step_row[:, :, None]).reshape(length, channels)
    preact_grad = mixed_grad * silu_slope(preact)
    conv_rows = []
    for index_row in range(tap_count - 1):
        running = jnp.zeros((channels,), jnp.float32)
        for offset in range(tap_count - 1 - index_row, tap_count):
            position = index_row - (tap_count - 1) + offset
            running = running + jnp.where(
                opening[position], conv_weight[offset] * preact_grad[position], 0.0
            )
        conv_rows.append(running)
    conv_grad = jnp.stack(conv_rows)
    return (jnp.concatenate([write_grad, read_grad], axis=1), state_grad, conv_grad)


def shards(
    tokens_in,
    mix_in,
    step_size,
    doc_ids,
    out_grad,
    proj_weight,
    conv_weight,
    decay_rate,
    carried_state,
    carried_conv,
    carry_from,
):
    rows_dev, length, model_width = tokens_in.shape
    head_count = step_size.shape[2]
    slot_count = carried_state.shape[0]
    part_p = carried_state.shape[2]
    nstate = carried_state.shape[3]
    tap_count = conv_weight.shape[0]
    doc_count = lax.axis_size("doc")
    head_dim = part_p * doc_count
    channels = head_count * head_dim
    picker = (carry_from[:, None] == jnp.arange(slot_count, dtype=jnp.int32)[None, :]).astype(
        jnp.bfloat16
    )
    chosen_state = jnp.einsum(
        "rs,shpn->rhpn", picker, carried_state, preferred_element_type=jnp.float32
    ).astype(jnp.bfloat16)
    chosen_conv = jnp.einsum(
        "rs,skhp->rkhp", picker, carried_conv, preferred_element_type=jnp.float32
    ).astype(jnp.bfloat16)
    chosen_state = chosen_state.reshape(slot_count, head_count, part_p * nstate)
    chosen_conv = chosen_conv.reshape(slot_count, (tap_count - 1) * head_count, part_p)
    start_state, start_conv = (
        lax.all_to_all(chosen_state, "doc", split_axis=0, concat_axis=2, tiled=True),
        lax.all_to_all(chosen_conv, "doc", split_axis=0, concat_axis=2, tiled=True),
    )
    start_state = start_state.reshape(rows_dev, head_count, head_dim, nstate)
    start_conv = start_conv.reshape(rows_dev, tap_count - 1, channels)
    flattened = tokens_in.reshape(rows_dev * length, model_width)
    coeff_sum = jnp.dot(
        flattened,
        lax.all_gather(proj_weight, "fsdp", axis=0, tiled=True),
        preferred_element_type=jnp.float32,
    )
    coeff = coeff_sum.astype(jnp.bfloat16).reshape(rows_dev, length, proj_weight.shape[1])
    coeff_grad, state_grad, conv_grad = row_pass(
        coeff[0],
        mix_in[0],
        step_size[0],
        doc_ids[0],
        out_grad[0],
        start_state[0],
        start_conv[0],
        conv_weight,
        decay_rate,
    )
    coeff_grads = [coeff_grad]
    state_grads = [state_grad]
    conv_grads = [conv_grad]
    back_state = (
        jnp.stack(state_grads).astype(jnp.bfloat16).reshape(rows_dev, head_count, head_dim * nstate)
    )
    back_conv = (
        jnp.stack(conv_grads)
        .astype(jnp.bfloat16)
        .reshape(rows_dev, (tap_count - 1) * head_count, head_dim)
    )
    got_state, got_conv = (
        lax.all_to_all(back_state, "doc", split_axis=2, concat_axis=0, tiled=True),
        lax.all_to_all(back_conv, "doc", split_axis=2, concat_axis=0, tiled=True),
    )
    grad_state = jnp.einsum(
        "rs,rx->sx", picker, got_state.reshape(slot_count, -1), preferred_element_type=jnp.float32
    )
    grad_state = grad_state.astype(jnp.bfloat16).reshape(carried_state.shape)
    grad_conv = jnp.einsum(
        "rs,rx->sx", picker, got_conv.reshape(slot_count, -1), preferred_element_type=jnp.float32
    )
    grad_conv = grad_conv.astype(jnp.bfloat16).reshape(carried_conv.shape)
    coeff_flat = jnp.stack(coeff_grads).reshape(rows_dev * length, -1)
    share = lax.psum_scatter(coeff_flat, "fsdp", scatter_dimension=1, tiled=True)
    partial_cols = jnp.einsum(
        "tj,tn->jn", flattened.astype(jnp.float32), share, precision=lax.Precision.HIGHEST
    )
    summed_cols = lax.psum_scatter(partial_cols, "doc", scatter_dimension=0, tiled=True)
    grad_proj = lax.all_to_all(summed_cols, "fsdp", split_axis=0, concat_axis=1, tiled=True)
    return (grad_proj, grad_state, grad_conv)


F32 = jnp.float32
BF16 = jnp.bfloat16
MESH = pl.DeviceIdType.MESH


def dot_nn(a, b, precision=None):
    return lax.dot_general(
        a, b, (((1,), (0,)), ((), ())), precision=precision, preferred_element_type=F32
    )


def dot_nt(a, b):
    return lax.dot_general(a, b, (((1,), (1,)), ((), ())), preferred_element_type=F32)


def dot_tn(a, b):
    return lax.dot_general(a, b, (((0,), (0,)), ((), ())), preferred_element_type=F32)


def iota(shape, axis):
    return lax.broadcasted_iota(jnp.int32, shape, axis)


def layer_kernel(
    docs,
    parts,
    carry_hbm,
    tokens_hbm,
    mix_hbm,
    step_hbm,
    seg_hbm,
    grad_hbm,
    weight_hbm,
    taps_hbm,
    rate_hbm,
    state_hbm,
    conv_hbm,
    proj_out,
    state_out,
    conv_out,
    carry_ref,
    mix_ref,
    step_ref,
    seg_ref,
    grad_ref,
    weight_ref,
    taps_ref,
    rate_ref,
    state_ref,
    conv_ref,
    tok_part,
    tok_cols,
    coeff_partial,
    coeff_recv,
    coeff,
    cg_partial,
    cg_recv,
    cg,
    state_send,
    state_recv,
    conv_send,
    conv_recv,
    sgrad_send,
    sgrad_recv,
    cgrad_send,
    cgrad_recv,
    fin_own,
    fin_send,
    fin_recv,
    ext,
    seg_ext,
    og_scaled,
    val_scaled,
    first_step,
    first_shrink,
    load_sem,
    part_send_sem,
    part_recv_sem,
    doc_send_sem,
    doc_recv_sem,
):
    d = lax.axis_index("doc")
    f = lax.axis_index("fsdp")
    length, channels = mix_ref.shape
    heads = step_ref.shape[0]
    head_dim = channels // heads
    part_p = head_dim // docs
    width = weight_ref.shape[1]
    nstate = width // 2
    slots = state_ref.shape[0]
    depth = weight_ref.shape[0]
    block = length // parts
    out_rows = proj_out.shape[0]
    taps = taps_ref.shape[0]

    own_columns = pl.ds(pl.multiple_of(f * depth, 128), depth)
    pairs = [
        (carry_hbm, carry_ref),
        (state_hbm, state_ref),
        (conv_hbm, conv_ref),
        (tokens_hbm.at[0, :, own_columns], tok_part),
        (weight_hbm, weight_ref),
        (step_hbm.at[0], step_ref),
        (rate_hbm, rate_ref),
        (seg_hbm, seg_ref),
        (taps_hbm, taps_ref),
        (mix_hbm.at[0], mix_ref),
        (grad_hbm.at[0], grad_ref),
    ]
    for q in range(docs):
        columns = pl.ds(pl.multiple_of((q * parts + f) * out_rows, 128), out_rows)
        pairs.append(
            (tokens_hbm.at[0, :, columns], tok_cols.at[:, pl.ds(q * out_rows, out_rows)])
        )
    loads = [
        pltpu.make_async_copy(src, dst, load_sem.at[i]) for i, (src, dst) in enumerate(pairs)
    ]
    for load in loads:
        load.start()

    barrier = pltpu.get_barrier_semaphore()
    for j in range(1, parts):
        pl.semaphore_signal(
            barrier, inc=1, device_id=(d, lax.rem(f + j, parts)), device_id_type=MESH
        )
    for j in range(1, docs):
        pl.semaphore_signal(
            barrier, inc=1, device_id=(lax.rem(d + j, docs), f), device_id_type=MESH
        )

    def part_copy(phase, j, src, dst):
        return pltpu.make_async_remote_copy(
            src_ref=src,
            dst_ref=dst,
            send_sem=part_send_sem.at[phase, j],
            recv_sem=part_recv_sem.at[phase, j],
            device_id=(d, lax.rem(f + j, parts)),
            device_id_type=MESH,
        )

    def doc_copy(phase, j, src, dst):
        return pltpu.make_async_remote_copy(
            src_ref=src,
            dst_ref=dst,
            send_sem=doc_send_sem.at[phase, j],
            recv_sem=doc_recv_sem.at[phase, j],
            device_id=(lax.rem(d + j, docs), f),
            device_id_type=MESH,
        )

    def rows_of(owner):
        return pl.ds(pl.multiple_of(owner * block, block), block)

    for load in loads[:3]:
        load.wait()
    for r in range(slots):
        source = carry_ref[r]
        usable = jnp.where(source >= 0, 1.0, 0.0)
        index = jnp.maximum(source, 0)
        state_send[r] = (state_ref[index].astype(F32) * usable).astype(BF16)
        conv_send[r] = (conv_ref[index].astype(F32) * usable).astype(BF16)

    for load in loads[3:5]:
        load.wait()
    coeff_partial[...] = dot_nn(tok_part[...], weight_ref[...])

    pl.semaphore_wait(barrier, parts - 1 + docs - 1)

    conv_copies = [
        doc_copy(0, j, conv_send.at[lax.rem(d + j, docs)], conv_recv.at[d]) for j in range(1, docs)
    ]
    coeff_copies = [
        part_copy(0, j, coeff_partial.at[rows_of(lax.rem(f + j, parts))], coeff_recv.at[j])
        for j in range(1, parts)
    ]
    state_copies = [
        doc_copy(1, j, state_send.at[lax.rem(d + j, docs)], state_recv.at[:, d])
        for j in range(1, docs)
    ]
    for copy in conv_copies + coeff_copies + state_copies:
        copy.start()
    conv_recv[d] = conv_send[d]
    state_recv[:, d] = state_send[d]

    for load in loads[5:11]:
        load.wait()
    lower = iota((length, length), 0) >= iota((length, length), 1)
    rate = jnp.sum(
        jnp.where(iota((heads, heads), 0) == iota((heads, heads), 1), rate_ref[...], 0.0),
        axis=1,
        keepdims=True,
    )
    steps = step_ref[...]
    log_decay = lax.dot_general(
        -(rate * steps),
        jnp.where(lower, 1.0, 0.0),
        (((1,), (1,)), ((), ())),
        precision=lax.Precision.HIGHEST,
        preferred_element_type=F32,
    )

    def halves(x):
        top = x.astype(BF16)
        return top, (x - top.astype(F32)).astype(BF16)

    grow = halves(jnp.exp(log_decay))
    shrink = halves(jnp.exp(-log_decay))
    step_halves = halves(steps)

    seg_row = seg_ref[...].astype(F32)
    seg_cols = jnp.broadcast_to(seg_row, (128, length)).T
    seg_ext[8:, :] = seg_cols
    seg_ext[:8, :] = jnp.broadcast_to(seg_cols[:1], (8, 128))
    opening = seg_cols == seg_cols[:1]

    def scaled_values(preact, step, shrink_factor):
        mixed = (preact / (1.0 + jnp.exp(-preact))).astype(BF16).astype(F32)
        values = (step * mixed).astype(BF16).astype(F32)
        return (values * shrink_factor).astype(BF16)

    ext[:8, :] = jnp.zeros((8, channels), F32)

    def chunk(c, carry):
        lanes = pl.ds(pl.multiple_of(c * 128, 128), 128)
        expand = jnp.where(
            iota((heads, 128), 0) == lax.div(iota((heads, 128), 1) + c * 128, head_dim), 1.0, 0.0
        ).astype(BF16)

        def per_channel(pair):
            return dot_tn(pair[0], expand) + dot_tn(pair[1], expand)

        ext[8:, lanes] = mix_ref[:, lanes].astype(F32)
        preact = jnp.zeros((length, 128), F32)
        for k in range(taps):
            same = seg_ext[8 - k : 8 - k + length, :] == seg_cols
            window = ext[8 - k : 8 - k + length, lanes]
            preact = preact + jnp.where(same, taps_ref[k : k + 1, lanes] * window, 0.0)
        step_c = per_channel(step_halves)
        shrink_c = per_channel(shrink)
        val_scaled[:, lanes] = scaled_values(preact, step_c, shrink_c)
        og_scaled[:, lanes] = (grad_ref[:, lanes].astype(F32) * per_channel(grow)).astype(BF16)
        first_step[:, lanes] = step_c[:16]
        first_shrink[:, lanes] = shrink_c[:16]
        return carry

    chunks = channels // 128
    lax.fori_loop(0, chunks // 2, chunk, 0)

    for copy in coeff_copies:
        copy.wait_recv()
    total = coeff_partial[rows_of(f)]
    for j in range(1, parts):
        total = total + coeff_recv[j]
    coeff[rows_of(f)] = total.astype(BF16)
    gather_copies = [
        part_copy(1, j, coeff.at[rows_of(f)], coeff.at[rows_of(f)]) for j in range(1, parts)
    ]
    for copy in gather_copies:
        copy.start()

    lax.fori_loop(chunks // 2, chunks, chunk, 0)

    for copy in conv_copies:
        copy.wait_recv()

    def place(q):
        lane = iota((part_p, channels), 1)
        return jnp.where(
            lax.rem(lane, head_dim) == iota((part_p, channels), 0) + q * part_p, 1.0, 0.0
        ).astype(BF16)

    places = [place(q) for q in range(docs)]
    head_rows = (taps - 1) * heads
    own_head = (
        lax.div(iota((taps - 1, heads, channels), 2), head_dim)
        == iota((taps - 1, heads, channels), 1)
    )
    spread = jnp.zeros((head_rows, channels), F32)
    for q in range(docs):
        spread = spread + dot_nn(conv_recv[q].reshape(head_rows, part_p), places[q])
    carried_rows = jnp.sum(
        jnp.where(own_head, spread.reshape(taps - 1, heads, channels), 0.0), axis=1
    )
    ext[8 - (taps - 1) : 8, :] = carried_rows
    pre = jnp.zeros((16, channels), F32)
    for k in range(taps):
        same = seg_ext[8 - k : 24 - k, :1] == seg_cols[:16, :1]
        window = ext[8 - k : 24 - k, :]
        pre = pre + jnp.where(same, taps_ref[k : k + 1, :] * window, 0.0)
    val_scaled[:16, :] = scaled_values(pre, first_step[...], first_shrink[...])

    upper = iota((length, length), 0) <= iota((length, length), 1)
    same_doc = seg_cols[:, :1] == seg_row
    score_grad = jnp.where(
        lower & same_doc, dot_nt(og_scaled[...], val_scaled[...]), 0.0
    ).astype(BF16)
    score_grad_t = jnp.where(
        upper & same_doc, dot_nt(val_scaled[...], og_scaled[...]), 0.0
    ).astype(BF16)

    for copy in state_copies:
        copy.wait_recv()
    from_state = jnp.where(
        opening, dot_nn(og_scaled[...], state_recv[...].reshape(channels, nstate)), 0.0
    )

    for copy in gather_copies:
        copy.wait_recv()
    write_coeff = coeff[:, :nstate]
    read_coeff = coeff[:, nstate:]
    cg_partial[:, :nstate] = dot_nn(score_grad_t, read_coeff)
    cg_partial[:, nstate:] = dot_nn(score_grad, write_coeff) + from_state
    sum_copies = [
        part_copy(2, j, cg_partial.at[rows_of(lax.rem(f + j, parts))], cg_recv.at[j])
        for j in range(1, parts)
    ]
    for copy in sum_copies:
        copy.start()

    open_read = jnp.where(opening, read_coeff.astype(F32), 0.0).astype(BF16)
    sgrad_send[...] = (
        dot_tn(og_scaled[...], open_read).astype(BF16).reshape(heads, docs, part_p, nstate)
    )
    sgrad_copies = [
        doc_copy(2, j, sgrad_send.at[:, lax.rem(d + j, docs)], sgrad_recv.at[d])
        for j in range(1, docs)
    ]
    for copy in sgrad_copies:
        copy.start()
    first_scores = dot_nt(write_coeff[:16], read_coeff)
    first_seg = jnp.broadcast_to(seg_row, (16, length)) == seg_cols[:16, :1]
    first_allowed = first_seg & (iota((16, length), 1) >= iota((16, length), 0))
    first_scores = jnp.where(first_allowed, first_scores, 0.0).astype(BF16)
    first_grad = dot_nn(first_scores, og_scaled[...])[:8]
    pre = pre[:8]
    gate = 1.0 / (1.0 + jnp.exp(-pre))
    pre_grad = first_grad * first_step[:8] * first_shrink[:8] * gate * (1.0 + pre * (1.0 - gate))
    pre_grad = jnp.where(seg_cols[:8, :1] == seg_cols[:1, :1], pre_grad, 0.0)
    conv_rows = []
    for row in range(taps - 1):
        running = jnp.zeros((1, channels), F32)
        for k in range(taps - 1 - row, taps):
            position = row - (taps - 1) + k
            running = running + taps_ref[k : k + 1, :] * pre_grad[position : position + 1]
        conv_rows.append(
            jnp.where(own_head[0], jnp.broadcast_to(running, (heads, channels)), 0.0).astype(BF16)
        )
    for q in range(docs):
        for row in range(taps - 1):
            cgrad_send[q, row] = dot_nt(conv_rows[row], places[q]).astype(BF16)
    cgrad_copies = [
        doc_copy(3, j, cgrad_send.at[lax.rem(d + j, docs)], cgrad_recv.at[d])
        for j in range(1, docs)
    ]
    for copy in cgrad_copies:
        copy.start()
    sgrad_recv[d] = sgrad_send[:, d]
    cgrad_recv[d] = cgrad_send[d]

    for copy in sum_copies:
        copy.wait_recv()
    total = cg_partial[rows_of(f)]
    for j in range(1, parts):
        total = total + cg_recv[j]
    cg[rows_of(f)] = total.astype(BF16)
    cg_copies = [part_copy(3, j, cg.at[rows_of(f)], cg.at[rows_of(f)]) for j in range(1, parts)]
    for copy in cg_copies:
        copy.start()
    for load in loads[11:]:
        load.wait()

    for copy in cg_copies:
        copy.wait_recv()
    product = dot_tn(tok_cols[...], cg[...])
    fin_own[...] = product.reshape(docs, out_rows, width)
    fin_send[...] = product.astype(BF16).reshape(docs, out_rows, width)
    fin_copies = [
        doc_copy(4, j, fin_send.at[lax.rem(d + j, docs)], fin_recv.at[j]) for j in range(1, docs)
    ]
    for copy in fin_copies:
        copy.start()

    for copy in sgrad_copies + cgrad_copies:
        copy.wait_recv()
    for s in range(slots):
        row_of = jnp.int32(0)
        found = jnp.float32(0.0)
        for r in range(slots):
            hit = carry_ref[r] == s
            row_of = jnp.where(hit, r, row_of)
            found = jnp.where(hit, 1.0, found)
        state_out[s] = (sgrad_recv[row_of].astype(F32) * found).astype(BF16)
        conv_out[s] = (cgrad_recv[row_of].astype(F32) * found).astype(BF16)

    for copy in fin_copies:
        copy.wait_recv()
    result = fin_own[d]
    for j in range(1, docs):
        result = result + fin_recv[j].astype(F32)
    proj_out[...] = result

    for copies in (
        conv_copies,
        coeff_copies,
        state_copies,
        gather_copies,
        sum_copies,
        sgrad_copies,
        cgrad_copies,
        cg_copies,
        fin_copies,
    ):
        for copy in copies:
            copy.wait_send()


def device_part(docs, parts, *args):
    (
        tokens_in,
        mix_in,
        step_size,
        doc_ids,
        out_grad,
        proj_weight,
        conv_weight,
        decay_rate,
        carried_state,
        carried_conv,
        carry_from,
    ) = args
    rows_dev, length, model_width = tokens_in.shape
    channels = mix_in.shape[2]
    heads = step_size.shape[2]
    depth, width = proj_weight.shape
    slots, _, part_p, nstate = carried_state.shape
    taps = conv_weight.shape[0]
    out_rows = model_width // (docs * parts)
    block = length // parts
    aligned = (
        rows_dev == 1
        and slots == docs
        and part_p % 16 == 0
        and heads % 16 == 0
        and block % 16 == 0
        and out_rows % 128 == 0
        and depth % 128 == 0
        and nstate == 128
        and channels % 128 == 0
        and taps <= 8
    )
    if not aligned:
        return shards(*args)
    vmem = pl.BlockSpec(memory_space=pltpu.VMEM)
    return pl.pallas_call(
        functools.partial(layer_kernel, docs, parts),
        out_shape=(
            jax.ShapeDtypeStruct((out_rows, width), F32),
            jax.ShapeDtypeStruct(carried_state.shape, BF16),
            jax.ShapeDtypeStruct(carried_conv.shape, BF16),
        ),
        in_specs=[pl.BlockSpec(memory_space=pltpu.HBM)] * 11,
        out_specs=(vmem, vmem, vmem),
        scratch_shapes=[
            pltpu.SMEM(carry_from.shape, jnp.int32),
            pltpu.VMEM((length, channels), BF16),
            pltpu.VMEM((heads, length), F32),
            pltpu.VMEM(doc_ids.shape, jnp.int32),
            pltpu.VMEM((length, channels), BF16),
            pltpu.VMEM(proj_weight.shape, BF16),
            pltpu.VMEM(conv_weight.shape, F32),
            pltpu.VMEM((1, heads), F32),
            pltpu.VMEM(carried_state.shape, BF16),
            pltpu.VMEM(carried_conv.shape, BF16),
            pltpu.VMEM((length, depth), BF16),
            pltpu.VMEM((length, docs * out_rows), BF16),
            pltpu.VMEM((length, width), F32),
            pltpu.VMEM((parts, block, width), F32),
            pltpu.VMEM((length, width), BF16),
            pltpu.VMEM((length, width), F32),
            pltpu.VMEM((parts, block, width), F32),
            pltpu.VMEM((length, width), BF16),
            pltpu.VMEM((slots, heads, part_p, nstate), BF16),
            pltpu.VMEM((heads, docs, part_p, nstate), BF16),
            pltpu.VMEM((slots, taps - 1, heads, part_p), BF16),
            pltpu.VMEM((docs, taps - 1, heads, part_p), BF16),
            pltpu.VMEM((heads, docs, part_p, nstate), BF16),
            pltpu.VMEM((docs, heads, part_p, nstate), BF16),
            pltpu.VMEM((docs, taps - 1, heads, part_p), BF16),
            pltpu.VMEM((docs, taps - 1, heads, part_p), BF16),
            pltpu.VMEM((docs, out_rows, width), F32),
            pltpu.VMEM((docs, out_rows, width), BF16),
            pltpu.VMEM((docs, out_rows, width), BF16),
            pltpu.VMEM((length + 8, channels), F32),
            pltpu.VMEM((length + 8, 128), F32),
            pltpu.VMEM((length, channels), BF16),
            pltpu.VMEM((length, channels), BF16),
            pltpu.VMEM((16, channels), F32),
            pltpu.VMEM((16, channels), F32),
            pltpu.SemaphoreType.DMA((11 + docs,)),
            pltpu.SemaphoreType.DMA((4, parts)),
            pltpu.SemaphoreType.DMA((4, parts)),
            pltpu.SemaphoreType.DMA((5, docs)),
            pltpu.SemaphoreType.DMA((5, docs)),
        ],
        compiler_params=pltpu.CompilerParams(
            collective_id=0, has_side_effects=True, vmem_limit_bytes=60 * 1024 * 1024
        ),
        cost_estimate=pl.CostEstimate(
            flops=2 * length * channels * length * 4, bytes_accessed=4 << 20, transcendentals=0
        ),
    )(
        carry_from,
        tokens_in,
        mix_in,
        jnp.swapaxes(step_size, 1, 2),
        doc_ids,
        out_grad,
        proj_weight,
        conv_weight,
        decay_rate.reshape(1, heads),
        carried_state,
        carried_conv,
    )


def solution(mesh):
    return jax.shard_map(
        functools.partial(device_part, mesh.shape["doc"], mesh.shape["fsdp"]),
        mesh=mesh,
        in_specs=(
            P("doc", None, None),
            P("doc", None, "fsdp"),
            P("doc", None, "fsdp"),
            P("doc", None),
            P("doc", None, "fsdp"),
            P("fsdp", None),
            P(None, "fsdp"),
            P("fsdp"),
            P(None, "fsdp", "doc", None),
            P(None, None, "fsdp", "doc"),
            P(),
        ),
        out_specs=(
            P(("doc", "fsdp"), None),
            P(None, "fsdp", "doc", None),
            P(None, None, "fsdp", "doc"),
        ),
        check_vma=False,
    )
```

```python
import functools

import jax
import jax.numpy as jnp
from jax import lax
from jax.experimental import pallas as pl
from jax.experimental.pallas import tpu as pltpu
from jax.sharding import PartitionSpec as P


def silu_slope(value):
    sigmoid_value = jax.nn.sigmoid(value)
    return sigmoid_value * (1.0 + value * (1.0 - sigmoid_value))


def conv_masks(seg_row, tap_count):
    length = seg_row.shape[0]
    opening = seg_row == seg_row[0]
    tap_masks = []
    for offset in range(tap_count):
        earlier = jnp.concatenate([jnp.full((offset,), -1, jnp.int32), seg_row[: length - offset]])
        inside = jnp.arange(length) >= offset
        tap_masks.append(jnp.where(inside, earlier == seg_row, opening))
    return (opening, tap_masks)


def row_pass(
    coeff, mix_row, step_row, seg_row, grad_rows, state_zero, conv_zero, conv_weight, decay_rate
):
    length, channels = mix_row.shape
    head_count = step_row.shape[1]
    head_dim = channels // head_count
    tap_count = conv_weight.shape[0]
    nstate = coeff.shape[1] // 2
    opening, tap_masks = conv_masks(seg_row, tap_count)
    extended = jnp.concatenate([conv_zero, mix_row], axis=0).astype(jnp.float32)
    preact = jnp.zeros((length, channels), jnp.float32)
    for offset in range(tap_count):
        window = extended[tap_count - 1 - offset : tap_count - 1 - offset + length]
        preact = preact + jnp.where(
            tap_masks[offset][:, None], conv_weight[offset][None, :] * window, 0.0
        )
    mixed_rows = jax.nn.silu(preact).astype(jnp.bfloat16)
    values = (
        step_row[:, :, None] * mixed_rows.reshape(length, head_count, head_dim).astype(jnp.float32)
    ).astype(jnp.bfloat16)
    write_coeff = coeff[:, :nstate]
    read_coeff = coeff[:, nstate:]
    scores = jnp.dot(read_coeff, write_coeff.T, preferred_element_type=jnp.float32)
    log_decay = jnp.cumsum(-(decay_rate[None, :] * step_row), axis=0).T
    lower = jnp.arange(length)[:, None] >= jnp.arange(length)[None, :]
    allowed = lower & (seg_row[:, None] == seg_row[None, :])
    spread = log_decay[:, :, None] - log_decay[:, None, :]
    decays = jnp.where(allowed[None], jnp.exp(jnp.where(allowed[None], spread, 0.0)), 0.0)
    edge_weight = jnp.where(opening[None, :], jnp.exp(log_decay), 0.0)
    weighted = (decays * scores[None]).astype(jnp.bfloat16)
    grad_heads = grad_rows.reshape(length, head_count, head_dim)
    values_grad = jnp.einsum(
        "hts,thp->shp", weighted, grad_heads, preferred_element_type=jnp.float32
    )
    products = jnp.einsum("thp,shp->hts", grad_heads, values, preferred_element_type=jnp.float32)
    score_grad = jnp.sum(decays * products, axis=0)
    carried = jnp.einsum("thp,hpn->thn", grad_heads, state_zero, preferred_element_type=jnp.float32)
    read_grad = jnp.dot(
        score_grad, write_coeff.astype(jnp.float32), precision=lax.Precision.HIGHEST
    )
    read_grad = read_grad + jnp.sum(edge_weight.T[:, :, None] * carried, axis=1)
    write_grad = jnp.dot(
        score_grad.T, read_coeff.astype(jnp.float32), precision=lax.Precision.HIGHEST
    )
    scaled = edge_weight.T[:, :, None] * grad_heads.astype(jnp.float32)
    state_grad = jnp.einsum(
        "thp,tn->hpn", scaled, read_coeff.astype(jnp.float32), precision=lax.Precision.HIGHEST
    )
    mixed_grad = (values_grad * step_row[:, :, None]).reshape(length, channels)
    preact_grad = mixed_grad * silu_slope(preact)
    conv_rows = []
    for index_row in range(tap_count - 1):
        running = jnp.zeros((channels,), jnp.float32)
        for offset in range(tap_count - 1 - index_row, tap_count):
            position = index_row - (tap_count - 1) + offset
            running = running + jnp.where(
                opening[position], conv_weight[offset] * preact_grad[position], 0.0
            )
        conv_rows.append(running)
    conv_grad = jnp.stack(conv_rows)
    return (jnp.concatenate([write_grad, read_grad], axis=1), state_grad, conv_grad)


def shards(
    tokens_in,
    mix_in,
    step_size,
    doc_ids,
    out_grad,
    proj_weight,
    conv_weight,
    decay_rate,
    carried_state,
    carried_conv,
    carry_from,
):
    rows_dev, length, model_width = tokens_in.shape
    head_count = step_size.shape[2]
    slot_count = carried_state.shape[0]
    part_p = carried_state.shape[2]
    nstate = carried_state.shape[3]
    tap_count = conv_weight.shape[0]
    doc_count = lax.axis_size("doc")
    head_dim = part_p * doc_count
    channels = head_count * head_dim
    picker = (carry_from[:, None] == jnp.arange(slot_count, dtype=jnp.int32)[None, :]).astype(
        jnp.bfloat16
    )
    chosen_state = jnp.einsum(
        "rs,shpn->rhpn", picker, carried_state, preferred_element_type=jnp.float32
    ).astype(jnp.bfloat16)
    chosen_conv = jnp.einsum(
        "rs,skhp->rkhp", picker, carried_conv, preferred_element_type=jnp.float32
    ).astype(jnp.bfloat16)
    chosen_state = chosen_state.reshape(slot_count, head_count, part_p * nstate)
    chosen_conv = chosen_conv.reshape(slot_count, (tap_count - 1) * head_count, part_p)
    start_state, start_conv = (
        lax.all_to_all(chosen_state, "doc", split_axis=0, concat_axis=2, tiled=True),
        lax.all_to_all(chosen_conv, "doc", split_axis=0, concat_axis=2, tiled=True),
    )
    start_state = start_state.reshape(rows_dev, head_count, head_dim, nstate)
    start_conv = start_conv.reshape(rows_dev, tap_count - 1, channels)
    flattened = tokens_in.reshape(rows_dev * length, model_width)
    coeff_sum = jnp.dot(
        flattened,
        lax.all_gather(proj_weight, "fsdp", axis=0, tiled=True),
        preferred_element_type=jnp.float32,
    )
    coeff = coeff_sum.astype(jnp.bfloat16).reshape(rows_dev, length, proj_weight.shape[1])
    coeff_grad, state_grad, conv_grad = row_pass(
        coeff[0],
        mix_in[0],
        step_size[0],
        doc_ids[0],
        out_grad[0],
        start_state[0],
        start_conv[0],
        conv_weight,
        decay_rate,
    )
    coeff_grads = [coeff_grad]
    state_grads = [state_grad]
    conv_grads = [conv_grad]
    back_state = (
        jnp.stack(state_grads).astype(jnp.bfloat16).reshape(rows_dev, head_count, head_dim * nstate)
    )
    back_conv = (
        jnp.stack(conv_grads)
        .astype(jnp.bfloat16)
        .reshape(rows_dev, (tap_count - 1) * head_count, head_dim)
    )
    got_state, got_conv = (
        lax.all_to_all(back_state, "doc", split_axis=2, concat_axis=0, tiled=True),
        lax.all_to_all(back_conv, "doc", split_axis=2, concat_axis=0, tiled=True),
    )
    grad_state = jnp.einsum(
        "rs,rx->sx", picker, got_state.reshape(slot_count, -1), preferred_element_type=jnp.float32
    )
    grad_state = grad_state.astype(jnp.bfloat16).reshape(carried_state.shape)
    grad_conv = jnp.einsum(
        "rs,rx->sx", picker, got_conv.reshape(slot_count, -1), preferred_element_type=jnp.float32
    )
    grad_conv = grad_conv.astype(jnp.bfloat16).reshape(carried_conv.shape)
    coeff_flat = jnp.stack(coeff_grads).reshape(rows_dev * length, -1)
    share = lax.psum_scatter(coeff_flat, "fsdp", scatter_dimension=1, tiled=True)
    partial_cols = jnp.einsum(
        "tj,tn->jn", flattened.astype(jnp.float32), share, precision=lax.Precision.HIGHEST
    )
    summed_cols = lax.psum_scatter(partial_cols, "doc", scatter_dimension=0, tiled=True)
    grad_proj = lax.all_to_all(summed_cols, "fsdp", split_axis=0, concat_axis=1, tiled=True)
    return (grad_proj, grad_state, grad_conv)


F32 = jnp.float32
BF16 = jnp.bfloat16
MESH = pl.DeviceIdType.MESH


def dot_nn(a, b, precision=None):
    return lax.dot_general(
        a, b, (((1,), (0,)), ((), ())), precision=precision, preferred_element_type=F32
    )


def dot_nt(a, b):
    return lax.dot_general(a, b, (((1,), (1,)), ((), ())), preferred_element_type=F32)


def dot_tn(a, b):
    return lax.dot_general(a, b, (((0,), (0,)), ((), ())), preferred_element_type=F32)


def iota(shape, axis):
    return lax.broadcasted_iota(jnp.int32, shape, axis)


def layer_kernel(
    docs,
    parts,
    carry_hbm,
    tokens_hbm,
    mix_hbm,
    step_hbm,
    seg_hbm,
    grad_hbm,
    weight_hbm,
    taps_hbm,
    rate_hbm,
    state_hbm,
    conv_hbm,
    fin_own,
    fin_recv,
    sgrad_recv,
    cgrad_recv,
    carry_ref,
    mix_ref,
    step_ref,
    seg_ref,
    grad_ref,
    weight_ref,
    taps_ref,
    rate_ref,
    state_ref,
    conv_ref,
    tok_part,
    tok_cols,
    coeff_partial,
    coeff_recv,
    coeff,
    cg_partial,
    cg_send,
    cg_recv,
    cg,
    state_send,
    state_recv,
    conv_send,
    conv_recv,
    sgrad_send,
    cgrad_send,
    fin_part,
    fin_send,
    ext,
    seg_ext,
    og_scaled,
    val_scaled,
    first_step,
    first_shrink,
    load_sem,
    store_sem,
    part_send_sem,
    part_recv_sem,
    doc_send_sem,
    doc_recv_sem,
):
    d = lax.axis_index("doc")
    f = lax.axis_index("fsdp")
    length, channels = mix_ref.shape
    heads = step_ref.shape[0]
    head_dim = channels // heads
    part_p = head_dim // docs
    width = weight_ref.shape[1]
    nstate = width // 2
    slots = state_ref.shape[0]
    depth = weight_ref.shape[0]
    block = length // parts
    out_rows = fin_own.shape[0]
    taps = taps_ref.shape[0]

    own_columns = pl.ds(pl.multiple_of(f * depth, 128), depth)
    pairs = [
        (carry_hbm, carry_ref),
        (state_hbm, state_ref),
        (conv_hbm, conv_ref),
        (tokens_hbm.at[0, :, own_columns], tok_part),
        (weight_hbm, weight_ref),
        (step_hbm.at[0], step_ref),
        (rate_hbm, rate_ref),
        (seg_hbm, seg_ref),
        (taps_hbm, taps_ref),
        (mix_hbm.at[0], mix_ref),
        (grad_hbm.at[0], grad_ref),
    ]
    for q in range(docs):
        columns = pl.ds(pl.multiple_of((q * parts + f) * out_rows, 128), out_rows)
        pairs.append(
            (tokens_hbm.at[0, :, columns], tok_cols.at[:, pl.ds(q * out_rows, out_rows)])
        )
    loads = [
        pltpu.make_async_copy(src, dst, load_sem.at[i]) for i, (src, dst) in enumerate(pairs)
    ]
    for load in loads:
        load.start()

    barrier = pltpu.get_barrier_semaphore()
    for j in range(1, parts):
        pl.semaphore_signal(
            barrier, inc=1, device_id=(d, lax.rem(f + j, parts)), device_id_type=MESH
        )
    for j in range(1, docs):
        pl.semaphore_signal(
            barrier, inc=1, device_id=(lax.rem(d + j, docs), f), device_id_type=MESH
        )

    def part_copy(phase, j, src, dst):
        return pltpu.make_async_remote_copy(
            src_ref=src,
            dst_ref=dst,
            send_sem=part_send_sem.at[phase, j],
            recv_sem=part_recv_sem.at[phase, j],
            device_id=(d, lax.rem(f + j, parts)),
            device_id_type=MESH,
        )

    def doc_copy(phase, j, src, dst):
        return pltpu.make_async_remote_copy(
            src_ref=src,
            dst_ref=dst,
            send_sem=doc_send_sem.at[phase, j],
            recv_sem=doc_recv_sem.at[phase, j],
            device_id=(lax.rem(d + j, docs), f),
            device_id_type=MESH,
        )

    def rows_of(owner):
        return pl.ds(pl.multiple_of(owner * block, block), block)

    lane = iota((1, channels), 1)
    head_of_lane = lax.div(lane, head_dim)
    lane_in_head = lane - head_of_lane * head_dim
    places = [
        jnp.where(
            jnp.broadcast_to(lane_in_head, (part_p, channels))
            == iota((part_p, channels), 0) + q * part_p,
            1.0,
            0.0,
        ).astype(BF16)
        for q in range(docs)
    ]
    head_rows = (taps - 1) * heads
    own_head = jnp.broadcast_to(head_of_lane, (heads, channels)) == iota((heads, channels), 0)

    for load in loads[:3]:
        load.wait()
    for r in range(slots):
        source = carry_ref[r]
        usable = jnp.where(source >= 0, 1.0, 0.0)
        index = jnp.maximum(source, 0)
        state_send[r] = (state_ref[index].astype(F32) * usable).astype(BF16)
        conv_send[r] = (conv_ref[index].astype(F32) * usable).astype(BF16)

    for load in loads[3:5]:
        load.wait()
    coeff_partial[...] = dot_nn(tok_part[...], weight_ref[...])

    pl.semaphore_wait(barrier, parts - 1 + docs - 1)

    conv_copies = [
        doc_copy(0, j, conv_send.at[lax.rem(d + j, docs)], conv_recv.at[d]) for j in range(1, docs)
    ]
    coeff_copies = [
        part_copy(0, j, coeff_partial.at[rows_of(lax.rem(f + j, parts))], coeff_recv.at[j])
        for j in range(1, parts)
    ]
    state_copies = [
        doc_copy(1, j, state_send.at[lax.rem(d + j, docs)], state_recv.at[:, d])
        for j in range(1, docs)
    ]
    for copy in conv_copies + coeff_copies + state_copies:
        copy.start()
    conv_recv[d] = conv_send[d]
    state_recv[:, d] = state_send[d]

    for load in loads[5:11]:
        load.wait()
    lower = iota((length, length), 0) >= iota((length, length), 1)
    rate = jnp.sum(
        jnp.where(iota((heads, heads), 0) == iota((heads, heads), 1), rate_ref[...], 0.0),
        axis=1,
        keepdims=True,
    )
    steps = step_ref[...]
    log_decay = lax.dot_general(
        -(rate * steps),
        jnp.where(lower, 1.0, 0.0),
        (((1,), (1,)), ((), ())),
        precision=lax.Precision.HIGHEST,
        preferred_element_type=F32,
    )

    def halves(x):
        top = x.astype(BF16).astype(F32)
        both = jnp.concatenate([top, x - top, jnp.zeros((128 - 2 * heads, length), F32)], axis=0)
        return both.T.astype(BF16)

    grow = halves(jnp.exp(log_decay))
    shrink = halves(jnp.exp(-log_decay))
    step_halves = halves(steps)

    seg_row = seg_ref[...].astype(F32)
    seg_cols = jnp.broadcast_to(seg_row, (128, length)).T
    seg_ext[8:, :] = seg_cols
    seg_ext[:8, :] = jnp.broadcast_to(seg_cols[:1], (8, 128))
    opening = seg_cols == seg_cols[:1]

    def scaled_values(preact, step, shrink_factor):
        mixed = (preact / (1.0 + jnp.exp(-preact))).astype(BF16).astype(F32)
        values = (step * mixed).astype(BF16).astype(F32)
        return (values * shrink_factor).astype(BF16)

    ext[:8, :] = jnp.zeros((8, channels), F32)

    def chunk(c, carry):
        lanes = pl.ds(pl.multiple_of(c * 128, 128), 128)
        row = iota((128, 128), 0)
        head = jnp.broadcast_to(
            lax.div(iota((1, 128), 1) + c * 128, head_dim), (128, 128)
        )
        expand = jnp.where((row == head) | (row == head + heads), 1.0, 0.0).astype(BF16)

        def per_channel(both):
            return dot_nn(both, expand)

        ext[8:, lanes] = mix_ref[:, lanes].astype(F32)
        preact = jnp.zeros((length, 128), F32)
        for k in range(taps):
            same = seg_ext[8 - k : 8 - k + length, :] == seg_cols
            window = ext[8 - k : 8 - k + length, lanes]
            preact = preact + jnp.where(same, taps_ref[k : k + 1, lanes] * window, 0.0)
        step_c = per_channel(step_halves)
        shrink_c = per_channel(shrink)
        val_scaled[:, lanes] = scaled_values(preact, step_c, shrink_c)
        og_scaled[:, lanes] = (grad_ref[:, lanes].astype(F32) * per_channel(grow)).astype(BF16)
        first_step[:, lanes] = step_c[:16]
        first_shrink[:, lanes] = shrink_c[:16]
        return carry

    chunks = channels // 128
    lax.fori_loop(0, chunks // 2, chunk, 0)

    for copy in coeff_copies:
        copy.wait_recv()
    total = coeff_partial[rows_of(f)]
    for j in range(1, parts):
        total = total + coeff_recv[j]
    coeff[rows_of(f)] = total.astype(BF16)
    gather_copies = [
        part_copy(1, j, coeff.at[rows_of(f)], coeff.at[rows_of(f)]) for j in range(1, parts)
    ]
    for copy in gather_copies:
        copy.start()

    lax.fori_loop(chunks // 2, chunks, chunk, 0)

    for copy in conv_copies:
        copy.wait_recv()

    spread = jnp.zeros((head_rows, channels), F32)
    for q in range(docs):
        spread = spread + dot_nn(conv_recv[q].reshape(head_rows, part_p), places[q])
    carried_rows = jnp.sum(
        jnp.where(own_head[None], spread.reshape(taps - 1, heads, channels), 0.0), axis=1
    )
    ext[8 - (taps - 1) : 8, :] = carried_rows
    pre = jnp.zeros((16, channels), F32)
    for k in range(taps):
        same = seg_ext[8 - k : 24 - k, :1] == seg_cols[:16, :1]
        window = ext[8 - k : 24 - k, :]
        pre = pre + jnp.where(same, taps_ref[k : k + 1, :] * window, 0.0)
    val_scaled[:16, :] = scaled_values(pre, first_step[...], first_shrink[...])

    upper = iota((length, length), 0) <= iota((length, length), 1)
    same_doc = seg_cols[:, :1] == seg_row
    score_grad = jnp.where(
        lower & same_doc, dot_nt(og_scaled[...], val_scaled[...]), 0.0
    ).astype(BF16)
    score_grad_t = jnp.where(
        upper & same_doc, dot_nt(val_scaled[...], og_scaled[...]), 0.0
    ).astype(BF16)

    for copy in state_copies:
        copy.wait_recv()
    from_state = jnp.where(
        opening, dot_nn(og_scaled[...], state_recv[...].reshape(channels, nstate)), 0.0
    )

    for copy in gather_copies:
        copy.wait_recv()
    write_coeff = coeff[:, :nstate]
    read_coeff = coeff[:, nstate:]
    cg_partial[:, :nstate] = dot_nn(score_grad_t, read_coeff)
    cg_partial[:, nstate:] = dot_nn(score_grad, write_coeff) + from_state
    cg_send[...] = cg_partial[...].astype(BF16)
    sum_copies = [
        part_copy(2, j, cg_send.at[rows_of(lax.rem(f + j, parts))], cg_recv.at[j])
        for j in range(1, parts)
    ]
    for copy in sum_copies:
        copy.start()

    open_read = jnp.where(opening, read_coeff.astype(F32), 0.0).astype(BF16)
    sgrad_send[...] = (
        dot_tn(og_scaled[...], open_read).astype(BF16).reshape(heads, docs, part_p, nstate)
    )
    sgrad_copies = [
        doc_copy(2, j, sgrad_send.at[:, lax.rem(d + j, docs)], sgrad_recv.at[d])
        for j in range(1, docs)
    ]
    for copy in sgrad_copies:
        copy.start()
    first_scores = dot_nt(write_coeff[:16], read_coeff)
    first_seg = jnp.broadcast_to(seg_row, (16, length)) == seg_cols[:16, :1]
    first_allowed = first_seg & (iota((16, length), 1) >= iota((16, length), 0))
    first_scores = jnp.where(first_allowed, first_scores, 0.0).astype(BF16)
    first_grad = dot_nn(first_scores, og_scaled[...])[:8]
    pre = pre[:8]
    gate = 1.0 / (1.0 + jnp.exp(-pre))
    pre_grad = first_grad * first_step[:8] * first_shrink[:8] * gate * (1.0 + pre * (1.0 - gate))
    pre_grad = jnp.where(seg_cols[:8, :1] == seg_cols[:1, :1], pre_grad, 0.0)
    conv_rows = []
    for row in range(taps - 1):
        running = jnp.zeros((1, channels), F32)
        for k in range(taps - 1 - row, taps):
            position = row - (taps - 1) + k
            running = running + taps_ref[k : k + 1, :] * pre_grad[position : position + 1]
        conv_rows.append(
            jnp.where(own_head, jnp.broadcast_to(running, (heads, channels)), 0.0).astype(BF16)
        )
    for q in range(docs):
        for row in range(taps - 1):
            cgrad_send[q, row] = dot_nt(conv_rows[row], places[q]).astype(BF16)
    cgrad_copies = [
        doc_copy(3, j, cgrad_send.at[lax.rem(d + j, docs)], cgrad_recv.at[d])
        for j in range(1, docs)
    ]
    for copy in cgrad_copies:
        copy.start()
    stores = [
        pltpu.make_async_copy(sgrad_send.at[:, d], sgrad_recv.at[d], store_sem.at[0]),
        pltpu.make_async_copy(cgrad_send.at[d], cgrad_recv.at[d], store_sem.at[1]),
    ]
    for store in stores:
        store.start()
    for load in loads[11:]:
        load.wait()
    tok_rows = tok_cols[...].T

    for copy in sum_copies:
        copy.wait_recv()
    total = cg_partial[rows_of(f)]
    for j in range(1, parts):
        total = total + cg_recv[j].astype(F32)
    cg[rows_of(f)] = total.astype(BF16)
    cg_copies = [part_copy(3, j, cg.at[rows_of(f)], cg.at[rows_of(f)]) for j in range(1, parts)]
    for copy in cg_copies:
        copy.start()

    for copy in cg_copies:
        copy.wait_recv()
    product = dot_nn(tok_rows, cg[...]).reshape(docs, out_rows, width)
    fin_send[...] = product.astype(BF16)
    fin_copies = [
        doc_copy(4, j, fin_send.at[lax.rem(d + j, docs)], fin_recv.at[j - 1])
        for j in range(1, docs)
    ]
    for copy in fin_copies:
        copy.start()
    fin_part[...] = product
    stores.append(pltpu.make_async_copy(fin_part.at[d], fin_own, store_sem.at[2]))
    stores[2].start()
    for copy in sgrad_copies + cgrad_copies + fin_copies:
        copy.wait_recv()
    for store in stores:
        store.wait()

    for copies in (
        conv_copies,
        coeff_copies,
        state_copies,
        gather_copies,
        sum_copies,
        sgrad_copies,
        cgrad_copies,
        cg_copies,
        fin_copies,
    ):
        for copy in copies:
            copy.wait_send()


def finish_kernel(
    carry_hbm,
    own_hbm,
    recv_hbm,
    sgrad_hbm,
    cgrad_hbm,
    proj_out,
    state_out,
    conv_out,
    carry_ref,
    own_ref,
    recv_ref,
    sgrad_ref,
    cgrad_ref,
    load_sem,
):
    pairs = (
        (carry_hbm, carry_ref),
        (sgrad_hbm, sgrad_ref),
        (cgrad_hbm, cgrad_ref),
        (own_hbm, own_ref),
        (recv_hbm, recv_ref),
    )
    loads = [
        pltpu.make_async_copy(src, dst, load_sem.at[i]) for i, (src, dst) in enumerate(pairs)
    ]
    for load in loads:
        load.start()
    for load in loads:
        load.wait()
    slots = state_out.shape[0]
    for s in range(slots):
        row_of = jnp.int32(0)
        found = jnp.float32(0.0)
        for r in range(slots):
            hit = carry_ref[r] == s
            row_of = jnp.where(hit, r, row_of)
            found = jnp.where(hit, 1.0, found)
        state_out[s] = (sgrad_ref[row_of].astype(F32) * found).astype(BF16)
        conv_out[s] = (cgrad_ref[row_of].astype(F32) * found).astype(BF16)
    result = own_ref[...]
    for j in range(recv_ref.shape[0]):
        result = result + recv_ref[j].astype(F32)
    proj_out[...] = result


def device_part(docs, parts, *args):
    (
        tokens_in,
        mix_in,
        step_size,
        doc_ids,
        out_grad,
        proj_weight,
        conv_weight,
        decay_rate,
        carried_state,
        carried_conv,
        carry_from,
    ) = args
    rows_dev, length, model_width = tokens_in.shape
    channels = mix_in.shape[2]
    heads = step_size.shape[2]
    depth, width = proj_weight.shape
    slots, _, part_p, nstate = carried_state.shape
    taps = conv_weight.shape[0]
    out_rows = model_width // (docs * parts)
    block = length // parts
    aligned = (
        rows_dev == 1
        and slots == docs
        and part_p % 16 == 0
        and heads % 16 == 0
        and 2 * heads <= 128
        and block % 16 == 0
        and out_rows % 128 == 0
        and depth % 128 == 0
        and nstate == 128
        and channels % 128 == 0
        and taps <= 8
    )
    if not aligned:
        return shards(*args)
    vmem = pl.BlockSpec(memory_space=pltpu.VMEM)
    hbm = pl.BlockSpec(memory_space=pltpu.HBM)
    landed = (
        jax.ShapeDtypeStruct((out_rows, width), F32),
        jax.ShapeDtypeStruct((docs - 1, out_rows, width), BF16),
        jax.ShapeDtypeStruct(carried_state.shape, BF16),
        jax.ShapeDtypeStruct(carried_conv.shape, BF16),
    )
    buffers = pl.pallas_call(
        functools.partial(layer_kernel, docs, parts),
        out_shape=landed,
        in_specs=[hbm] * 11,
        out_specs=(hbm,) * 4,
        scratch_shapes=[
            pltpu.SMEM(carry_from.shape, jnp.int32),
            pltpu.VMEM((length, channels), BF16),
            pltpu.VMEM((heads, length), F32),
            pltpu.VMEM(doc_ids.shape, jnp.int32),
            pltpu.VMEM((length, channels), BF16),
            pltpu.VMEM(proj_weight.shape, BF16),
            pltpu.VMEM(conv_weight.shape, F32),
            pltpu.VMEM((1, heads), F32),
            pltpu.VMEM(carried_state.shape, BF16),
            pltpu.VMEM(carried_conv.shape, BF16),
            pltpu.VMEM((length, depth), BF16),
            pltpu.VMEM((length, docs * out_rows), BF16),
            pltpu.VMEM((length, width), F32),
            pltpu.VMEM((parts, block, width), F32),
            pltpu.VMEM((length, width), BF16),
            pltpu.VMEM((length, width), F32),
            pltpu.VMEM((length, width), BF16),
            pltpu.VMEM((parts, block, width), BF16),
            pltpu.VMEM((length, width), BF16),
            pltpu.VMEM((slots, heads, part_p, nstate), BF16),
            pltpu.VMEM((heads, docs, part_p, nstate), BF16),
            pltpu.VMEM((slots, taps - 1, heads, part_p), BF16),
            pltpu.VMEM((docs, taps - 1, heads, part_p), BF16),
            pltpu.VMEM((heads, docs, part_p, nstate), BF16),
            pltpu.VMEM((docs, taps - 1, heads, part_p), BF16),
            pltpu.VMEM((docs, out_rows, width), F32),
            pltpu.VMEM((docs, out_rows, width), BF16),
            pltpu.VMEM((length + 8, channels), F32),
            pltpu.VMEM((length + 8, 128), F32),
            pltpu.VMEM((length, channels), BF16),
            pltpu.VMEM((length, channels), BF16),
            pltpu.VMEM((16, channels), F32),
            pltpu.VMEM((16, channels), F32),
            pltpu.SemaphoreType.DMA((11 + docs,)),
            pltpu.SemaphoreType.DMA((3,)),
            pltpu.SemaphoreType.DMA((4, parts)),
            pltpu.SemaphoreType.DMA((4, parts)),
            pltpu.SemaphoreType.DMA((5, docs)),
            pltpu.SemaphoreType.DMA((5, docs)),
        ],
        compiler_params=pltpu.CompilerParams(
            collective_id=0, has_side_effects=True, vmem_limit_bytes=60 * 1024 * 1024
        ),
        cost_estimate=pl.CostEstimate(
            flops=2 * length * channels * length * 4, bytes_accessed=4 << 20, transcendentals=0
        ),
    )(
        carry_from,
        tokens_in,
        mix_in,
        jnp.swapaxes(step_size, 1, 2),
        doc_ids,
        out_grad,
        proj_weight,
        conv_weight,
        decay_rate.reshape(1, heads),
        carried_state,
        carried_conv,
    )
    return pl.pallas_call(
        finish_kernel,
        out_shape=(
            jax.ShapeDtypeStruct((out_rows, width), F32),
            jax.ShapeDtypeStruct(carried_state.shape, BF16),
            jax.ShapeDtypeStruct(carried_conv.shape, BF16),
        ),
        in_specs=[hbm] * 5,
        out_specs=(vmem,) * 3,
        scratch_shapes=[pltpu.SMEM(carry_from.shape, jnp.int32)]
        + [pltpu.VMEM(leaf.shape, leaf.dtype) for leaf in landed]
        + [pltpu.SemaphoreType.DMA((5,))],
        compiler_params=pltpu.CompilerParams(vmem_limit_bytes=60 * 1024 * 1024),
    )(carry_from, *buffers)


def solution(mesh):
    return jax.shard_map(
        functools.partial(device_part, mesh.shape["doc"], mesh.shape["fsdp"]),
        mesh=mesh,
        in_specs=(
            P("doc", None, None),
            P("doc", None, "fsdp"),
            P("doc", None, "fsdp"),
            P("doc", None),
            P("doc", None, "fsdp"),
            P("fsdp", None),
            P(None, "fsdp"),
            P("fsdp"),
            P(None, "fsdp", "doc", None),
            P(None, None, "fsdp", "doc"),
            P(),
        ),
        out_specs=(
            P(("doc", "fsdp"), None),
            P(None, "fsdp", "doc", None),
            P(None, None, "fsdp", "doc"),
        ),
        check_vma=False,
    )
```

```python
import functools

import jax
import jax.numpy as jnp
from jax import lax
from jax.experimental import pallas as pl
from jax.experimental.pallas import tpu as pltpu
from jax.sharding import PartitionSpec as P


def silu_slope(value):
    sigmoid_value = jax.nn.sigmoid(value)
    return sigmoid_value * (1.0 + value * (1.0 - sigmoid_value))


def conv_masks(seg_row, tap_count):
    length = seg_row.shape[0]
    opening = seg_row == seg_row[0]
    tap_masks = []
    for offset in range(tap_count):
        earlier = jnp.concatenate([jnp.full((offset,), -1, jnp.int32), seg_row[: length - offset]])
        inside = jnp.arange(length) >= offset
        tap_masks.append(jnp.where(inside, earlier == seg_row, opening))
    return (opening, tap_masks)


def row_pass(
    coeff, mix_row, step_row, seg_row, grad_rows, state_zero, conv_zero, conv_weight, decay_rate
):
    length, channels = mix_row.shape
    head_count = step_row.shape[1]
    head_dim = channels // head_count
    tap_count = conv_weight.shape[0]
    nstate = coeff.shape[1] // 2
    opening, tap_masks = conv_masks(seg_row, tap_count)
    extended = jnp.concatenate([conv_zero, mix_row], axis=0).astype(jnp.float32)
    preact = jnp.zeros((length, channels), jnp.float32)
    for offset in range(tap_count):
        window = extended[tap_count - 1 - offset : tap_count - 1 - offset + length]
        preact = preact + jnp.where(
            tap_masks[offset][:, None], conv_weight[offset][None, :] * window, 0.0
        )
    mixed_rows = jax.nn.silu(preact).astype(jnp.bfloat16)
    values = (
        step_row[:, :, None] * mixed_rows.reshape(length, head_count, head_dim).astype(jnp.float32)
    ).astype(jnp.bfloat16)
    write_coeff = coeff[:, :nstate]
    read_coeff = coeff[:, nstate:]
    scores = jnp.dot(read_coeff, write_coeff.T, preferred_element_type=jnp.float32)
    log_decay = jnp.cumsum(-(decay_rate[None, :] * step_row), axis=0).T
    lower = jnp.arange(length)[:, None] >= jnp.arange(length)[None, :]
    allowed = lower & (seg_row[:, None] == seg_row[None, :])
    spread = log_decay[:, :, None] - log_decay[:, None, :]
    decays = jnp.where(allowed[None], jnp.exp(jnp.where(allowed[None], spread, 0.0)), 0.0)
    edge_weight = jnp.where(opening[None, :], jnp.exp(log_decay), 0.0)
    weighted = (decays * scores[None]).astype(jnp.bfloat16)
    grad_heads = grad_rows.reshape(length, head_count, head_dim)
    values_grad = jnp.einsum(
        "hts,thp->shp", weighted, grad_heads, preferred_element_type=jnp.float32
    )
    products = jnp.einsum("thp,shp->hts", grad_heads, values, preferred_element_type=jnp.float32)
    score_grad = jnp.sum(decays * products, axis=0)
    carried = jnp.einsum("thp,hpn->thn", grad_heads, state_zero, preferred_element_type=jnp.float32)
    read_grad = jnp.dot(
        score_grad, write_coeff.astype(jnp.float32), precision=lax.Precision.HIGHEST
    )
    read_grad = read_grad + jnp.sum(edge_weight.T[:, :, None] * carried, axis=1)
    write_grad = jnp.dot(
        score_grad.T, read_coeff.astype(jnp.float32), precision=lax.Precision.HIGHEST
    )
    scaled = edge_weight.T[:, :, None] * grad_heads.astype(jnp.float32)
    state_grad = jnp.einsum(
        "thp,tn->hpn", scaled, read_coeff.astype(jnp.float32), precision=lax.Precision.HIGHEST
    )
    mixed_grad = (values_grad * step_row[:, :, None]).reshape(length, channels)
    preact_grad = mixed_grad * silu_slope(preact)
    conv_rows = []
    for index_row in range(tap_count - 1):
        running = jnp.zeros((channels,), jnp.float32)
        for offset in range(tap_count - 1 - index_row, tap_count):
            position = index_row - (tap_count - 1) + offset
            running = running + jnp.where(
                opening[position], conv_weight[offset] * preact_grad[position], 0.0
            )
        conv_rows.append(running)
    conv_grad = jnp.stack(conv_rows)
    return (jnp.concatenate([write_grad, read_grad], axis=1), state_grad, conv_grad)


def shards(
    tokens_in,
    mix_in,
    step_size,
    doc_ids,
    out_grad,
    proj_weight,
    conv_weight,
    decay_rate,
    carried_state,
    carried_conv,
    carry_from,
):
    rows_dev, length, model_width = tokens_in.shape
    head_count = step_size.shape[2]
    slot_count = carried_state.shape[0]
    part_p = carried_state.shape[2]
    nstate = carried_state.shape[3]
    tap_count = conv_weight.shape[0]
    doc_count = lax.axis_size("doc")
    head_dim = part_p * doc_count
    channels = head_count * head_dim
    picker = (carry_from[:, None] == jnp.arange(slot_count, dtype=jnp.int32)[None, :]).astype(
        jnp.bfloat16
    )
    chosen_state = jnp.einsum(
        "rs,shpn->rhpn", picker, carried_state, preferred_element_type=jnp.float32
    ).astype(jnp.bfloat16)
    chosen_conv = jnp.einsum(
        "rs,skhp->rkhp", picker, carried_conv, preferred_element_type=jnp.float32
    ).astype(jnp.bfloat16)
    chosen_state = chosen_state.reshape(slot_count, head_count, part_p * nstate)
    chosen_conv = chosen_conv.reshape(slot_count, (tap_count - 1) * head_count, part_p)
    start_state, start_conv = (
        lax.all_to_all(chosen_state, "doc", split_axis=0, concat_axis=2, tiled=True),
        lax.all_to_all(chosen_conv, "doc", split_axis=0, concat_axis=2, tiled=True),
    )
    start_state = start_state.reshape(rows_dev, head_count, head_dim, nstate)
    start_conv = start_conv.reshape(rows_dev, tap_count - 1, channels)
    flattened = tokens_in.reshape(rows_dev * length, model_width)
    coeff_sum = jnp.dot(
        flattened,
        lax.all_gather(proj_weight, "fsdp", axis=0, tiled=True),
        preferred_element_type=jnp.float32,
    )
    coeff = coeff_sum.astype(jnp.bfloat16).reshape(rows_dev, length, proj_weight.shape[1])
    coeff_grad, state_grad, conv_grad = row_pass(
        coeff[0],
        mix_in[0],
        step_size[0],
        doc_ids[0],
        out_grad[0],
        start_state[0],
        start_conv[0],
        conv_weight,
        decay_rate,
    )
    coeff_grads = [coeff_grad]
    state_grads = [state_grad]
    conv_grads = [conv_grad]
    back_state = (
        jnp.stack(state_grads).astype(jnp.bfloat16).reshape(rows_dev, head_count, head_dim * nstate)
    )
    back_conv = (
        jnp.stack(conv_grads)
        .astype(jnp.bfloat16)
        .reshape(rows_dev, (tap_count - 1) * head_count, head_dim)
    )
    got_state, got_conv = (
        lax.all_to_all(back_state, "doc", split_axis=2, concat_axis=0, tiled=True),
        lax.all_to_all(back_conv, "doc", split_axis=2, concat_axis=0, tiled=True),
    )
    grad_state = jnp.einsum(
        "rs,rx->sx", picker, got_state.reshape(slot_count, -1), preferred_element_type=jnp.float32
    )
    grad_state = grad_state.astype(jnp.bfloat16).reshape(carried_state.shape)
    grad_conv = jnp.einsum(
        "rs,rx->sx", picker, got_conv.reshape(slot_count, -1), preferred_element_type=jnp.float32
    )
    grad_conv = grad_conv.astype(jnp.bfloat16).reshape(carried_conv.shape)
    coeff_flat = jnp.stack(coeff_grads).reshape(rows_dev * length, -1)
    share = lax.psum_scatter(coeff_flat, "fsdp", scatter_dimension=1, tiled=True)
    partial_cols = jnp.einsum(
        "tj,tn->jn", flattened.astype(jnp.float32), share, precision=lax.Precision.HIGHEST
    )
    summed_cols = lax.psum_scatter(partial_cols, "doc", scatter_dimension=0, tiled=True)
    grad_proj = lax.all_to_all(summed_cols, "fsdp", split_axis=0, concat_axis=1, tiled=True)
    return (grad_proj, grad_state, grad_conv)


F32 = jnp.float32
BF16 = jnp.bfloat16
MESH = pl.DeviceIdType.MESH


def dot_nn(a, b, precision=None):
    return lax.dot_general(
        a, b, (((1,), (0,)), ((), ())), precision=precision, preferred_element_type=F32
    )


def dot_nt(a, b):
    return lax.dot_general(a, b, (((1,), (1,)), ((), ())), preferred_element_type=F32)


def dot_tn(a, b):
    return lax.dot_general(a, b, (((0,), (0,)), ((), ())), preferred_element_type=F32)


def iota(shape, axis):
    return lax.broadcasted_iota(jnp.int32, shape, axis)


def layer_kernel(
    docs,
    parts,
    carry_hbm,
    tokens_hbm,
    mix_hbm,
    step_hbm,
    seg_hbm,
    grad_hbm,
    weight_hbm,
    taps_hbm,
    rate_hbm,
    state_hbm,
    conv_hbm,
    fin_own,
    fin_recv,
    sgrad_recv,
    cgrad_recv,
    carry_ref,
    mix_ref,
    step_ref,
    seg_ref,
    grad_ref,
    weight_ref,
    taps_ref,
    rate_ref,
    state_ref,
    conv_ref,
    tok_part,
    tok_cols,
    coeff_partial,
    coeff_send,
    coeff_recv,
    coeff,
    cg_partial,
    cg_send,
    cg_recv,
    cg,
    state_send,
    state_recv,
    conv_send,
    conv_recv,
    sgrad_send,
    cgrad_send,
    fin_part,
    fin_send,
    ext,
    seg_ext,
    og_scaled,
    val_scaled,
    first_step,
    first_shrink,
    load_sem,
    store_sem,
    part_send_sem,
    part_recv_sem,
    doc_send_sem,
    doc_recv_sem,
):
    d = lax.axis_index("doc")
    f = lax.axis_index("fsdp")
    length, channels = mix_ref.shape
    heads = step_ref.shape[0]
    head_dim = channels // heads
    part_p = head_dim // docs
    width = weight_ref.shape[1]
    nstate = width // 2
    slots = state_ref.shape[0]
    depth = weight_ref.shape[0]
    block = length // parts
    out_rows = fin_own.shape[0]
    taps = taps_ref.shape[0]

    own_columns = pl.ds(pl.multiple_of(f * depth, 128), depth)
    pairs = [
        (carry_hbm, carry_ref),
        (state_hbm, state_ref),
        (conv_hbm, conv_ref),
        (tokens_hbm.at[0, :, own_columns], tok_part),
        (weight_hbm, weight_ref),
        (step_hbm.at[0], step_ref),
        (rate_hbm, rate_ref),
        (seg_hbm, seg_ref),
        (taps_hbm, taps_ref),
        (mix_hbm.at[0], mix_ref),
        (grad_hbm.at[0], grad_ref),
    ]
    for q in range(docs):
        columns = pl.ds(pl.multiple_of((q * parts + f) * out_rows, 128), out_rows)
        pairs.append(
            (tokens_hbm.at[0, :, columns], tok_cols.at[:, pl.ds(q * out_rows, out_rows)])
        )
    loads = [
        pltpu.make_async_copy(src, dst, load_sem.at[i]) for i, (src, dst) in enumerate(pairs)
    ]
    for load in loads:
        load.start()

    barrier = pltpu.get_barrier_semaphore()
    for j in range(1, parts):
        pl.semaphore_signal(
            barrier, inc=1, device_id=(d, lax.rem(f + j, parts)), device_id_type=MESH
        )
    for j in range(1, docs):
        pl.semaphore_signal(
            barrier, inc=1, device_id=(lax.rem(d + j, docs), f), device_id_type=MESH
        )

    def part_copy(phase, j, src, dst):
        return pltpu.make_async_remote_copy(
            src_ref=src,
            dst_ref=dst,
            send_sem=part_send_sem.at[phase, j],
            recv_sem=part_recv_sem.at[phase, j],
            device_id=(d, lax.rem(f + j, parts)),
            device_id_type=MESH,
        )

    def doc_copy(phase, j, src, dst):
        return pltpu.make_async_remote_copy(
            src_ref=src,
            dst_ref=dst,
            send_sem=doc_send_sem.at[phase, j],
            recv_sem=doc_recv_sem.at[phase, j],
            device_id=(lax.rem(d + j, docs), f),
            device_id_type=MESH,
        )

    def rows_of(owner):
        return pl.ds(pl.multiple_of(owner * block, block), block)

    lane = iota((1, channels), 1)
    head_of_lane = lax.div(lane, head_dim)
    lane_in_head = lane - head_of_lane * head_dim
    places = [
        jnp.where(
            jnp.broadcast_to(lane_in_head, (part_p, channels))
            == iota((part_p, channels), 0) + q * part_p,
            1.0,
            0.0,
        ).astype(BF16)
        for q in range(docs)
    ]
    head_rows = (taps - 1) * heads
    own_head = jnp.broadcast_to(head_of_lane, (heads, channels)) == iota((heads, channels), 0)

    for load in loads[:3]:
        load.wait()
    for r in range(slots):
        source = carry_ref[r]
        usable = jnp.where(source >= 0, 1.0, 0.0)
        index = jnp.maximum(source, 0)
        state_send[r] = (state_ref[index].astype(F32) * usable).astype(BF16)
        conv_send[r] = (conv_ref[index].astype(F32) * usable).astype(BF16)

    for load in loads[3:5]:
        load.wait()
    coeff_partial[...] = dot_nn(tok_part[...], weight_ref[...])
    coeff_send[...] = coeff_partial[...].astype(BF16)

    pl.semaphore_wait(barrier, parts - 1 + docs - 1)

    conv_copies = [
        doc_copy(0, j, conv_send.at[lax.rem(d + j, docs)], conv_recv.at[d]) for j in range(1, docs)
    ]
    coeff_copies = [
        part_copy(0, j, coeff_send.at[rows_of(lax.rem(f + j, parts))], coeff_recv.at[j])
        for j in range(1, parts)
    ]
    state_copies = [
        doc_copy(1, j, state_send.at[lax.rem(d + j, docs)], state_recv.at[:, d])
        for j in range(1, docs)
    ]
    for copy in conv_copies + coeff_copies + state_copies:
        copy.start()
    conv_recv[d] = conv_send[d]
    state_recv[:, d] = state_send[d]

    for load in loads[5:11]:
        load.wait()
    lower = iota((length, length), 0) >= iota((length, length), 1)
    rate = jnp.sum(
        jnp.where(iota((heads, heads), 0) == iota((heads, heads), 1), rate_ref[...], 0.0),
        axis=1,
        keepdims=True,
    )
    steps = step_ref[...]
    log_decay = lax.dot_general(
        -(rate * steps),
        jnp.where(lower, 1.0, 0.0),
        (((1,), (1,)), ((), ())),
        precision=lax.Precision.HIGHEST,
        preferred_element_type=F32,
    )

    def halves(x):
        top = x.astype(BF16).astype(F32)
        both = jnp.concatenate([top, x - top, jnp.zeros((128 - 2 * heads, length), F32)], axis=0)
        return both.T.astype(BF16)

    grow = halves(jnp.exp(log_decay))
    shrink = halves(jnp.exp(-log_decay))
    step_halves = halves(steps)

    seg_row = seg_ref[...].astype(F32)
    seg_cols = jnp.broadcast_to(seg_row, (128, length)).T
    seg_ext[8:, :] = seg_cols
    seg_ext[:8, :] = jnp.broadcast_to(seg_cols[:1], (8, 128))
    opening = seg_cols == seg_cols[:1]

    def scaled_values(preact, step, shrink_factor):
        mixed = (preact / (1.0 + jnp.exp(-preact))).astype(BF16).astype(F32)
        values = (step * mixed).astype(BF16).astype(F32)
        return (values * shrink_factor).astype(BF16)

    ext[:8, :] = jnp.zeros((8, channels), F32)

    def chunk(c, carry):
        lanes = pl.ds(pl.multiple_of(c * 128, 128), 128)
        row = iota((128, 128), 0)
        head = jnp.broadcast_to(
            lax.div(iota((1, 128), 1) + c * 128, head_dim), (128, 128)
        )
        expand = jnp.where((row == head) | (row == head + heads), 1.0, 0.0).astype(BF16)

        def per_channel(both):
            return dot_nn(both, expand)

        ext[8:, lanes] = mix_ref[:, lanes].astype(F32)
        preact = jnp.zeros((length, 128), F32)
        for k in range(taps):
            same = seg_ext[8 - k : 8 - k + length, :] == seg_cols
            window = ext[8 - k : 8 - k + length, lanes]
            preact = preact + jnp.where(same, taps_ref[k : k + 1, lanes] * window, 0.0)
        step_c = per_channel(step_halves)
        shrink_c = per_channel(shrink)
        val_scaled[:, lanes] = scaled_values(preact, step_c, shrink_c)
        og_scaled[:, lanes] = (grad_ref[:, lanes].astype(F32) * per_channel(grow)).astype(BF16)
        first_step[:, lanes] = step_c[:16]
        first_shrink[:, lanes] = shrink_c[:16]
        return carry

    chunks = channels // 128
    lax.fori_loop(0, chunks // 2, chunk, 0)

    for copy in coeff_copies:
        copy.wait_recv()
    total = coeff_partial[rows_of(f)]
    for j in range(1, parts):
        total = total + coeff_recv[j].astype(F32)
    coeff[rows_of(f)] = total.astype(BF16)
    gather_copies = [
        part_copy(1, j, coeff.at[rows_of(f)], coeff.at[rows_of(f)]) for j in range(1, parts)
    ]
    for copy in gather_copies:
        copy.start()

    lax.fori_loop(chunks // 2, chunks, chunk, 0)

    for copy in gather_copies:
        copy.wait_recv()
    write_coeff = coeff[:, :nstate]
    read_coeff = coeff[:, nstate:]
    open_read = jnp.where(opening, read_coeff.astype(F32), 0.0).astype(BF16)
    sgrad_send[...] = (
        dot_tn(og_scaled[...], open_read).astype(BF16).reshape(heads, docs, part_p, nstate)
    )
    sgrad_copies = [
        doc_copy(2, j, sgrad_send.at[:, lax.rem(d + j, docs)], sgrad_recv.at[d])
        for j in range(1, docs)
    ]
    for copy in sgrad_copies:
        copy.start()

    for copy in conv_copies:
        copy.wait_recv()

    spread = jnp.zeros((head_rows, channels), F32)
    for q in range(docs):
        spread = spread + dot_nn(conv_recv[q].reshape(head_rows, part_p), places[q])
    carried_rows = jnp.sum(
        jnp.where(own_head[None], spread.reshape(taps - 1, heads, channels), 0.0), axis=1
    )
    ext[8 - (taps - 1) : 8, :] = carried_rows
    pre = jnp.zeros((16, channels), F32)
    for k in range(taps):
        same = seg_ext[8 - k : 24 - k, :1] == seg_cols[:16, :1]
        window = ext[8 - k : 24 - k, :]
        pre = pre + jnp.where(same, taps_ref[k : k + 1, :] * window, 0.0)
    val_scaled[:16, :] = scaled_values(pre, first_step[...], first_shrink[...])

    upper = iota((length, length), 0) <= iota((length, length), 1)
    same_doc = seg_cols[:, :1] == seg_row
    score_grad = jnp.where(
        lower & same_doc, dot_nt(og_scaled[...], val_scaled[...]), 0.0
    ).astype(BF16)
    score_grad_t = jnp.where(
        upper & same_doc, dot_nt(val_scaled[...], og_scaled[...]), 0.0
    ).astype(BF16)

    halves_of = [pl.ds(0, nstate), pl.ds(nstate, nstate)]
    sum_copies = [[], []]

    def send_half(half, value):
        columns = halves_of[half]
        cg_partial[:, columns] = value
        cg_send[:, columns] = value.astype(BF16)
        for j in range(1, parts):
            copy = part_copy(
                2 + half,
                j,
                cg_send.at[rows_of(lax.rem(f + j, parts)), columns],
                cg_recv.at[j, :, columns],
            )
            copy.start()
            sum_copies[half].append(copy)

    send_half(0, dot_nn(score_grad_t, read_coeff))
    for copy in state_copies:
        copy.wait_recv()
    from_state = jnp.where(
        opening, dot_nn(og_scaled[...], state_recv[...].reshape(channels, nstate)), 0.0
    )
    send_half(1, dot_nn(score_grad, write_coeff) + from_state)

    first_scores = dot_nt(write_coeff[:16], read_coeff)
    first_seg = jnp.broadcast_to(seg_row, (16, length)) == seg_cols[:16, :1]
    first_allowed = first_seg & (iota((16, length), 1) >= iota((16, length), 0))
    first_scores = jnp.where(first_allowed, first_scores, 0.0).astype(BF16)
    first_grad = dot_nn(first_scores, og_scaled[...])[:8]
    pre = pre[:8]
    gate = 1.0 / (1.0 + jnp.exp(-pre))
    pre_grad = first_grad * first_step[:8] * first_shrink[:8] * gate * (1.0 + pre * (1.0 - gate))
    pre_grad = jnp.where(seg_cols[:8, :1] == seg_cols[:1, :1], pre_grad, 0.0)
    conv_rows = []
    for row in range(taps - 1):
        running = jnp.zeros((1, channels), F32)
        for k in range(taps - 1 - row, taps):
            position = row - (taps - 1) + k
            running = running + taps_ref[k : k + 1, :] * pre_grad[position : position + 1]
        conv_rows.append(
            jnp.where(own_head, jnp.broadcast_to(running, (heads, channels)), 0.0).astype(BF16)
        )
    for q in range(docs):
        for row in range(taps - 1):
            cgrad_send[q, row] = dot_nt(conv_rows[row], places[q]).astype(BF16)
    cgrad_copies = [
        doc_copy(3, j, cgrad_send.at[lax.rem(d + j, docs)], cgrad_recv.at[d])
        for j in range(1, docs)
    ]
    for copy in cgrad_copies:
        copy.start()
    stores = [
        pltpu.make_async_copy(sgrad_send.at[:, d], sgrad_recv.at[d], store_sem.at[0]),
        pltpu.make_async_copy(cgrad_send.at[d], cgrad_recv.at[d], store_sem.at[1]),
    ]
    for store in stores:
        store.start()
    for load in loads[11:]:
        load.wait()
    tok_rows = tok_cols[...].T

    cg_copies = [[], []]
    for half in range(2):
        columns = halves_of[half]
        for copy in sum_copies[half]:
            copy.wait_recv()
        total = cg_partial[rows_of(f), columns]
        for j in range(1, parts):
            total = total + cg_recv[j, :, columns].astype(F32)
        cg[rows_of(f), columns] = total.astype(BF16)
        own = cg.at[rows_of(f), columns]
        for j in range(1, parts):
            copy = part_copy(4 + half, j, own, own)
            copy.start()
            cg_copies[half].append(copy)

    fin_copies = []
    for half in range(2):
        columns = halves_of[half]
        for copy in cg_copies[half]:
            copy.wait_recv()
        product = dot_nn(tok_rows, cg[:, columns]).reshape(docs, out_rows, nstate)
        fin_send[:, :, columns] = product.astype(BF16)
        for j in range(1, docs):
            copy = doc_copy(
                4 + half,
                j,
                fin_send.at[lax.rem(d + j, docs), :, columns],
                fin_recv.at[j - 1, :, columns],
            )
            copy.start()
            fin_copies.append(copy)
        fin_part[:, :, columns] = product
    stores.append(pltpu.make_async_copy(fin_part.at[d], fin_own, store_sem.at[2]))
    stores[2].start()
    for copy in sgrad_copies + cgrad_copies + fin_copies:
        copy.wait_recv()
    for store in stores:
        store.wait()

    for copies in (
        conv_copies,
        coeff_copies,
        state_copies,
        gather_copies,
        *sum_copies,
        sgrad_copies,
        cgrad_copies,
        *cg_copies,
        fin_copies,
    ):
        for copy in copies:
            copy.wait_send()


def finish_kernel(
    carry_hbm,
    own_hbm,
    recv_hbm,
    sgrad_hbm,
    cgrad_hbm,
    proj_out,
    state_out,
    conv_out,
    carry_ref,
    own_ref,
    recv_ref,
    sgrad_ref,
    cgrad_ref,
    load_sem,
):
    pairs = (
        (carry_hbm, carry_ref),
        (sgrad_hbm, sgrad_ref),
        (cgrad_hbm, cgrad_ref),
        (own_hbm, own_ref),
        (recv_hbm, recv_ref),
    )
    loads = [
        pltpu.make_async_copy(src, dst, load_sem.at[i]) for i, (src, dst) in enumerate(pairs)
    ]
    for load in loads:
        load.start()
    for load in loads:
        load.wait()
    slots = state_out.shape[0]
    for s in range(slots):
        row_of = jnp.int32(0)
        found = jnp.float32(0.0)
        for r in range(slots):
            hit = carry_ref[r] == s
            row_of = jnp.where(hit, r, row_of)
            found = jnp.where(hit, 1.0, found)
        state_out[s] = (sgrad_ref[row_of].astype(F32) * found).astype(BF16)
        conv_out[s] = (cgrad_ref[row_of].astype(F32) * found).astype(BF16)
    result = own_ref[...]
    for j in range(recv_ref.shape[0]):
        result = result + recv_ref[j].astype(F32)
    proj_out[...] = result


def device_part(docs, parts, *args):
    (
        tokens_in,
        mix_in,
        step_size,
        doc_ids,
        out_grad,
        proj_weight,
        conv_weight,
        decay_rate,
        carried_state,
        carried_conv,
        carry_from,
    ) = args
    rows_dev, length, model_width = tokens_in.shape
    channels = mix_in.shape[2]
    heads = step_size.shape[2]
    depth, width = proj_weight.shape
    slots, _, part_p, nstate = carried_state.shape
    taps = conv_weight.shape[0]
    out_rows = model_width // (docs * parts)
    block = length // parts
    aligned = (
        rows_dev == 1
        and slots == docs
        and part_p % 16 == 0
        and heads % 16 == 0
        and 2 * heads <= 128
        and block % 16 == 0
        and out_rows % 128 == 0
        and depth % 128 == 0
        and nstate == 128
        and channels % 128 == 0
        and taps <= 8
    )
    if not aligned:
        return shards(*args)
    vmem = pl.BlockSpec(memory_space=pltpu.VMEM)
    hbm = pl.BlockSpec(memory_space=pltpu.HBM)
    landed = (
        jax.ShapeDtypeStruct((out_rows, width), F32),
        jax.ShapeDtypeStruct((docs - 1, out_rows, width), BF16),
        jax.ShapeDtypeStruct(carried_state.shape, BF16),
        jax.ShapeDtypeStruct(carried_conv.shape, BF16),
    )
    buffers = pl.pallas_call(
        functools.partial(layer_kernel, docs, parts),
        out_shape=landed,
        in_specs=[hbm] * 11,
        out_specs=(hbm,) * 4,
        scratch_shapes=[
            pltpu.SMEM(carry_from.shape, jnp.int32),
            pltpu.VMEM((length, channels), BF16),
            pltpu.VMEM((heads, length), F32),
            pltpu.VMEM(doc_ids.shape, jnp.int32),
            pltpu.VMEM((length, channels), BF16),
            pltpu.VMEM(proj_weight.shape, BF16),
            pltpu.VMEM(conv_weight.shape, F32),
            pltpu.VMEM((1, heads), F32),
            pltpu.VMEM(carried_state.shape, BF16),
            pltpu.VMEM(carried_conv.shape, BF16),
            pltpu.VMEM((length, depth), BF16),
            pltpu.VMEM((length, docs * out_rows), BF16),
            pltpu.VMEM((length, width), F32),
            pltpu.VMEM((length, width), BF16),
            pltpu.VMEM((parts, block, width), BF16),
            pltpu.VMEM((length, width), BF16),
            pltpu.VMEM((length, width), F32),
            pltpu.VMEM((length, width), BF16),
            pltpu.VMEM((parts, block, width), BF16),
            pltpu.VMEM((length, width), BF16),
            pltpu.VMEM((slots, heads, part_p, nstate), BF16),
            pltpu.VMEM((heads, docs, part_p, nstate), BF16),
            pltpu.VMEM((slots, taps - 1, heads, part_p), BF16),
            pltpu.VMEM((docs, taps - 1, heads, part_p), BF16),
            pltpu.VMEM((heads, docs, part_p, nstate), BF16),
            pltpu.VMEM((docs, taps - 1, heads, part_p), BF16),
            pltpu.VMEM((docs, out_rows, width), F32),
            pltpu.VMEM((docs, out_rows, width), BF16),
            pltpu.VMEM((length + 8, channels), F32),
            pltpu.VMEM((length + 8, 128), F32),
            pltpu.VMEM((length, channels), BF16),
            pltpu.VMEM((length, channels), BF16),
            pltpu.VMEM((16, channels), F32),
            pltpu.VMEM((16, channels), F32),
            pltpu.SemaphoreType.DMA((11 + docs,)),
            pltpu.SemaphoreType.DMA((3,)),
            pltpu.SemaphoreType.DMA((6, parts)),
            pltpu.SemaphoreType.DMA((6, parts)),
            pltpu.SemaphoreType.DMA((6, docs)),
            pltpu.SemaphoreType.DMA((6, docs)),
        ],
        compiler_params=pltpu.CompilerParams(
            collective_id=0, has_side_effects=True, vmem_limit_bytes=60 * 1024 * 1024
        ),
        cost_estimate=pl.CostEstimate(
            flops=2 * length * channels * length * 4, bytes_accessed=4 << 20, transcendentals=0
        ),
    )(
        carry_from,
        tokens_in,
        mix_in,
        jnp.swapaxes(step_size, 1, 2),
        doc_ids,
        out_grad,
        proj_weight,
        conv_weight,
        decay_rate.reshape(1, heads),
        carried_state,
        carried_conv,
    )
    return pl.pallas_call(
        finish_kernel,
        out_shape=(
            jax.ShapeDtypeStruct((out_rows, width), F32),
            jax.ShapeDtypeStruct(carried_state.shape, BF16),
            jax.ShapeDtypeStruct(carried_conv.shape, BF16),
        ),
        in_specs=[hbm] * 5,
        out_specs=(vmem,) * 3,
        scratch_shapes=[pltpu.SMEM(carry_from.shape, jnp.int32)]
        + [pltpu.VMEM(leaf.shape, leaf.dtype) for leaf in landed]
        + [pltpu.SemaphoreType.DMA((5,))],
        compiler_params=pltpu.CompilerParams(vmem_limit_bytes=60 * 1024 * 1024),
    )(carry_from, *buffers)


def solution(mesh):
    return jax.shard_map(
        functools.partial(device_part, mesh.shape["doc"], mesh.shape["fsdp"]),
        mesh=mesh,
        in_specs=(
            P("doc", None, None),
            P("doc", None, "fsdp"),
            P("doc", None, "fsdp"),
            P("doc", None),
            P("doc", None, "fsdp"),
            P("fsdp", None),
            P(None, "fsdp"),
            P("fsdp"),
            P(None, "fsdp", "doc", None),
            P(None, None, "fsdp", "doc"),
            P(),
        ),
        out_specs=(
            P(("doc", "fsdp"), None),
            P(None, "fsdp", "doc", None),
            P(None, None, "fsdp", "doc"),
        ),
        check_vma=False,
    )
```

```python
import functools

import jax
import jax.numpy as jnp
from jax import lax
from jax.experimental import pallas as pl
from jax.experimental.pallas import tpu as pltpu
from jax.sharding import PartitionSpec as P


def silu_slope(value):
    sigmoid_value = jax.nn.sigmoid(value)
    return sigmoid_value * (1.0 + value * (1.0 - sigmoid_value))


def conv_masks(seg_row, tap_count):
    length = seg_row.shape[0]
    opening = seg_row == seg_row[0]
    tap_masks = []
    for offset in range(tap_count):
        earlier = jnp.concatenate([jnp.full((offset,), -1, jnp.int32), seg_row[: length - offset]])
        inside = jnp.arange(length) >= offset
        tap_masks.append(jnp.where(inside, earlier == seg_row, opening))
    return (opening, tap_masks)


def row_pass(
    coeff, mix_row, step_row, seg_row, grad_rows, state_zero, conv_zero, conv_weight, decay_rate
):
    length, channels = mix_row.shape
    head_count = step_row.shape[1]
    head_dim = channels // head_count
    tap_count = conv_weight.shape[0]
    nstate = coeff.shape[1] // 2
    opening, tap_masks = conv_masks(seg_row, tap_count)
    extended = jnp.concatenate([conv_zero, mix_row], axis=0).astype(jnp.float32)
    preact = jnp.zeros((length, channels), jnp.float32)
    for offset in range(tap_count):
        window = extended[tap_count - 1 - offset : tap_count - 1 - offset + length]
        preact = preact + jnp.where(
            tap_masks[offset][:, None], conv_weight[offset][None, :] * window, 0.0
        )
    mixed_rows = jax.nn.silu(preact).astype(jnp.bfloat16)
    values = (
        step_row[:, :, None] * mixed_rows.reshape(length, head_count, head_dim).astype(jnp.float32)
    ).astype(jnp.bfloat16)
    write_coeff = coeff[:, :nstate]
    read_coeff = coeff[:, nstate:]
    scores = jnp.dot(read_coeff, write_coeff.T, preferred_element_type=jnp.float32)
    log_decay = jnp.cumsum(-(decay_rate[None, :] * step_row), axis=0).T
    lower = jnp.arange(length)[:, None] >= jnp.arange(length)[None, :]
    allowed = lower & (seg_row[:, None] == seg_row[None, :])
    spread = log_decay[:, :, None] - log_decay[:, None, :]
    decays = jnp.where(allowed[None], jnp.exp(jnp.where(allowed[None], spread, 0.0)), 0.0)
    edge_weight = jnp.where(opening[None, :], jnp.exp(log_decay), 0.0)
    weighted = (decays * scores[None]).astype(jnp.bfloat16)
    grad_heads = grad_rows.reshape(length, head_count, head_dim)
    values_grad = jnp.einsum(
        "hts,thp->shp", weighted, grad_heads, preferred_element_type=jnp.float32
    )
    products = jnp.einsum("thp,shp->hts", grad_heads, values, preferred_element_type=jnp.float32)
    score_grad = jnp.sum(decays * products, axis=0)
    carried = jnp.einsum("thp,hpn->thn", grad_heads, state_zero, preferred_element_type=jnp.float32)
    read_grad = jnp.dot(
        score_grad, write_coeff.astype(jnp.float32), precision=lax.Precision.HIGHEST
    )
    read_grad = read_grad + jnp.sum(edge_weight.T[:, :, None] * carried, axis=1)
    write_grad = jnp.dot(
        score_grad.T, read_coeff.astype(jnp.float32), precision=lax.Precision.HIGHEST
    )
    scaled = edge_weight.T[:, :, None] * grad_heads.astype(jnp.float32)
    state_grad = jnp.einsum(
        "thp,tn->hpn", scaled, read_coeff.astype(jnp.float32), precision=lax.Precision.HIGHEST
    )
    mixed_grad = (values_grad * step_row[:, :, None]).reshape(length, channels)
    preact_grad = mixed_grad * silu_slope(preact)
    conv_rows = []
    for index_row in range(tap_count - 1):
        running = jnp.zeros((channels,), jnp.float32)
        for offset in range(tap_count - 1 - index_row, tap_count):
            position = index_row - (tap_count - 1) + offset
            running = running + jnp.where(
                opening[position], conv_weight[offset] * preact_grad[position], 0.0
            )
        conv_rows.append(running)
    conv_grad = jnp.stack(conv_rows)
    return (jnp.concatenate([write_grad, read_grad], axis=1), state_grad, conv_grad)


def shards(
    tokens_in,
    mix_in,
    step_size,
    doc_ids,
    out_grad,
    proj_weight,
    conv_weight,
    decay_rate,
    carried_state,
    carried_conv,
    carry_from,
):
    rows_dev, length, model_width = tokens_in.shape
    head_count = step_size.shape[2]
    slot_count = carried_state.shape[0]
    part_p = carried_state.shape[2]
    nstate = carried_state.shape[3]
    tap_count = conv_weight.shape[0]
    doc_count = lax.axis_size("doc")
    head_dim = part_p * doc_count
    channels = head_count * head_dim
    picker = (carry_from[:, None] == jnp.arange(slot_count, dtype=jnp.int32)[None, :]).astype(
        jnp.bfloat16
    )
    chosen_state = jnp.einsum(
        "rs,shpn->rhpn", picker, carried_state, preferred_element_type=jnp.float32
    ).astype(jnp.bfloat16)
    chosen_conv = jnp.einsum(
        "rs,skhp->rkhp", picker, carried_conv, preferred_element_type=jnp.float32
    ).astype(jnp.bfloat16)
    chosen_state = chosen_state.reshape(slot_count, head_count, part_p * nstate)
    chosen_conv = chosen_conv.reshape(slot_count, (tap_count - 1) * head_count, part_p)
    start_state, start_conv = (
        lax.all_to_all(chosen_state, "doc", split_axis=0, concat_axis=2, tiled=True),
        lax.all_to_all(chosen_conv, "doc", split_axis=0, concat_axis=2, tiled=True),
    )
    start_state = start_state.reshape(rows_dev, head_count, head_dim, nstate)
    start_conv = start_conv.reshape(rows_dev, tap_count - 1, channels)
    flattened = tokens_in.reshape(rows_dev * length, model_width)
    coeff_sum = jnp.dot(
        flattened,
        lax.all_gather(proj_weight, "fsdp", axis=0, tiled=True),
        preferred_element_type=jnp.float32,
    )
    coeff = coeff_sum.astype(jnp.bfloat16).reshape(rows_dev, length, proj_weight.shape[1])
    coeff_grad, state_grad, conv_grad = row_pass(
        coeff[0],
        mix_in[0],
        step_size[0],
        doc_ids[0],
        out_grad[0],
        start_state[0],
        start_conv[0],
        conv_weight,
        decay_rate,
    )
    coeff_grads = [coeff_grad]
    state_grads = [state_grad]
    conv_grads = [conv_grad]
    back_state = (
        jnp.stack(state_grads).astype(jnp.bfloat16).reshape(rows_dev, head_count, head_dim * nstate)
    )
    back_conv = (
        jnp.stack(conv_grads)
        .astype(jnp.bfloat16)
        .reshape(rows_dev, (tap_count - 1) * head_count, head_dim)
    )
    got_state, got_conv = (
        lax.all_to_all(back_state, "doc", split_axis=2, concat_axis=0, tiled=True),
        lax.all_to_all(back_conv, "doc", split_axis=2, concat_axis=0, tiled=True),
    )
    grad_state = jnp.einsum(
        "rs,rx->sx", picker, got_state.reshape(slot_count, -1), preferred_element_type=jnp.float32
    )
    grad_state = grad_state.astype(jnp.bfloat16).reshape(carried_state.shape)
    grad_conv = jnp.einsum(
        "rs,rx->sx", picker, got_conv.reshape(slot_count, -1), preferred_element_type=jnp.float32
    )
    grad_conv = grad_conv.astype(jnp.bfloat16).reshape(carried_conv.shape)
    coeff_flat = jnp.stack(coeff_grads).reshape(rows_dev * length, -1)
    share = lax.psum_scatter(coeff_flat, "fsdp", scatter_dimension=1, tiled=True)
    partial_cols = jnp.einsum(
        "tj,tn->jn", flattened.astype(jnp.float32), share, precision=lax.Precision.HIGHEST
    )
    summed_cols = lax.psum_scatter(partial_cols, "doc", scatter_dimension=0, tiled=True)
    grad_proj = lax.all_to_all(summed_cols, "fsdp", split_axis=0, concat_axis=1, tiled=True)
    return (grad_proj, grad_state, grad_conv)


F32 = jnp.float32
BF16 = jnp.bfloat16
MESH = pl.DeviceIdType.MESH


def dot_nn(a, b, precision=None):
    return lax.dot_general(
        a, b, (((1,), (0,)), ((), ())), precision=precision, preferred_element_type=F32
    )


def dot_nt(a, b):
    return lax.dot_general(a, b, (((1,), (1,)), ((), ())), preferred_element_type=F32)


def dot_tn(a, b):
    return lax.dot_general(a, b, (((0,), (0,)), ((), ())), preferred_element_type=F32)


def iota(shape, axis):
    return lax.broadcasted_iota(jnp.int32, shape, axis)


def layer_kernel(
    docs,
    parts,
    carry_hbm,
    tokens_hbm,
    mix_hbm,
    step_hbm,
    seg_hbm,
    grad_hbm,
    weight_hbm,
    taps_hbm,
    rate_hbm,
    state_hbm,
    conv_hbm,
    fin_own,
    fin_recv,
    sgrad_recv,
    cgrad_recv,
    carry_ref,
    mix_ref,
    step_ref,
    seg_ref,
    grad_ref,
    weight_ref,
    taps_ref,
    rate_ref,
    state_ref,
    conv_ref,
    tok_part,
    tok_cols,
    coeff_partial,
    coeff_recv,
    coeff,
    cg_partial,
    cg_send,
    cg_recv,
    cg,
    state_send,
    state_recv,
    conv_send,
    conv_recv,
    sgrad_send,
    cgrad_send,
    fin_part,
    fin_send,
    ext,
    seg_ext,
    og_scaled,
    val_scaled,
    first_scale,
    tap_mask,
    factors,
    load_sem,
    store_sem,
    part_send_sem,
    part_recv_sem,
    doc_send_sem,
    doc_recv_sem,
):
    d = lax.axis_index("doc")
    f = lax.axis_index("fsdp")
    length, channels = mix_ref.shape
    heads = step_ref.shape[0]
    head_dim = channels // heads
    part_p = head_dim // docs
    width = weight_ref.shape[1]
    nstate = width // 2
    slots = state_ref.shape[0]
    depth = weight_ref.shape[0]
    block = length // parts
    out_rows = fin_own.shape[0]
    taps = taps_ref.shape[0]

    own_columns = pl.ds(pl.multiple_of(f * depth, 128), depth)
    pairs = [
        (carry_hbm, carry_ref),
        (state_hbm, state_ref),
        (conv_hbm, conv_ref),
        (tokens_hbm.at[0, :, own_columns], tok_part),
        (weight_hbm, weight_ref),
        (step_hbm.at[0], step_ref),
        (rate_hbm, rate_ref),
        (seg_hbm, seg_ref),
        (taps_hbm, taps_ref),
        (mix_hbm.at[0], mix_ref),
        (grad_hbm.at[0], grad_ref),
    ]
    for q in range(docs):
        columns = pl.ds(pl.multiple_of((q * parts + f) * out_rows, 128), out_rows)
        pairs.append(
            (tokens_hbm.at[0, :, columns], tok_cols.at[:, pl.ds(q * out_rows, out_rows)])
        )
    loads = [
        pltpu.make_async_copy(src, dst, load_sem.at[i]) for i, (src, dst) in enumerate(pairs)
    ]
    for load in loads:
        load.start()

    barrier = pltpu.get_barrier_semaphore()
    for j in range(1, parts):
        pl.semaphore_signal(
            barrier, inc=1, device_id=(d, lax.rem(f + j, parts)), device_id_type=MESH
        )
    for j in range(1, docs):
        pl.semaphore_signal(
            barrier, inc=1, device_id=(lax.rem(d + j, docs), f), device_id_type=MESH
        )

    def part_copy(phase, j, src, dst):
        return pltpu.make_async_remote_copy(
            src_ref=src,
            dst_ref=dst,
            send_sem=part_send_sem.at[phase, j],
            recv_sem=part_recv_sem.at[phase, j],
            device_id=(d, lax.rem(f + j, parts)),
            device_id_type=MESH,
        )

    def doc_copy(phase, j, src, dst):
        return pltpu.make_async_remote_copy(
            src_ref=src,
            dst_ref=dst,
            send_sem=doc_send_sem.at[phase, j],
            recv_sem=doc_recv_sem.at[phase, j],
            device_id=(lax.rem(d + j, docs), f),
            device_id_type=MESH,
        )

    def rows_of(owner):
        return pl.ds(pl.multiple_of(owner * block, block), block)

    lane = iota((1, channels), 1)
    head_of_lane = lax.div(lane, head_dim)
    lane_in_head = lane - head_of_lane * head_dim
    place = jnp.where(
        jnp.broadcast_to(lane_in_head, (head_dim, channels)) == iota((head_dim, channels), 0),
        1.0,
        0.0,
    ).astype(BF16)
    head_rows = (taps - 1) * heads
    own_head = jnp.broadcast_to(head_of_lane, (heads, channels)) == iota((heads, channels), 0)

    for load in loads[:3]:
        load.wait()
    for r in range(slots):
        source = carry_ref[r]
        usable = jnp.where(source >= 0, 1.0, 0.0)
        index = jnp.maximum(source, 0)
        state_send[r] = (state_ref[index].astype(F32) * usable).astype(BF16)
        conv_send[r] = (conv_ref[index].astype(F32) * usable).astype(BF16)

    for load in loads[3:5]:
        load.wait()
    coeff_partial[...] = dot_nn(tok_part[...], weight_ref[...])

    pl.semaphore_wait(barrier, parts - 1 + docs - 1)

    conv_copies = [
        doc_copy(0, j, conv_send.at[lax.rem(d + j, docs)], conv_recv.at[d]) for j in range(1, docs)
    ]
    coeff_copies = [
        part_copy(0, j, coeff_partial.at[rows_of(lax.rem(f + j, parts))], coeff_recv.at[j])
        for j in range(1, parts)
    ]
    state_copies = [
        doc_copy(1, j, state_send.at[lax.rem(d + j, docs)], state_recv.at[:, d])
        for j in range(1, docs)
    ]
    for copy in conv_copies + coeff_copies + state_copies:
        copy.start()
    conv_recv[d] = conv_send[d]
    state_recv[:, d] = state_send[d]

    for load in loads[5:11]:
        load.wait()
    lower = iota((length, length), 0) >= iota((length, length), 1)
    rate = jnp.sum(
        jnp.where(iota((heads, heads), 0) == iota((heads, heads), 1), rate_ref[...], 0.0),
        axis=1,
        keepdims=True,
    )
    steps = step_ref[...]
    rest = -(rate * steps)
    pieces = []
    for _ in range(3):
        piece = rest.astype(BF16)
        pieces.append(piece)
        rest = rest - piece.astype(F32)
    sums = dot_nt(
        jnp.concatenate(pieces, axis=0), jnp.where(lower, 1.0, 0.0).astype(BF16)
    )
    log_decay = sums[:heads] + sums[heads : 2 * heads] + sums[2 * heads :]

    def halves(x):
        top = x.astype(BF16).astype(F32)
        both = jnp.concatenate([top, x - top, jnp.zeros((128 - 2 * heads, length), F32)], axis=0)
        return both.T.astype(BF16)

    grow = halves(jnp.exp(log_decay))
    shrink = halves(steps * jnp.exp(-log_decay))

    seg_row = seg_ref[...].astype(F32)
    seg_cols = jnp.broadcast_to(seg_row, (128, length)).T
    seg_ext[8:, :] = seg_cols
    seg_ext[:8, :] = jnp.broadcast_to(seg_cols[:1], (8, 128))
    opening = seg_cols == seg_cols[:1]

    for k in range(1, taps):
        tap_mask[k - 1] = jnp.where(seg_ext[8 - k : 8 - k + length, :] == seg_cols, 1.0, 0.0)

    def scaled_values(preact, factor):
        return (preact * (0.5 + 0.5 * jnp.tanh(0.5 * preact)) * factor).astype(BF16)

    ext[:8, :] = jnp.zeros((8, channels), F32)

    def chunk(c, carry):
        lanes = pl.ds(pl.multiple_of(c * 128, 128), 128)
        row = iota((128, 128), 0)
        head = jnp.broadcast_to(
            lax.div(iota((1, 128), 1) + c * 128, head_dim), (128, 128)
        )
        expand = jnp.where((row == head) | (row == head + heads), 1.0, 0.0).astype(BF16)

        def per_channel(both):
            return dot_nn(both, expand)

        ext[8:, lanes] = mix_ref[:, lanes].astype(F32)
        factors[0] = per_channel(grow)
        factors[1] = per_channel(shrink)
        first_scale[:, lanes] = factors[1, :16, :]
        for base in range(0, length, 64):
            rows = slice(base, base + 64)
            preact = taps_ref[0:1, lanes] * ext[8 + base : 72 + base, lanes]
            for k in range(1, taps):
                window = ext[8 - k + base : 72 - k + base, lanes]
                preact = preact + taps_ref[k : k + 1, lanes] * (tap_mask[k - 1, rows, :] * window)
            val_scaled[rows, lanes] = scaled_values(preact, factors[1, rows, :])
            og_scaled[rows, lanes] = (
                grad_ref[rows, lanes].astype(F32) * factors[0, rows, :]
            ).astype(BF16)
        return carry

    chunks = channels // 128
    lax.fori_loop(0, chunks // 2, chunk, 0)

    for copy in coeff_copies:
        copy.wait_recv()
    total = coeff_partial[rows_of(f)]
    for j in range(1, parts):
        total = total + coeff_recv[j]
    coeff[rows_of(f)] = total.astype(BF16)
    gather_copies = [
        part_copy(1, j, coeff.at[rows_of(f)], coeff.at[rows_of(f)]) for j in range(1, parts)
    ]
    for copy in gather_copies:
        copy.start()

    lax.fori_loop(chunks // 2, chunks, chunk, 0)

    for copy in conv_copies:
        copy.wait_recv()

    spread = dot_nn(
        jnp.concatenate(
            [conv_recv[q].reshape(head_rows, part_p) for q in range(docs)], axis=1
        ),
        place,
    )
    carried_rows = jnp.sum(
        jnp.where(own_head[None], spread.reshape(taps - 1, heads, channels), 0.0), axis=1
    )
    ext[8 - (taps - 1) : 8, :] = carried_rows
    pre = jnp.zeros((16, channels), F32)
    for k in range(taps):
        same = seg_ext[8 - k : 24 - k, :1] == seg_cols[:16, :1]
        window = ext[8 - k : 24 - k, :]
        pre = pre + jnp.where(same, taps_ref[k : k + 1, :] * window, 0.0)
    val_scaled[:16, :] = scaled_values(pre, first_scale[...])

    same_doc = seg_cols[:, :1] == seg_row
    score_grad = jnp.where(
        lower & same_doc, dot_nt(og_scaled[...], val_scaled[...]), 0.0
    ).astype(BF16)
    score_grad_t = score_grad.T

    for copy in state_copies:
        copy.wait_recv()
    from_state = jnp.where(
        opening, dot_nn(og_scaled[...], state_recv[...].reshape(channels, nstate)), 0.0
    )

    for copy in gather_copies:
        copy.wait_recv()
    write_coeff = coeff[:, :nstate]
    read_coeff = coeff[:, nstate:]
    cg_partial[:, :nstate] = dot_nn(score_grad_t, read_coeff)
    cg_partial[:, nstate:] = dot_nn(score_grad, write_coeff) + from_state
    cg_send[...] = cg_partial[...].astype(BF16)
    sum_copies = [
        part_copy(2, j, cg_send.at[rows_of(lax.rem(f + j, parts))], cg_recv.at[j])
        for j in range(1, parts)
    ]
    for copy in sum_copies:
        copy.start()

    open_read = jnp.where(opening, read_coeff.astype(F32), 0.0).astype(BF16)
    sgrad_send[...] = (
        dot_tn(og_scaled[...], open_read).astype(BF16).reshape(heads, docs, part_p, nstate)
    )
    sgrad_copies = [
        doc_copy(2, j, sgrad_send.at[:, lax.rem(d + j, docs)], sgrad_recv.at[d])
        for j in range(1, docs)
    ]
    for copy in sgrad_copies:
        copy.start()
    stores = [
        pltpu.make_async_copy(sgrad_send.at[:, d], sgrad_recv.at[d], store_sem.at[0]),
    ]
    stores[0].start()
    for load in loads[11:]:
        load.wait()
    tok_rows = tok_cols[...].T

    for copy in sum_copies:
        copy.wait_recv()
    total = cg_partial[rows_of(f)]
    for j in range(1, parts):
        total = total + cg_recv[j].astype(F32)
    cg[rows_of(f)] = total.astype(BF16)
    cg_copies = [part_copy(3, j, cg.at[rows_of(f)], cg.at[rows_of(f)]) for j in range(1, parts)]
    for copy in cg_copies:
        copy.start()

    first_scores = dot_nt(write_coeff[:16], read_coeff)
    first_seg = jnp.broadcast_to(seg_row, (16, length)) == seg_cols[:16, :1]
    first_allowed = first_seg & (iota((16, length), 1) >= iota((16, length), 0))
    first_scores = jnp.where(first_allowed, first_scores, 0.0).astype(BF16)
    first_grad = dot_nn(first_scores, og_scaled[...])[:8]
    pre = pre[:8]
    gate = 1.0 / (1.0 + jnp.exp(-pre))
    pre_grad = first_grad * first_scale[:8] * gate * (1.0 + pre * (1.0 - gate))
    pre_grad = jnp.where(seg_cols[:8, :1] == seg_cols[:1, :1], pre_grad, 0.0)
    conv_rows = []
    for row in range(taps - 1):
        running = jnp.zeros((1, channels), F32)
        for k in range(taps - 1 - row, taps):
            position = row - (taps - 1) + k
            running = running + taps_ref[k : k + 1, :] * pre_grad[position : position + 1]
        conv_rows.append(
            jnp.where(own_head, jnp.broadcast_to(running, (heads, channels)), 0.0).astype(BF16)
        )
    placed = dot_nt(jnp.concatenate(conv_rows, axis=0), place).astype(BF16)
    for q in range(docs):
        cgrad_send[q] = placed[:, q * part_p : (q + 1) * part_p].reshape(
            taps - 1, heads, part_p
        )
    cgrad_copies = [
        doc_copy(3, j, cgrad_send.at[lax.rem(d + j, docs)], cgrad_recv.at[d])
        for j in range(1, docs)
    ]
    for copy in cgrad_copies:
        copy.start()
    stores.append(pltpu.make_async_copy(cgrad_send.at[d], cgrad_recv.at[d], store_sem.at[1]))
    stores[1].start()

    for copy in cg_copies:
        copy.wait_recv()
    product = dot_nn(tok_rows, cg[...]).reshape(docs, out_rows, width)
    fin_send[...] = product.astype(BF16)
    fin_copies = [
        doc_copy(4, j, fin_send.at[lax.rem(d + j, docs)], fin_recv.at[j - 1])
        for j in range(1, docs)
    ]
    for copy in fin_copies:
        copy.start()
    fin_part[...] = product
    stores.append(pltpu.make_async_copy(fin_part.at[d], fin_own, store_sem.at[2]))
    stores[2].start()
    for copy in sgrad_copies + cgrad_copies + fin_copies:
        copy.wait_recv()
    for store in stores:
        store.wait()

    for copies in (
        conv_copies,
        coeff_copies,
        state_copies,
        gather_copies,
        sum_copies,
        sgrad_copies,
        cgrad_copies,
        cg_copies,
        fin_copies,
    ):
        for copy in copies:
            copy.wait_send()


def finish_kernel(
    carry_hbm,
    own_hbm,
    recv_hbm,
    sgrad_hbm,
    cgrad_hbm,
    proj_out,
    state_out,
    conv_out,
    carry_ref,
    own_ref,
    recv_ref,
    sgrad_ref,
    cgrad_ref,
    load_sem,
):
    pairs = (
        (carry_hbm, carry_ref),
        (sgrad_hbm, sgrad_ref),
        (cgrad_hbm, cgrad_ref),
        (own_hbm, own_ref),
        (recv_hbm, recv_ref),
    )
    loads = [
        pltpu.make_async_copy(src, dst, load_sem.at[i]) for i, (src, dst) in enumerate(pairs)
    ]
    for load in loads:
        load.start()
    for load in loads:
        load.wait()
    slots = state_out.shape[0]
    for s in range(slots):
        row_of = jnp.int32(0)
        found = jnp.float32(0.0)
        for r in range(slots):
            hit = carry_ref[r] == s
            row_of = jnp.where(hit, r, row_of)
            found = jnp.where(hit, 1.0, found)
        state_out[s] = (sgrad_ref[row_of].astype(F32) * found).astype(BF16)
        conv_out[s] = (cgrad_ref[row_of].astype(F32) * found).astype(BF16)
    result = own_ref[...]
    for j in range(recv_ref.shape[0]):
        result = result + recv_ref[j].astype(F32)
    proj_out[...] = result


def device_part(docs, parts, *args):
    (
        tokens_in,
        mix_in,
        step_size,
        doc_ids,
        out_grad,
        proj_weight,
        conv_weight,
        decay_rate,
        carried_state,
        carried_conv,
        carry_from,
    ) = args
    rows_dev, length, model_width = tokens_in.shape
    channels = mix_in.shape[2]
    heads = step_size.shape[2]
    depth, width = proj_weight.shape
    slots, _, part_p, nstate = carried_state.shape
    taps = conv_weight.shape[0]
    out_rows = model_width // (docs * parts)
    block = length // parts
    aligned = (
        rows_dev == 1
        and slots == docs
        and part_p % 16 == 0
        and heads % 16 == 0
        and 2 * heads <= 128
        and block % 16 == 0
        and length % 64 == 0
        and out_rows % 128 == 0
        and depth % 128 == 0
        and nstate == 128
        and channels % 128 == 0
        and taps <= 8
    )
    if not aligned:
        return shards(*args)
    vmem = pl.BlockSpec(memory_space=pltpu.VMEM)
    hbm = pl.BlockSpec(memory_space=pltpu.HBM)
    landed = (
        jax.ShapeDtypeStruct((out_rows, width), F32),
        jax.ShapeDtypeStruct((docs - 1, out_rows, width), BF16),
        jax.ShapeDtypeStruct(carried_state.shape, BF16),
        jax.ShapeDtypeStruct(carried_conv.shape, BF16),
    )
    buffers = pl.pallas_call(
        functools.partial(layer_kernel, docs, parts),
        out_shape=landed,
        in_specs=[hbm] * 11,
        out_specs=(hbm,) * 4,
        scratch_shapes=[
            pltpu.SMEM(carry_from.shape, jnp.int32),
            pltpu.VMEM((length, channels), BF16),
            pltpu.VMEM((heads, length), F32),
            pltpu.VMEM(doc_ids.shape, jnp.int32),
            pltpu.VMEM((length, channels), BF16),
            pltpu.VMEM(proj_weight.shape, BF16),
            pltpu.VMEM(conv_weight.shape, F32),
            pltpu.VMEM((1, heads), F32),
            pltpu.VMEM(carried_state.shape, BF16),
            pltpu.VMEM(carried_conv.shape, BF16),
            pltpu.VMEM((length, depth), BF16),
            pltpu.VMEM((length, docs * out_rows), BF16),
            pltpu.VMEM((length, width), F32),
            pltpu.VMEM((parts, block, width), F32),
            pltpu.VMEM((length, width), BF16),
            pltpu.VMEM((length, width), F32),
            pltpu.VMEM((length, width), BF16),
            pltpu.VMEM((parts, block, width), BF16),
            pltpu.VMEM((length, width), BF16),
            pltpu.VMEM((slots, heads, part_p, nstate), BF16),
            pltpu.VMEM((heads, docs, part_p, nstate), BF16),
            pltpu.VMEM((slots, taps - 1, heads, part_p), BF16),
            pltpu.VMEM((docs, taps - 1, heads, part_p), BF16),
            pltpu.VMEM((heads, docs, part_p, nstate), BF16),
            pltpu.VMEM((docs, taps - 1, heads, part_p), BF16),
            pltpu.VMEM((docs, out_rows, width), F32),
            pltpu.VMEM((docs, out_rows, width), BF16),
            pltpu.VMEM((length + 8, channels), F32),
            pltpu.VMEM((length + 8, 128), F32),
            pltpu.VMEM((length, channels), BF16),
            pltpu.VMEM((length, channels), BF16),
            pltpu.VMEM((16, channels), F32),
            pltpu.VMEM((taps - 1, length, 128), F32),
            pltpu.VMEM((2, length, 128), F32),
            pltpu.SemaphoreType.DMA((11 + docs,)),
            pltpu.SemaphoreType.DMA((3,)),
            pltpu.SemaphoreType.DMA((4, parts)),
            pltpu.SemaphoreType.DMA((4, parts)),
            pltpu.SemaphoreType.DMA((5, docs)),
            pltpu.SemaphoreType.DMA((5, docs)),
        ],
        compiler_params=pltpu.CompilerParams(
            collective_id=0, has_side_effects=True, vmem_limit_bytes=60 * 1024 * 1024
        ),
        cost_estimate=pl.CostEstimate(
            flops=2 * length * channels * length * 4, bytes_accessed=4 << 20, transcendentals=0
        ),
    )(
        carry_from,
        tokens_in,
        mix_in,
        jnp.swapaxes(step_size, 1, 2),
        doc_ids,
        out_grad,
        proj_weight,
        conv_weight,
        decay_rate.reshape(1, heads),
        carried_state,
        carried_conv,
    )
    return pl.pallas_call(
        finish_kernel,
        out_shape=(
            jax.ShapeDtypeStruct((out_rows, width), F32),
            jax.ShapeDtypeStruct(carried_state.shape, BF16),
            jax.ShapeDtypeStruct(carried_conv.shape, BF16),
        ),
        in_specs=[hbm] * 5,
        out_specs=(vmem,) * 3,
        scratch_shapes=[pltpu.SMEM(carry_from.shape, jnp.int32)]
        + [pltpu.VMEM(leaf.shape, leaf.dtype) for leaf in landed]
        + [pltpu.SemaphoreType.DMA((5,))],
        compiler_params=pltpu.CompilerParams(vmem_limit_bytes=60 * 1024 * 1024),
    )(carry_from, *buffers)


def solution(mesh):
    return jax.shard_map(
        functools.partial(device_part, mesh.shape["doc"], mesh.shape["fsdp"]),
        mesh=mesh,
        in_specs=(
            P("doc", None, None),
            P("doc", None, "fsdp"),
            P("doc", None, "fsdp"),
            P("doc", None),
            P("doc", None, "fsdp"),
            P("fsdp", None),
            P(None, "fsdp"),
            P("fsdp"),
            P(None, "fsdp", "doc", None),
            P(None, None, "fsdp", "doc"),
            P(),
        ),
        out_specs=(
            P(("doc", "fsdp"), None),
            P(None, "fsdp", "doc", None),
            P(None, None, "fsdp", "doc"),
        ),
        check_vma=False,
    )
```

```python
import functools

import jax
import jax.numpy as jnp
from jax import lax
from jax.experimental import pallas as pl
from jax.experimental.pallas import tpu as pltpu
from jax.sharding import PartitionSpec as P


def silu_slope(value):
    sigmoid_value = jax.nn.sigmoid(value)
    return sigmoid_value * (1.0 + value * (1.0 - sigmoid_value))


def conv_masks(seg_row, tap_count):
    length = seg_row.shape[0]
    opening = seg_row == seg_row[0]
    tap_masks = []
    for offset in range(tap_count):
        earlier = jnp.concatenate([jnp.full((offset,), -1, jnp.int32), seg_row[: length - offset]])
        inside = jnp.arange(length) >= offset
        tap_masks.append(jnp.where(inside, earlier == seg_row, opening))
    return (opening, tap_masks)


def row_pass(
    coeff, mix_row, step_row, seg_row, grad_rows, state_zero, conv_zero, conv_weight, decay_rate
):
    length, channels = mix_row.shape
    head_count = step_row.shape[1]
    head_dim = channels // head_count
    tap_count = conv_weight.shape[0]
    nstate = coeff.shape[1] // 2
    opening, tap_masks = conv_masks(seg_row, tap_count)
    extended = jnp.concatenate([conv_zero, mix_row], axis=0).astype(jnp.float32)
    preact = jnp.zeros((length, channels), jnp.float32)
    for offset in range(tap_count):
        window = extended[tap_count - 1 - offset : tap_count - 1 - offset + length]
        preact = preact + jnp.where(
            tap_masks[offset][:, None], conv_weight[offset][None, :] * window, 0.0
        )
    mixed_rows = jax.nn.silu(preact).astype(jnp.bfloat16)
    values = (
        step_row[:, :, None] * mixed_rows.reshape(length, head_count, head_dim).astype(jnp.float32)
    ).astype(jnp.bfloat16)
    write_coeff = coeff[:, :nstate]
    read_coeff = coeff[:, nstate:]
    scores = jnp.dot(read_coeff, write_coeff.T, preferred_element_type=jnp.float32)
    log_decay = jnp.cumsum(-(decay_rate[None, :] * step_row), axis=0).T
    lower = jnp.arange(length)[:, None] >= jnp.arange(length)[None, :]
    allowed = lower & (seg_row[:, None] == seg_row[None, :])
    spread = log_decay[:, :, None] - log_decay[:, None, :]
    decays = jnp.where(allowed[None], jnp.exp(jnp.where(allowed[None], spread, 0.0)), 0.0)
    edge_weight = jnp.where(opening[None, :], jnp.exp(log_decay), 0.0)
    weighted = (decays * scores[None]).astype(jnp.bfloat16)
    grad_heads = grad_rows.reshape(length, head_count, head_dim)
    values_grad = jnp.einsum(
        "hts,thp->shp", weighted, grad_heads, preferred_element_type=jnp.float32
    )
    products = jnp.einsum("thp,shp->hts", grad_heads, values, preferred_element_type=jnp.float32)
    score_grad = jnp.sum(decays * products, axis=0)
    carried = jnp.einsum("thp,hpn->thn", grad_heads, state_zero, preferred_element_type=jnp.float32)
    read_grad = jnp.dot(
        score_grad, write_coeff.astype(jnp.float32), precision=lax.Precision.HIGHEST
    )
    read_grad = read_grad + jnp.sum(edge_weight.T[:, :, None] * carried, axis=1)
    write_grad = jnp.dot(
        score_grad.T, read_coeff.astype(jnp.float32), precision=lax.Precision.HIGHEST
    )
    scaled = edge_weight.T[:, :, None] * grad_heads.astype(jnp.float32)
    state_grad = jnp.einsum(
        "thp,tn->hpn", scaled, read_coeff.astype(jnp.float32), precision=lax.Precision.HIGHEST
    )
    mixed_grad = (values_grad * step_row[:, :, None]).reshape(length, channels)
    preact_grad = mixed_grad * silu_slope(preact)
    conv_rows = []
    for index_row in range(tap_count - 1):
        running = jnp.zeros((channels,), jnp.float32)
        for offset in range(tap_count - 1 - index_row, tap_count):
            position = index_row - (tap_count - 1) + offset
            running = running + jnp.where(
                opening[position], conv_weight[offset] * preact_grad[position], 0.0
            )
        conv_rows.append(running)
    conv_grad = jnp.stack(conv_rows)
    return (jnp.concatenate([write_grad, read_grad], axis=1), state_grad, conv_grad)


def shards(
    tokens_in,
    mix_in,
    step_size,
    doc_ids,
    out_grad,
    proj_weight,
    conv_weight,
    decay_rate,
    carried_state,
    carried_conv,
    carry_from,
):
    rows_dev, length, model_width = tokens_in.shape
    head_count = step_size.shape[2]
    slot_count = carried_state.shape[0]
    part_p = carried_state.shape[2]
    nstate = carried_state.shape[3]
    tap_count = conv_weight.shape[0]
    doc_count = lax.axis_size("doc")
    head_dim = part_p * doc_count
    channels = head_count * head_dim
    picker = (carry_from[:, None] == jnp.arange(slot_count, dtype=jnp.int32)[None, :]).astype(
        jnp.bfloat16
    )
    chosen_state = jnp.einsum(
        "rs,shpn->rhpn", picker, carried_state, preferred_element_type=jnp.float32
    ).astype(jnp.bfloat16)
    chosen_conv = jnp.einsum(
        "rs,skhp->rkhp", picker, carried_conv, preferred_element_type=jnp.float32
    ).astype(jnp.bfloat16)
    chosen_state = chosen_state.reshape(slot_count, head_count, part_p * nstate)
    chosen_conv = chosen_conv.reshape(slot_count, (tap_count - 1) * head_count, part_p)
    start_state, start_conv = (
        lax.all_to_all(chosen_state, "doc", split_axis=0, concat_axis=2, tiled=True),
        lax.all_to_all(chosen_conv, "doc", split_axis=0, concat_axis=2, tiled=True),
    )
    start_state = start_state.reshape(rows_dev, head_count, head_dim, nstate)
    start_conv = start_conv.reshape(rows_dev, tap_count - 1, channels)
    flattened = tokens_in.reshape(rows_dev * length, model_width)
    coeff_sum = jnp.dot(
        flattened,
        lax.all_gather(proj_weight, "fsdp", axis=0, tiled=True),
        preferred_element_type=jnp.float32,
    )
    coeff = coeff_sum.astype(jnp.bfloat16).reshape(rows_dev, length, proj_weight.shape[1])
    coeff_grad, state_grad, conv_grad = row_pass(
        coeff[0],
        mix_in[0],
        step_size[0],
        doc_ids[0],
        out_grad[0],
        start_state[0],
        start_conv[0],
        conv_weight,
        decay_rate,
    )
    coeff_grads = [coeff_grad]
    state_grads = [state_grad]
    conv_grads = [conv_grad]
    back_state = (
        jnp.stack(state_grads).astype(jnp.bfloat16).reshape(rows_dev, head_count, head_dim * nstate)
    )
    back_conv = (
        jnp.stack(conv_grads)
        .astype(jnp.bfloat16)
        .reshape(rows_dev, (tap_count - 1) * head_count, head_dim)
    )
    got_state, got_conv = (
        lax.all_to_all(back_state, "doc", split_axis=2, concat_axis=0, tiled=True),
        lax.all_to_all(back_conv, "doc", split_axis=2, concat_axis=0, tiled=True),
    )
    grad_state = jnp.einsum(
        "rs,rx->sx", picker, got_state.reshape(slot_count, -1), preferred_element_type=jnp.float32
    )
    grad_state = grad_state.astype(jnp.bfloat16).reshape(carried_state.shape)
    grad_conv = jnp.einsum(
        "rs,rx->sx", picker, got_conv.reshape(slot_count, -1), preferred_element_type=jnp.float32
    )
    grad_conv = grad_conv.astype(jnp.bfloat16).reshape(carried_conv.shape)
    coeff_flat = jnp.stack(coeff_grads).reshape(rows_dev * length, -1)
    share = lax.psum_scatter(coeff_flat, "fsdp", scatter_dimension=1, tiled=True)
    partial_cols = jnp.einsum(
        "tj,tn->jn", flattened.astype(jnp.float32), share, precision=lax.Precision.HIGHEST
    )
    summed_cols = lax.psum_scatter(partial_cols, "doc", scatter_dimension=0, tiled=True)
    grad_proj = lax.all_to_all(summed_cols, "fsdp", split_axis=0, concat_axis=1, tiled=True)
    return (grad_proj, grad_state, grad_conv)


F32 = jnp.float32
BF16 = jnp.bfloat16
MESH = pl.DeviceIdType.MESH


def dot_nn(a, b, precision=None):
    return lax.dot_general(
        a, b, (((1,), (0,)), ((), ())), precision=precision, preferred_element_type=F32
    )


def dot_nt(a, b):
    return lax.dot_general(a, b, (((1,), (1,)), ((), ())), preferred_element_type=F32)


def dot_tn(a, b):
    return lax.dot_general(a, b, (((0,), (0,)), ((), ())), preferred_element_type=F32)


def iota(shape, axis):
    return lax.broadcasted_iota(jnp.int32, shape, axis)


def layer_kernel(
    docs,
    parts,
    carry_hbm,
    tokens_hbm,
    mix_hbm,
    step_hbm,
    seg_hbm,
    grad_hbm,
    weight_hbm,
    taps_hbm,
    rate_hbm,
    state_hbm,
    conv_hbm,
    fin_own,
    fin_recv,
    sgrad_recv,
    cgrad_recv,
    carry_ref,
    mix_ref,
    step_ref,
    seg_ref,
    grad_ref,
    weight_ref,
    taps_ref,
    rate_ref,
    state_ref,
    conv_ref,
    tok_part,
    tok_cols,
    coeff_partial,
    coeff_recv,
    coeff,
    cg_partial,
    cg_send,
    cg_recv,
    cg,
    state_send,
    state_recv,
    conv_send,
    conv_recv,
    sgrad_send,
    cgrad_send,
    fin_part,
    fin_send,
    fin_pair,
    fin_cross,
    ext,
    seg_ext,
    og_scaled,
    val_scaled,
    first_scale,
    tap_mask,
    factors,
    load_sem,
    store_sem,
    part_send_sem,
    part_recv_sem,
    doc_send_sem,
    doc_recv_sem,
):
    d = lax.axis_index("doc")
    f = lax.axis_index("fsdp")
    length, channels = mix_ref.shape
    heads = step_ref.shape[0]
    head_dim = channels // heads
    part_p = head_dim // docs
    width = weight_ref.shape[1]
    nstate = width // 2
    slots = state_ref.shape[0]
    depth = weight_ref.shape[0]
    block = length // parts
    out_rows = fin_own.shape[0]
    taps = taps_ref.shape[0]

    own_columns = pl.ds(pl.multiple_of(f * depth, 128), depth)
    pairs = [
        (carry_hbm, carry_ref),
        (state_hbm, state_ref),
        (conv_hbm, conv_ref),
        (tokens_hbm.at[0, :, own_columns], tok_part),
        (weight_hbm, weight_ref),
        (step_hbm.at[0], step_ref),
        (rate_hbm, rate_ref),
        (seg_hbm, seg_ref),
        (taps_hbm, taps_ref),
        (mix_hbm.at[0], mix_ref),
        (grad_hbm.at[0], grad_ref),
    ]
    for q in range(docs):
        columns = pl.ds(pl.multiple_of((q * parts + f) * out_rows, 128), out_rows)
        pairs.append(
            (tokens_hbm.at[0, :, columns], tok_cols.at[:, pl.ds(q * out_rows, out_rows)])
        )
    loads = [
        pltpu.make_async_copy(src, dst, load_sem.at[i]) for i, (src, dst) in enumerate(pairs)
    ]
    for load in loads:
        load.start()

    barrier = pltpu.get_barrier_semaphore()
    for j in range(1, parts):
        pl.semaphore_signal(
            barrier, inc=1, device_id=(d, lax.rem(f + j, parts)), device_id_type=MESH
        )
    for j in range(1, docs):
        pl.semaphore_signal(
            barrier, inc=1, device_id=(lax.rem(d + j, docs), f), device_id_type=MESH
        )

    def part_copy(phase, j, src, dst):
        return pltpu.make_async_remote_copy(
            src_ref=src,
            dst_ref=dst,
            send_sem=part_send_sem.at[phase, j],
            recv_sem=part_recv_sem.at[phase, j],
            device_id=(d, lax.rem(f + j, parts)),
            device_id_type=MESH,
        )

    def doc_copy(phase, j, src, dst):
        return pltpu.make_async_remote_copy(
            src_ref=src,
            dst_ref=dst,
            send_sem=doc_send_sem.at[phase, j],
            recv_sem=doc_recv_sem.at[phase, j],
            device_id=(lax.rem(d + j, docs), f),
            device_id_type=MESH,
        )

    def rows_of(owner):
        return pl.ds(pl.multiple_of(owner * block, block), block)

    lane = iota((1, channels), 1)
    head_of_lane = lax.div(lane, head_dim)
    lane_in_head = lane - head_of_lane * head_dim
    place = jnp.where(
        jnp.broadcast_to(lane_in_head, (head_dim, channels)) == iota((head_dim, channels), 0),
        1.0,
        0.0,
    ).astype(BF16)
    head_rows = (taps - 1) * heads
    own_head = jnp.broadcast_to(head_of_lane, (heads, channels)) == iota((heads, channels), 0)

    for load in loads[:3]:
        load.wait()
    for r in range(slots):
        source = carry_ref[r]
        usable = jnp.where(source >= 0, 1.0, 0.0)
        index = jnp.maximum(source, 0)
        state_send[r] = (state_ref[index].astype(F32) * usable).astype(BF16)
        conv_send[r] = (conv_ref[index].astype(F32) * usable).astype(BF16)

    for load in loads[3:5]:
        load.wait()
    coeff_partial[...] = dot_nn(tok_part[...], weight_ref[...])

    pl.semaphore_wait(barrier, parts - 1 + docs - 1)

    conv_copies = [
        doc_copy(0, j, conv_send.at[lax.rem(d + j, docs)], conv_recv.at[d]) for j in range(1, docs)
    ]
    coeff_copies = [
        part_copy(0, j, coeff_partial.at[rows_of(lax.rem(f + j, parts))], coeff_recv.at[j])
        for j in range(1, parts)
    ]
    state_copies = [
        doc_copy(1, j, state_send.at[lax.rem(d + j, docs)], state_recv.at[:, d])
        for j in range(1, docs)
    ]
    for copy in conv_copies + coeff_copies + state_copies:
        copy.start()
    conv_recv[d] = conv_send[d]
    state_recv[:, d] = state_send[d]

    for load in loads[5:11]:
        load.wait()
    lower = iota((length, length), 0) >= iota((length, length), 1)
    rate = jnp.sum(
        jnp.where(iota((heads, heads), 0) == iota((heads, heads), 1), rate_ref[...], 0.0),
        axis=1,
        keepdims=True,
    )
    steps = step_ref[...]
    rest = -(rate * steps)
    pieces = []
    for _ in range(3):
        piece = rest.astype(BF16)
        pieces.append(piece)
        rest = rest - piece.astype(F32)
    sums = dot_nt(
        jnp.concatenate(pieces, axis=0), jnp.where(lower, 1.0, 0.0).astype(BF16)
    )
    log_decay = sums[:heads] + sums[heads : 2 * heads] + sums[2 * heads :]

    def halves(x):
        top = x.astype(BF16).astype(F32)
        both = jnp.concatenate([top, x - top, jnp.zeros((128 - 2 * heads, length), F32)], axis=0)
        return both.T.astype(BF16)

    grow = halves(jnp.exp(log_decay))
    shrink = halves(steps * jnp.exp(-log_decay))

    seg_row = seg_ref[...].astype(F32)
    seg_cols = jnp.broadcast_to(seg_row, (128, length)).T
    seg_ext[8:, :] = seg_cols
    seg_ext[:8, :] = jnp.broadcast_to(seg_cols[:1], (8, 128))
    opening = seg_cols == seg_cols[:1]

    for k in range(1, taps):
        tap_mask[k - 1] = jnp.where(seg_ext[8 - k : 8 - k + length, :] == seg_cols, 1.0, 0.0)

    def scaled_values(preact, factor):
        return (preact * (0.5 + 0.5 * jnp.tanh(0.5 * preact)) * factor).astype(BF16)

    ext[:8, :] = jnp.zeros((8, channels), F32)

    def chunk(c, carry):
        lanes = pl.ds(pl.multiple_of(c * 128, 128), 128)
        row = iota((128, 128), 0)
        head = jnp.broadcast_to(
            lax.div(iota((1, 128), 1) + c * 128, head_dim), (128, 128)
        )
        expand = jnp.where((row == head) | (row == head + heads), 1.0, 0.0).astype(BF16)

        def per_channel(both):
            return dot_nn(both, expand)

        ext[8:, lanes] = mix_ref[:, lanes].astype(F32)
        factors[0] = per_channel(grow)
        factors[1] = per_channel(shrink)
        first_scale[:, lanes] = factors[1, :16, :]
        for base in range(0, length, 64):
            rows = slice(base, base + 64)
            preact = taps_ref[0:1, lanes] * ext[8 + base : 72 + base, lanes]
            for k in range(1, taps):
                window = ext[8 - k + base : 72 - k + base, lanes]
                preact = preact + taps_ref[k : k + 1, lanes] * (tap_mask[k - 1, rows, :] * window)
            val_scaled[rows, lanes] = scaled_values(preact, factors[1, rows, :])
            og_scaled[rows, lanes] = (
                grad_ref[rows, lanes].astype(F32) * factors[0, rows, :]
            ).astype(BF16)
        return carry

    chunks = channels // 128
    lax.fori_loop(0, chunks // 2, chunk, 0)

    for copy in coeff_copies:
        copy.wait_recv()
    total = coeff_partial[rows_of(f)]
    for j in range(1, parts):
        total = total + coeff_recv[j]
    coeff[rows_of(f)] = total.astype(BF16)
    gather_copies = [
        part_copy(1, j, coeff.at[rows_of(f)], coeff.at[rows_of(f)]) for j in range(1, parts)
    ]
    for copy in gather_copies:
        copy.start()

    lax.fori_loop(chunks // 2, chunks, chunk, 0)

    for copy in conv_copies:
        copy.wait_recv()

    spread = dot_nn(
        jnp.concatenate(
            [conv_recv[q].reshape(head_rows, part_p) for q in range(docs)], axis=1
        ),
        place,
    )
    carried_rows = jnp.sum(
        jnp.where(own_head[None], spread.reshape(taps - 1, heads, channels), 0.0), axis=1
    )
    ext[8 - (taps - 1) : 8, :] = carried_rows
    pre = jnp.zeros((16, channels), F32)
    for k in range(taps):
        same = seg_ext[8 - k : 24 - k, :1] == seg_cols[:16, :1]
        window = ext[8 - k : 24 - k, :]
        pre = pre + jnp.where(same, taps_ref[k : k + 1, :] * window, 0.0)
    val_scaled[:16, :] = scaled_values(pre, first_scale[...])

    same_doc = seg_cols[:, :1] == seg_row
    score_grad = jnp.where(
        lower & same_doc, dot_nt(og_scaled[...], val_scaled[...]), 0.0
    ).astype(BF16)
    score_grad_t = score_grad.T

    for copy in state_copies:
        copy.wait_recv()
    from_state = jnp.where(
        opening, dot_nn(og_scaled[...], state_recv[...].reshape(channels, nstate)), 0.0
    )

    for copy in gather_copies:
        copy.wait_recv()
    write_coeff = coeff[:, :nstate]
    read_coeff = coeff[:, nstate:]
    cg_partial[:, :nstate] = dot_nn(score_grad_t, read_coeff)
    cg_partial[:, nstate:] = dot_nn(score_grad, write_coeff) + from_state
    cg_send[...] = cg_partial[...].astype(BF16)
    sum_copies = [
        part_copy(2, j, cg_send.at[rows_of(lax.rem(f + j, parts))], cg_recv.at[j])
        for j in range(1, parts)
    ]
    for copy in sum_copies:
        copy.start()

    open_read = jnp.where(opening, read_coeff.astype(F32), 0.0).astype(BF16)
    sgrad_send[...] = (
        dot_tn(og_scaled[...], open_read).astype(BF16).reshape(heads, docs, part_p, nstate)
    )
    sgrad_copies = [
        doc_copy(2, j, sgrad_send.at[:, lax.rem(d + j, docs)], sgrad_recv.at[d])
        for j in range(1, docs)
    ]
    for copy in sgrad_copies:
        copy.start()
    stores = [
        pltpu.make_async_copy(sgrad_send.at[:, d], sgrad_recv.at[d], store_sem.at[0]),
    ]
    stores[0].start()
    for load in loads[11:]:
        load.wait()
    tok_rows = tok_cols[...].T

    for copy in sum_copies:
        copy.wait_recv()
    total = cg_partial[rows_of(f)]
    for j in range(1, parts):
        total = total + cg_recv[j].astype(F32)
    cg[rows_of(f)] = total.astype(BF16)
    cg_copies = [part_copy(3, j, cg.at[rows_of(f)], cg.at[rows_of(f)]) for j in range(1, parts)]
    for copy in cg_copies:
        copy.start()

    first_scores = dot_nt(write_coeff[:16], read_coeff)
    first_seg = jnp.broadcast_to(seg_row, (16, length)) == seg_cols[:16, :1]
    first_allowed = first_seg & (iota((16, length), 1) >= iota((16, length), 0))
    first_scores = jnp.where(first_allowed, first_scores, 0.0).astype(BF16)
    first_grad = dot_nn(first_scores, og_scaled[...])[:8]
    pre = pre[:8]
    gate = 1.0 / (1.0 + jnp.exp(-pre))
    pre_grad = first_grad * first_scale[:8] * gate * (1.0 + pre * (1.0 - gate))
    pre_grad = jnp.where(seg_cols[:8, :1] == seg_cols[:1, :1], pre_grad, 0.0)
    conv_rows = []
    for row in range(taps - 1):
        running = jnp.zeros((1, channels), F32)
        for k in range(taps - 1 - row, taps):
            position = row - (taps - 1) + k
            running = running + taps_ref[k : k + 1, :] * pre_grad[position : position + 1]
        conv_rows.append(
            jnp.where(own_head, jnp.broadcast_to(running, (heads, channels)), 0.0).astype(BF16)
        )
    placed = dot_nt(jnp.concatenate(conv_rows, axis=0), place).astype(BF16)
    for q in range(docs):
        cgrad_send[q] = placed[:, q * part_p : (q + 1) * part_p].reshape(
            taps - 1, heads, part_p
        )
    cgrad_copies = [
        doc_copy(3, j, cgrad_send.at[lax.rem(d + j, docs)], cgrad_recv.at[d])
        for j in range(1, docs)
    ]
    for copy in cgrad_copies:
        copy.start()
    stores.append(pltpu.make_async_copy(cgrad_send.at[d], cgrad_recv.at[d], store_sem.at[1]))
    stores[1].start()

    for copy in cg_copies:
        copy.wait_recv()
    product = dot_nn(tok_rows, cg[...]).reshape(docs, out_rows, width)
    fin_send[...] = product.astype(BF16)
    fin_part[...] = product
    near = d + 1 - 2 * lax.rem(d, 2)
    far = lax.rem(d + docs // 2, docs)
    near_far = lax.rem(near + docs // 2, docs)

    def fin_copy(k, src, dst, target):
        return pltpu.make_async_remote_copy(
            src_ref=src,
            dst_ref=dst,
            send_sem=doc_send_sem.at[4, k],
            recv_sem=doc_recv_sem.at[4, k],
            device_id=(target, f),
            device_id_type=MESH,
        )

    fin_copies = [
        fin_copy(0, fin_send.at[near_far], fin_pair, near),
        fin_copy(1, fin_send.at[near], fin_recv.at[0], near),
    ]
    for copy in fin_copies:
        copy.start()
    fin_copies[0].wait_recv()
    fin_cross[...] = (fin_part[far] + fin_pair[...].astype(F32)).astype(BF16)
    fin_copies.append(fin_copy(2, fin_cross, fin_recv.at[1], far))
    fin_copies[2].start()
    stores.append(pltpu.make_async_copy(fin_part.at[d], fin_own, store_sem.at[2]))
    stores[2].start()
    for copy in sgrad_copies + cgrad_copies + fin_copies[1:]:
        copy.wait_recv()
    for store in stores:
        store.wait()

    for copies in (
        conv_copies,
        coeff_copies,
        state_copies,
        gather_copies,
        sum_copies,
        sgrad_copies,
        cgrad_copies,
        cg_copies,
        fin_copies,
    ):
        for copy in copies:
            copy.wait_send()


def finish_kernel(
    carry_hbm,
    own_hbm,
    recv_hbm,
    sgrad_hbm,
    cgrad_hbm,
    proj_out,
    state_out,
    conv_out,
    carry_ref,
    own_ref,
    recv_ref,
    sgrad_ref,
    cgrad_ref,
    load_sem,
):
    pairs = (
        (carry_hbm, carry_ref),
        (sgrad_hbm, sgrad_ref),
        (cgrad_hbm, cgrad_ref),
        (own_hbm, own_ref),
        (recv_hbm, recv_ref),
    )
    loads = [
        pltpu.make_async_copy(src, dst, load_sem.at[i]) for i, (src, dst) in enumerate(pairs)
    ]
    for load in loads:
        load.start()
    for load in loads:
        load.wait()
    slots = state_out.shape[0]
    for s in range(slots):
        row_of = jnp.int32(0)
        found = jnp.float32(0.0)
        for r in range(slots):
            hit = carry_ref[r] == s
            row_of = jnp.where(hit, r, row_of)
            found = jnp.where(hit, 1.0, found)
        state_out[s] = (sgrad_ref[row_of].astype(F32) * found).astype(BF16)
        conv_out[s] = (cgrad_ref[row_of].astype(F32) * found).astype(BF16)
    result = own_ref[...]
    for j in range(recv_ref.shape[0]):
        result = result + recv_ref[j].astype(F32)
    proj_out[...] = result


def device_part(docs, parts, *args):
    (
        tokens_in,
        mix_in,
        step_size,
        doc_ids,
        out_grad,
        proj_weight,
        conv_weight,
        decay_rate,
        carried_state,
        carried_conv,
        carry_from,
    ) = args
    rows_dev, length, model_width = tokens_in.shape
    channels = mix_in.shape[2]
    heads = step_size.shape[2]
    depth, width = proj_weight.shape
    slots, _, part_p, nstate = carried_state.shape
    taps = conv_weight.shape[0]
    out_rows = model_width // (docs * parts)
    block = length // parts
    aligned = (
        rows_dev == 1
        and slots == docs
        and docs == 4
        and part_p % 16 == 0
        and heads % 16 == 0
        and 2 * heads <= 128
        and block % 16 == 0
        and length % 64 == 0
        and out_rows % 128 == 0
        and depth % 128 == 0
        and nstate == 128
        and channels % 128 == 0
        and taps <= 8
    )
    if not aligned:
        return shards(*args)
    vmem = pl.BlockSpec(memory_space=pltpu.VMEM)
    hbm = pl.BlockSpec(memory_space=pltpu.HBM)
    landed = (
        jax.ShapeDtypeStruct((out_rows, width), F32),
        jax.ShapeDtypeStruct((2, out_rows, width), BF16),
        jax.ShapeDtypeStruct(carried_state.shape, BF16),
        jax.ShapeDtypeStruct(carried_conv.shape, BF16),
    )
    buffers = pl.pallas_call(
        functools.partial(layer_kernel, docs, parts),
        out_shape=landed,
        in_specs=[hbm] * 11,
        out_specs=(hbm,) * 4,
        scratch_shapes=[
            pltpu.SMEM(carry_from.shape, jnp.int32),
            pltpu.VMEM((length, channels), BF16),
            pltpu.VMEM((heads, length), F32),
            pltpu.VMEM(doc_ids.shape, jnp.int32),
            pltpu.VMEM((length, channels), BF16),
            pltpu.VMEM(proj_weight.shape, BF16),
            pltpu.VMEM(conv_weight.shape, F32),
            pltpu.VMEM((1, heads), F32),
            pltpu.VMEM(carried_state.shape, BF16),
            pltpu.VMEM(carried_conv.shape, BF16),
            pltpu.VMEM((length, depth), BF16),
            pltpu.VMEM((length, docs * out_rows), BF16),
            pltpu.VMEM((length, width), F32),
            pltpu.VMEM((parts, block, width), F32),
            pltpu.VMEM((length, width), BF16),
            pltpu.VMEM((length, width), F32),
            pltpu.VMEM((length, width), BF16),
            pltpu.VMEM((parts, block, width), BF16),
            pltpu.VMEM((length, width), BF16),
            pltpu.VMEM((slots, heads, part_p, nstate), BF16),
            pltpu.VMEM((heads, docs, part_p, nstate), BF16),
            pltpu.VMEM((slots, taps - 1, heads, part_p), BF16),
            pltpu.VMEM((docs, taps - 1, heads, part_p), BF16),
            pltpu.VMEM((heads, docs, part_p, nstate), BF16),
            pltpu.VMEM((docs, taps - 1, heads, part_p), BF16),
            pltpu.VMEM((docs, out_rows, width), F32),
            pltpu.VMEM((docs, out_rows, width), BF16),
            pltpu.VMEM((out_rows, width), BF16),
            pltpu.VMEM((out_rows, width), BF16),
            pltpu.VMEM((length + 8, channels), F32),
            pltpu.VMEM((length + 8, 128), F32),
            pltpu.VMEM((length, channels), BF16),
            pltpu.VMEM((length, channels), BF16),
            pltpu.VMEM((16, channels), F32),
            pltpu.VMEM((taps - 1, length, 128), F32),
            pltpu.VMEM((2, length, 128), F32),
            pltpu.SemaphoreType.DMA((11 + docs,)),
            pltpu.SemaphoreType.DMA((3,)),
            pltpu.SemaphoreType.DMA((4, parts)),
            pltpu.SemaphoreType.DMA((4, parts)),
            pltpu.SemaphoreType.DMA((5, docs)),
            pltpu.SemaphoreType.DMA((5, docs)),
        ],
        compiler_params=pltpu.CompilerParams(
            collective_id=0, has_side_effects=True, vmem_limit_bytes=60 * 1024 * 1024
        ),
        cost_estimate=pl.CostEstimate(
            flops=2 * length * channels * length * 4, bytes_accessed=4 << 20, transcendentals=0
        ),
    )(
        carry_from,
        tokens_in,
        mix_in,
        jnp.swapaxes(step_size, 1, 2),
        doc_ids,
        out_grad,
        proj_weight,
        conv_weight,
        decay_rate.reshape(1, heads),
        carried_state,
        carried_conv,
    )
    return pl.pallas_call(
        finish_kernel,
        out_shape=(
            jax.ShapeDtypeStruct((out_rows, width), F32),
            jax.ShapeDtypeStruct(carried_state.shape, BF16),
            jax.ShapeDtypeStruct(carried_conv.shape, BF16),
        ),
        in_specs=[hbm] * 5,
        out_specs=(vmem,) * 3,
        scratch_shapes=[pltpu.SMEM(carry_from.shape, jnp.int32)]
        + [pltpu.VMEM(leaf.shape, leaf.dtype) for leaf in landed]
        + [pltpu.SemaphoreType.DMA((5,))],
        compiler_params=pltpu.CompilerParams(vmem_limit_bytes=60 * 1024 * 1024),
    )(carry_from, *buffers)


def solution(mesh):
    return jax.shard_map(
        functools.partial(device_part, mesh.shape["doc"], mesh.shape["fsdp"]),
        mesh=mesh,
        in_specs=(
            P("doc", None, None),
            P("doc", None, "fsdp"),
            P("doc", None, "fsdp"),
            P("doc", None),
            P("doc", None, "fsdp"),
            P("fsdp", None),
            P(None, "fsdp"),
            P("fsdp"),
            P(None, "fsdp", "doc", None),
            P(None, None, "fsdp", "doc"),
            P(),
        ),
        out_specs=(
            P(("doc", "fsdp"), None),
            P(None, "fsdp", "doc", None),
            P(None, None, "fsdp", "doc"),
        ),
        check_vma=False,
    )
```

```python
import functools

import jax
import jax.numpy as jnp
from jax import lax
from jax.experimental import pallas as pl
from jax.experimental.pallas import tpu as pltpu
from jax.sharding import PartitionSpec as P


def silu_slope(value):
    sigmoid_value = jax.nn.sigmoid(value)
    return sigmoid_value * (1.0 + value * (1.0 - sigmoid_value))


def conv_masks(seg_row, tap_count):
    length = seg_row.shape[0]
    opening = seg_row == seg_row[0]
    tap_masks = []
    for offset in range(tap_count):
        earlier = jnp.concatenate([jnp.full((offset,), -1, jnp.int32), seg_row[: length - offset]])
        inside = jnp.arange(length) >= offset
        tap_masks.append(jnp.where(inside, earlier == seg_row, opening))
    return (opening, tap_masks)


def row_pass(
    coeff, mix_row, step_row, seg_row, grad_rows, state_zero, conv_zero, conv_weight, decay_rate
):
    length, channels = mix_row.shape
    head_count = step_row.shape[1]
    head_dim = channels // head_count
    tap_count = conv_weight.shape[0]
    nstate = coeff.shape[1] // 2
    opening, tap_masks = conv_masks(seg_row, tap_count)
    extended = jnp.concatenate([conv_zero, mix_row], axis=0).astype(jnp.float32)
    preact = jnp.zeros((length, channels), jnp.float32)
    for offset in range(tap_count):
        window = extended[tap_count - 1 - offset : tap_count - 1 - offset + length]
        preact = preact + jnp.where(
            tap_masks[offset][:, None], conv_weight[offset][None, :] * window, 0.0
        )
    mixed_rows = jax.nn.silu(preact).astype(jnp.bfloat16)
    values = (
        step_row[:, :, None] * mixed_rows.reshape(length, head_count, head_dim).astype(jnp.float32)
    ).astype(jnp.bfloat16)
    write_coeff = coeff[:, :nstate]
    read_coeff = coeff[:, nstate:]
    scores = jnp.dot(read_coeff, write_coeff.T, preferred_element_type=jnp.float32)
    log_decay = jnp.cumsum(-(decay_rate[None, :] * step_row), axis=0).T
    lower = jnp.arange(length)[:, None] >= jnp.arange(length)[None, :]
    allowed = lower & (seg_row[:, None] == seg_row[None, :])
    spread = log_decay[:, :, None] - log_decay[:, None, :]
    decays = jnp.where(allowed[None], jnp.exp(jnp.where(allowed[None], spread, 0.0)), 0.0)
    edge_weight = jnp.where(opening[None, :], jnp.exp(log_decay), 0.0)
    weighted = (decays * scores[None]).astype(jnp.bfloat16)
    grad_heads = grad_rows.reshape(length, head_count, head_dim)
    values_grad = jnp.einsum(
        "hts,thp->shp", weighted, grad_heads, preferred_element_type=jnp.float32
    )
    products = jnp.einsum("thp,shp->hts", grad_heads, values, preferred_element_type=jnp.float32)
    score_grad = jnp.sum(decays * products, axis=0)
    carried = jnp.einsum("thp,hpn->thn", grad_heads, state_zero, preferred_element_type=jnp.float32)
    read_grad = jnp.dot(
        score_grad, write_coeff.astype(jnp.float32), precision=lax.Precision.HIGHEST
    )
    read_grad = read_grad + jnp.sum(edge_weight.T[:, :, None] * carried, axis=1)
    write_grad = jnp.dot(
        score_grad.T, read_coeff.astype(jnp.float32), precision=lax.Precision.HIGHEST
    )
    scaled = edge_weight.T[:, :, None] * grad_heads.astype(jnp.float32)
    state_grad = jnp.einsum(
        "thp,tn->hpn", scaled, read_coeff.astype(jnp.float32), precision=lax.Precision.HIGHEST
    )
    mixed_grad = (values_grad * step_row[:, :, None]).reshape(length, channels)
    preact_grad = mixed_grad * silu_slope(preact)
    conv_rows = []
    for index_row in range(tap_count - 1):
        running = jnp.zeros((channels,), jnp.float32)
        for offset in range(tap_count - 1 - index_row, tap_count):
            position = index_row - (tap_count - 1) + offset
            running = running + jnp.where(
                opening[position], conv_weight[offset] * preact_grad[position], 0.0
            )
        conv_rows.append(running)
    conv_grad = jnp.stack(conv_rows)
    return (jnp.concatenate([write_grad, read_grad], axis=1), state_grad, conv_grad)


def shards(
    tokens_in,
    mix_in,
    step_size,
    doc_ids,
    out_grad,
    proj_weight,
    conv_weight,
    decay_rate,
    carried_state,
    carried_conv,
    carry_from,
):
    rows_dev, length, model_width = tokens_in.shape
    head_count = step_size.shape[2]
    slot_count = carried_state.shape[0]
    part_p = carried_state.shape[2]
    nstate = carried_state.shape[3]
    tap_count = conv_weight.shape[0]
    doc_count = lax.axis_size("doc")
    head_dim = part_p * doc_count
    channels = head_count * head_dim
    picker = (carry_from[:, None] == jnp.arange(slot_count, dtype=jnp.int32)[None, :]).astype(
        jnp.bfloat16
    )
    chosen_state = jnp.einsum(
        "rs,shpn->rhpn", picker, carried_state, preferred_element_type=jnp.float32
    ).astype(jnp.bfloat16)
    chosen_conv = jnp.einsum(
        "rs,skhp->rkhp", picker, carried_conv, preferred_element_type=jnp.float32
    ).astype(jnp.bfloat16)
    chosen_state = chosen_state.reshape(slot_count, head_count, part_p * nstate)
    chosen_conv = chosen_conv.reshape(slot_count, (tap_count - 1) * head_count, part_p)
    start_state, start_conv = (
        lax.all_to_all(chosen_state, "doc", split_axis=0, concat_axis=2, tiled=True),
        lax.all_to_all(chosen_conv, "doc", split_axis=0, concat_axis=2, tiled=True),
    )
    start_state = start_state.reshape(rows_dev, head_count, head_dim, nstate)
    start_conv = start_conv.reshape(rows_dev, tap_count - 1, channels)
    flattened = tokens_in.reshape(rows_dev * length, model_width)
    coeff_sum = jnp.dot(
        flattened,
        lax.all_gather(proj_weight, "fsdp", axis=0, tiled=True),
        preferred_element_type=jnp.float32,
    )
    coeff = coeff_sum.astype(jnp.bfloat16).reshape(rows_dev, length, proj_weight.shape[1])
    coeff_grad, state_grad, conv_grad = row_pass(
        coeff[0],
        mix_in[0],
        step_size[0],
        doc_ids[0],
        out_grad[0],
        start_state[0],
        start_conv[0],
        conv_weight,
        decay_rate,
    )
    coeff_grads = [coeff_grad]
    state_grads = [state_grad]
    conv_grads = [conv_grad]
    back_state = (
        jnp.stack(state_grads).astype(jnp.bfloat16).reshape(rows_dev, head_count, head_dim * nstate)
    )
    back_conv = (
        jnp.stack(conv_grads)
        .astype(jnp.bfloat16)
        .reshape(rows_dev, (tap_count - 1) * head_count, head_dim)
    )
    got_state, got_conv = (
        lax.all_to_all(back_state, "doc", split_axis=2, concat_axis=0, tiled=True),
        lax.all_to_all(back_conv, "doc", split_axis=2, concat_axis=0, tiled=True),
    )
    grad_state = jnp.einsum(
        "rs,rx->sx", picker, got_state.reshape(slot_count, -1), preferred_element_type=jnp.float32
    )
    grad_state = grad_state.astype(jnp.bfloat16).reshape(carried_state.shape)
    grad_conv = jnp.einsum(
        "rs,rx->sx", picker, got_conv.reshape(slot_count, -1), preferred_element_type=jnp.float32
    )
    grad_conv = grad_conv.astype(jnp.bfloat16).reshape(carried_conv.shape)
    coeff_flat = jnp.stack(coeff_grads).reshape(rows_dev * length, -1)
    share = lax.psum_scatter(coeff_flat, "fsdp", scatter_dimension=1, tiled=True)
    partial_cols = jnp.einsum(
        "tj,tn->jn", flattened.astype(jnp.float32), share, precision=lax.Precision.HIGHEST
    )
    summed_cols = lax.psum_scatter(partial_cols, "doc", scatter_dimension=0, tiled=True)
    grad_proj = lax.all_to_all(summed_cols, "fsdp", split_axis=0, concat_axis=1, tiled=True)
    return (grad_proj, grad_state, grad_conv)


F32 = jnp.float32
BF16 = jnp.bfloat16
MESH = pl.DeviceIdType.MESH


def dot_nn(a, b, precision=None):
    return lax.dot_general(
        a, b, (((1,), (0,)), ((), ())), precision=precision, preferred_element_type=F32
    )


def dot_nt(a, b):
    return lax.dot_general(a, b, (((1,), (1,)), ((), ())), preferred_element_type=F32)


def dot_tn(a, b):
    return lax.dot_general(a, b, (((0,), (0,)), ((), ())), preferred_element_type=F32)


def iota(shape, axis):
    return lax.broadcasted_iota(jnp.int32, shape, axis)


def layer_kernel(
    docs,
    parts,
    carry_hbm,
    tokens_hbm,
    mix_hbm,
    step_hbm,
    seg_hbm,
    grad_hbm,
    weight_hbm,
    taps_hbm,
    rate_hbm,
    state_hbm,
    conv_hbm,
    fin_own,
    fin_recv,
    sgrad_recv,
    cgrad_recv,
    carry_ref,
    mix_ref,
    step_ref,
    seg_ref,
    grad_ref,
    weight_ref,
    taps_ref,
    rate_ref,
    state_ref,
    conv_ref,
    tok_part,
    tok_cols,
    coeff_partial,
    coeff_recv,
    coeff,
    sum_partial,
    sum_send,
    sum_recv,
    sums_of,
    state_send,
    state_recv,
    conv_send,
    conv_recv,
    sgrad_send,
    cgrad_send,
    fin_part,
    fin_send,
    ext,
    seg_ext,
    og_scaled,
    val_scaled,
    first_scale,
    tap_mask,
    factors,
    load_sem,
    store_sem,
    part_send_sem,
    part_recv_sem,
    doc_send_sem,
    doc_recv_sem,
):
    d = lax.axis_index("doc")
    f = lax.axis_index("fsdp")
    length, channels = mix_ref.shape
    heads = step_ref.shape[0]
    head_dim = channels // heads
    part_p = head_dim // docs
    width = weight_ref.shape[1]
    nstate = width // 2
    slots = state_ref.shape[0]
    depth = weight_ref.shape[0]
    block = length // parts
    out_rows = fin_own.shape[0]
    taps = taps_ref.shape[0]

    own_columns = pl.ds(pl.multiple_of(f * depth, 128), depth)
    pairs = [
        (carry_hbm, carry_ref),
        (state_hbm, state_ref),
        (conv_hbm, conv_ref),
        (tokens_hbm.at[0, :, own_columns], tok_part),
        (weight_hbm, weight_ref),
        (step_hbm.at[0], step_ref),
        (rate_hbm, rate_ref),
        (seg_hbm, seg_ref),
        (taps_hbm, taps_ref),
        (mix_hbm.at[0], mix_ref),
        (grad_hbm.at[0], grad_ref),
    ]
    for q in range(docs):
        columns = pl.ds(pl.multiple_of((q * parts + f) * out_rows, 128), out_rows)
        pairs.append(
            (tokens_hbm.at[0, :, columns], tok_cols.at[:, pl.ds(q * out_rows, out_rows)])
        )
    loads = [
        pltpu.make_async_copy(src, dst, load_sem.at[i]) for i, (src, dst) in enumerate(pairs)
    ]
    for load in loads:
        load.start()

    barrier = pltpu.get_barrier_semaphore()
    for j in range(1, parts):
        pl.semaphore_signal(
            barrier, inc=1, device_id=(d, lax.rem(f + j, parts)), device_id_type=MESH
        )
    for j in range(1, docs):
        pl.semaphore_signal(
            barrier, inc=1, device_id=(lax.rem(d + j, docs), f), device_id_type=MESH
        )

    def part_copy(phase, j, src, dst):
        return pltpu.make_async_remote_copy(
            src_ref=src,
            dst_ref=dst,
            send_sem=part_send_sem.at[phase, j],
            recv_sem=part_recv_sem.at[phase, j],
            device_id=(d, lax.rem(f + j, parts)),
            device_id_type=MESH,
        )

    def doc_copy(phase, j, src, dst):
        return pltpu.make_async_remote_copy(
            src_ref=src,
            dst_ref=dst,
            send_sem=doc_send_sem.at[phase, j],
            recv_sem=doc_recv_sem.at[phase, j],
            device_id=(lax.rem(d + j, docs), f),
            device_id_type=MESH,
        )

    def rows_of(owner):
        return pl.ds(pl.multiple_of(owner * block, block), block)

    lane = iota((1, channels), 1)
    head_of_lane = lax.div(lane, head_dim)
    lane_in_head = lane - head_of_lane * head_dim
    place = jnp.where(
        jnp.broadcast_to(lane_in_head, (head_dim, channels)) == iota((head_dim, channels), 0),
        1.0,
        0.0,
    ).astype(BF16)
    head_rows = (taps - 1) * heads
    own_head = jnp.broadcast_to(head_of_lane, (heads, channels)) == iota((heads, channels), 0)

    for load in loads[:3]:
        load.wait()
    for r in range(slots):
        source = carry_ref[r]
        usable = jnp.where(source >= 0, 1.0, 0.0)
        index = jnp.maximum(source, 0)
        state_send[r] = (state_ref[index].astype(F32) * usable).astype(BF16)
        conv_send[r] = (conv_ref[index].astype(F32) * usable).astype(BF16)

    for load in loads[3:5]:
        load.wait()
    coeff_partial[...] = dot_nn(tok_part[...], weight_ref[...])

    pl.semaphore_wait(barrier, parts - 1 + docs - 1)

    conv_copies = [
        doc_copy(0, j, conv_send.at[lax.rem(d + j, docs)], conv_recv.at[d]) for j in range(1, docs)
    ]
    coeff_copies = [
        part_copy(0, j, coeff_partial.at[rows_of(lax.rem(f + j, parts))], coeff_recv.at[j])
        for j in range(1, parts)
    ]
    state_copies = [
        doc_copy(1, j, state_send.at[lax.rem(d + j, docs)], state_recv.at[:, d])
        for j in range(1, docs)
    ]
    for copy in conv_copies + coeff_copies + state_copies:
        copy.start()
    conv_recv[d] = conv_send[d]
    state_recv[:, d] = state_send[d]

    for load in loads[5:11]:
        load.wait()
    lower = iota((length, length), 0) >= iota((length, length), 1)
    rate = jnp.sum(
        jnp.where(iota((heads, heads), 0) == iota((heads, heads), 1), rate_ref[...], 0.0),
        axis=1,
        keepdims=True,
    )
    steps = step_ref[...]
    rest = -(rate * steps)
    pieces = []
    for _ in range(3):
        piece = rest.astype(BF16)
        pieces.append(piece)
        rest = rest - piece.astype(F32)
    sums = dot_nt(
        jnp.concatenate(pieces, axis=0), jnp.where(lower, 1.0, 0.0).astype(BF16)
    )
    log_decay = sums[:heads] + sums[heads : 2 * heads] + sums[2 * heads :]

    def halves(x):
        top = x.astype(BF16).astype(F32)
        both = jnp.concatenate([top, x - top, jnp.zeros((128 - 2 * heads, length), F32)], axis=0)
        return both.T.astype(BF16)

    grow = halves(jnp.exp(log_decay))
    shrink = halves(steps * jnp.exp(-log_decay))

    seg_row = seg_ref[...].astype(F32)
    seg_cols = jnp.broadcast_to(seg_row, (128, length)).T
    seg_ext[8:, :] = seg_cols
    seg_ext[:8, :] = jnp.broadcast_to(seg_cols[:1], (8, 128))
    opening = seg_cols == seg_cols[:1]

    for k in range(1, taps):
        tap_mask[k - 1] = jnp.where(seg_ext[8 - k : 8 - k + length, :] == seg_cols, 1.0, 0.0)

    def scaled_values(preact, factor):
        return (preact * (0.5 + 0.5 * jnp.tanh(0.5 * preact)) * factor).astype(BF16)

    ext[:8, :] = jnp.zeros((8, channels), F32)

    def chunk(c, carry):
        lanes = pl.ds(pl.multiple_of(c * 128, 128), 128)
        row = iota((128, 128), 0)
        head = jnp.broadcast_to(
            lax.div(iota((1, 128), 1) + c * 128, head_dim), (128, 128)
        )
        expand = jnp.where((row == head) | (row == head + heads), 1.0, 0.0).astype(BF16)

        def per_channel(both):
            return dot_nn(both, expand)

        ext[8:, lanes] = mix_ref[:, lanes].astype(F32)
        factors[0] = per_channel(grow)
        factors[1] = per_channel(shrink)
        first_scale[:, lanes] = factors[1, :16, :]
        for base in range(0, length, 64):
            rows = slice(base, base + 64)
            preact = taps_ref[0:1, lanes] * ext[8 + base : 72 + base, lanes]
            for k in range(1, taps):
                window = ext[8 - k + base : 72 - k + base, lanes]
                preact = preact + taps_ref[k : k + 1, lanes] * (tap_mask[k - 1, rows, :] * window)
            val_scaled[rows, lanes] = scaled_values(preact, factors[1, rows, :])
            og_scaled[rows, lanes] = (
                grad_ref[rows, lanes].astype(F32) * factors[0, rows, :]
            ).astype(BF16)
        return carry

    chunks = channels // 128
    lax.fori_loop(0, chunks, chunk, 0)

    for copy in coeff_copies:
        copy.wait_recv()
    total = coeff_partial[rows_of(f)]
    for j in range(1, parts):
        total = total + coeff_recv[j]
    coeff[rows_of(f)] = total.astype(BF16)
    gather_copies = [
        part_copy(1, j, coeff.at[rows_of(f)], coeff.at[rows_of(f)]) for j in range(1, parts)
    ]
    for copy in gather_copies:
        copy.start()


    for copy in conv_copies:
        copy.wait_recv()

    spread = dot_nn(
        jnp.concatenate(
            [conv_recv[q].reshape(head_rows, part_p) for q in range(docs)], axis=1
        ),
        place,
    )
    carried_rows = jnp.sum(
        jnp.where(own_head[None], spread.reshape(taps - 1, heads, channels), 0.0), axis=1
    )
    ext[8 - (taps - 1) : 8, :] = carried_rows
    pre = jnp.zeros((16, channels), F32)
    for k in range(taps):
        same = seg_ext[8 - k : 24 - k, :1] == seg_cols[:16, :1]
        window = ext[8 - k : 24 - k, :]
        pre = pre + jnp.where(same, taps_ref[k : k + 1, :] * window, 0.0)
    val_scaled[:16, :] = scaled_values(pre, first_scale[...])

    same_doc = seg_cols[:, :1] == seg_row
    score_grad = jnp.where(lower & same_doc, dot_nt(og_scaled[...], val_scaled[...]), 0.0)
    sum_partial[:, :length] = score_grad
    sum_send[:, :length] = score_grad.astype(BF16)
    for copy in state_copies:
        copy.wait_recv()
    from_state = jnp.where(
        opening, dot_nn(og_scaled[...], state_recv[...].reshape(channels, nstate)), 0.0
    )
    sum_partial[:, length:] = from_state
    sum_send[:, length:] = from_state.astype(BF16)

    sum_copies = [
        part_copy(2, j, sum_send.at[rows_of(lax.rem(f + j, parts))], sum_recv.at[j])
        for j in range(1, parts)
    ]
    for copy in sum_copies:
        copy.start()

    for copy in gather_copies:
        copy.wait_recv()
    write_coeff = coeff[:, :nstate]
    read_coeff = coeff[:, nstate:]

    open_read = jnp.where(opening, read_coeff.astype(F32), 0.0).astype(BF16)
    sgrad_send[...] = (
        dot_tn(og_scaled[...], open_read).astype(BF16).reshape(heads, docs, part_p, nstate)
    )
    sgrad_copies = [
        doc_copy(2, j, sgrad_send.at[:, lax.rem(d + j, docs)], sgrad_recv.at[d])
        for j in range(1, docs)
    ]
    for copy in sgrad_copies:
        copy.start()
    stores = [
        pltpu.make_async_copy(sgrad_send.at[:, d], sgrad_recv.at[d], store_sem.at[0]),
    ]
    stores[0].start()
    for load in loads[11:]:
        load.wait()
    tok_rows = tok_cols[...].T

    for copy in sum_copies:
        copy.wait_recv()
    total = sum_partial[rows_of(f)]
    for j in range(1, parts):
        total = total + sum_recv[j].astype(F32)
    sums_of[rows_of(f)] = total.astype(BF16)
    total_copies = [
        part_copy(3, j, sums_of.at[rows_of(f)], sums_of.at[rows_of(f)]) for j in range(1, parts)
    ]
    for copy in total_copies:
        copy.start()

    first_scores = dot_nt(write_coeff[:16], read_coeff)
    first_seg = jnp.broadcast_to(seg_row, (16, length)) == seg_cols[:16, :1]
    first_allowed = first_seg & (iota((16, length), 1) >= iota((16, length), 0))
    first_scores = jnp.where(first_allowed, first_scores, 0.0).astype(BF16)
    first_grad = dot_nn(first_scores, og_scaled[...])[:8]
    pre = pre[:8]
    gate = 1.0 / (1.0 + jnp.exp(-pre))
    pre_grad = first_grad * first_scale[:8] * gate * (1.0 + pre * (1.0 - gate))
    pre_grad = jnp.where(seg_cols[:8, :1] == seg_cols[:1, :1], pre_grad, 0.0)
    conv_rows = []
    for row in range(taps - 1):
        running = jnp.zeros((1, channels), F32)
        for k in range(taps - 1 - row, taps):
            position = row - (taps - 1) + k
            running = running + taps_ref[k : k + 1, :] * pre_grad[position : position + 1]
        conv_rows.append(
            jnp.where(own_head, jnp.broadcast_to(running, (heads, channels)), 0.0).astype(BF16)
        )
    placed = dot_nt(jnp.concatenate(conv_rows, axis=0), place).astype(BF16)
    for q in range(docs):
        cgrad_send[q] = placed[:, q * part_p : (q + 1) * part_p].reshape(
            taps - 1, heads, part_p
        )
    cgrad_copies = [
        doc_copy(3, j, cgrad_send.at[lax.rem(d + j, docs)], cgrad_recv.at[d])
        for j in range(1, docs)
    ]
    for copy in cgrad_copies:
        copy.start()
    stores.append(pltpu.make_async_copy(cgrad_send.at[d], cgrad_recv.at[d], store_sem.at[1]))
    stores[1].start()

    for copy in total_copies:
        copy.wait_recv()
    score_total = sums_of[:, :length]
    write_grad = dot_tn(score_total, read_coeff)
    read_grad = dot_nn(score_total, write_coeff) + sums_of[:, length:].astype(F32)
    cg = jnp.concatenate([write_grad, read_grad], axis=1).astype(BF16)
    product = dot_nn(tok_rows, cg).reshape(docs, out_rows, width)
    fin_send[...] = product.astype(BF16)
    fin_copies = [
        doc_copy(4, j, fin_send.at[lax.rem(d + j, docs)], fin_recv.at[j - 1])
        for j in range(1, docs)
    ]
    for copy in fin_copies:
        copy.start()
    fin_part[...] = product
    stores.append(pltpu.make_async_copy(fin_part.at[d], fin_own, store_sem.at[2]))
    stores[2].start()
    for copy in sgrad_copies + cgrad_copies + fin_copies:
        copy.wait_recv()
    for store in stores:
        store.wait()

    for copies in (
        conv_copies,
        coeff_copies,
        state_copies,
        gather_copies,
        sum_copies,
        sgrad_copies,
        cgrad_copies,
        total_copies,
        fin_copies,
    ):
        for copy in copies:
            copy.wait_send()


def finish_kernel(
    carry_hbm,
    own_hbm,
    recv_hbm,
    sgrad_hbm,
    cgrad_hbm,
    proj_out,
    state_out,
    conv_out,
    carry_ref,
    own_ref,
    recv_ref,
    sgrad_ref,
    cgrad_ref,
    load_sem,
):
    pairs = (
        (carry_hbm, carry_ref),
        (sgrad_hbm, sgrad_ref),
        (cgrad_hbm, cgrad_ref),
        (own_hbm, own_ref),
        (recv_hbm, recv_ref),
    )
    loads = [
        pltpu.make_async_copy(src, dst, load_sem.at[i]) for i, (src, dst) in enumerate(pairs)
    ]
    for load in loads:
        load.start()
    for load in loads:
        load.wait()
    slots = state_out.shape[0]
    for s in range(slots):
        row_of = jnp.int32(0)
        found = jnp.float32(0.0)
        for r in range(slots):
            hit = carry_ref[r] == s
            row_of = jnp.where(hit, r, row_of)
            found = jnp.where(hit, 1.0, found)
        state_out[s] = (sgrad_ref[row_of].astype(F32) * found).astype(BF16)
        conv_out[s] = (cgrad_ref[row_of].astype(F32) * found).astype(BF16)
    result = own_ref[...]
    for j in range(recv_ref.shape[0]):
        result = result + recv_ref[j].astype(F32)
    proj_out[...] = result


def device_part(docs, parts, *args):
    (
        tokens_in,
        mix_in,
        step_size,
        doc_ids,
        out_grad,
        proj_weight,
        conv_weight,
        decay_rate,
        carried_state,
        carried_conv,
        carry_from,
    ) = args
    rows_dev, length, model_width = tokens_in.shape
    channels = mix_in.shape[2]
    heads = step_size.shape[2]
    depth, width = proj_weight.shape
    slots, _, part_p, nstate = carried_state.shape
    taps = conv_weight.shape[0]
    out_rows = model_width // (docs * parts)
    block = length // parts
    aligned = (
        rows_dev == 1
        and slots == docs
        and part_p % 16 == 0
        and heads % 16 == 0
        and 2 * heads <= 128
        and block % 16 == 0
        and length % 128 == 0
        and out_rows % 128 == 0
        and depth % 128 == 0
        and nstate == 128
        and channels % 128 == 0
        and taps <= 8
    )
    if not aligned:
        return shards(*args)
    vmem = pl.BlockSpec(memory_space=pltpu.VMEM)
    hbm = pl.BlockSpec(memory_space=pltpu.HBM)
    landed = (
        jax.ShapeDtypeStruct((out_rows, width), F32),
        jax.ShapeDtypeStruct((docs - 1, out_rows, width), BF16),
        jax.ShapeDtypeStruct(carried_state.shape, BF16),
        jax.ShapeDtypeStruct(carried_conv.shape, BF16),
    )
    buffers = pl.pallas_call(
        functools.partial(layer_kernel, docs, parts),
        out_shape=landed,
        in_specs=[hbm] * 11,
        out_specs=(hbm,) * 4,
        scratch_shapes=[
            pltpu.SMEM(carry_from.shape, jnp.int32),
            pltpu.VMEM((length, channels), BF16),
            pltpu.VMEM((heads, length), F32),
            pltpu.VMEM(doc_ids.shape, jnp.int32),
            pltpu.VMEM((length, channels), BF16),
            pltpu.VMEM(proj_weight.shape, BF16),
            pltpu.VMEM(conv_weight.shape, F32),
            pltpu.VMEM((1, heads), F32),
            pltpu.VMEM(carried_state.shape, BF16),
            pltpu.VMEM(carried_conv.shape, BF16),
            pltpu.VMEM((length, depth), BF16),
            pltpu.VMEM((length, docs * out_rows), BF16),
            pltpu.VMEM((length, width), F32),
            pltpu.VMEM((parts, block, width), F32),
            pltpu.VMEM((length, width), BF16),
            pltpu.VMEM((length, length + nstate), F32),
            pltpu.VMEM((length, length + nstate), BF16),
            pltpu.VMEM((parts, block, length + nstate), BF16),
            pltpu.VMEM((length, length + nstate), BF16),
            pltpu.VMEM((slots, heads, part_p, nstate), BF16),
            pltpu.VMEM((heads, docs, part_p, nstate), BF16),
            pltpu.VMEM((slots, taps - 1, heads, part_p), BF16),
            pltpu.VMEM((docs, taps - 1, heads, part_p), BF16),
            pltpu.VMEM((heads, docs, part_p, nstate), BF16),
            pltpu.VMEM((docs, taps - 1, heads, part_p), BF16),
            pltpu.VMEM((docs, out_rows, width), F32),
            pltpu.VMEM((docs, out_rows, width), BF16),
            pltpu.VMEM((length + 8, channels), F32),
            pltpu.VMEM((length + 8, 128), F32),
            pltpu.VMEM((length, channels), BF16),
            pltpu.VMEM((length, channels), BF16),
            pltpu.VMEM((16, channels), F32),
            pltpu.VMEM((taps - 1, length, 128), F32),
            pltpu.VMEM((2, length, 128), F32),
            pltpu.SemaphoreType.DMA((11 + docs,)),
            pltpu.SemaphoreType.DMA((3,)),
            pltpu.SemaphoreType.DMA((4, parts)),
            pltpu.SemaphoreType.DMA((4, parts)),
            pltpu.SemaphoreType.DMA((5, docs)),
            pltpu.SemaphoreType.DMA((5, docs)),
        ],
        compiler_params=pltpu.CompilerParams(
            collective_id=0, has_side_effects=True, vmem_limit_bytes=60 * 1024 * 1024
        ),
        cost_estimate=pl.CostEstimate(
            flops=2 * length * channels * length * 4, bytes_accessed=4 << 20, transcendentals=0
        ),
    )(
        carry_from,
        tokens_in,
        mix_in,
        jnp.swapaxes(step_size, 1, 2),
        doc_ids,
        out_grad,
        proj_weight,
        conv_weight,
        decay_rate.reshape(1, heads),
        carried_state,
        carried_conv,
    )
    return pl.pallas_call(
        finish_kernel,
        out_shape=(
            jax.ShapeDtypeStruct((out_rows, width), F32),
            jax.ShapeDtypeStruct(carried_state.shape, BF16),
            jax.ShapeDtypeStruct(carried_conv.shape, BF16),
        ),
        in_specs=[hbm] * 5,
        out_specs=(vmem,) * 3,
        scratch_shapes=[pltpu.SMEM(carry_from.shape, jnp.int32)]
        + [pltpu.VMEM(leaf.shape, leaf.dtype) for leaf in landed]
        + [pltpu.SemaphoreType.DMA((5,))],
        compiler_params=pltpu.CompilerParams(vmem_limit_bytes=60 * 1024 * 1024),
    )(carry_from, *buffers)


def solution(mesh):
    return jax.shard_map(
        functools.partial(device_part, mesh.shape["doc"], mesh.shape["fsdp"]),
        mesh=mesh,
        in_specs=(
            P("doc", None, None),
            P("doc", None, "fsdp"),
            P("doc", None, "fsdp"),
            P("doc", None),
            P("doc", None, "fsdp"),
            P("fsdp", None),
            P(None, "fsdp"),
            P("fsdp"),
            P(None, "fsdp", "doc", None),
            P(None, None, "fsdp", "doc"),
            P(),
        ),
        out_specs=(
            P(("doc", "fsdp"), None),
            P(None, "fsdp", "doc", None),
            P(None, None, "fsdp", "doc"),
        ),
        check_vma=False,
    )
```

```python
import functools

import jax
import jax.numpy as jnp
from jax import lax
from jax.experimental import pallas as pl
from jax.experimental.pallas import tpu as pltpu
from jax.sharding import PartitionSpec as P


def silu_slope(value):
    sigmoid_value = jax.nn.sigmoid(value)
    return sigmoid_value * (1.0 + value * (1.0 - sigmoid_value))


def conv_masks(seg_row, tap_count):
    length = seg_row.shape[0]
    opening = seg_row == seg_row[0]
    tap_masks = []
    for offset in range(tap_count):
        earlier = jnp.concatenate([jnp.full((offset,), -1, jnp.int32), seg_row[: length - offset]])
        inside = jnp.arange(length) >= offset
        tap_masks.append(jnp.where(inside, earlier == seg_row, opening))
    return (opening, tap_masks)


def row_pass(
    coeff, mix_row, step_row, seg_row, grad_rows, state_zero, conv_zero, conv_weight, decay_rate
):
    length, channels = mix_row.shape
    head_count = step_row.shape[1]
    head_dim = channels // head_count
    tap_count = conv_weight.shape[0]
    nstate = coeff.shape[1] // 2
    opening, tap_masks = conv_masks(seg_row, tap_count)
    extended = jnp.concatenate([conv_zero, mix_row], axis=0).astype(jnp.float32)
    preact = jnp.zeros((length, channels), jnp.float32)
    for offset in range(tap_count):
        window = extended[tap_count - 1 - offset : tap_count - 1 - offset + length]
        preact = preact + jnp.where(
            tap_masks[offset][:, None], conv_weight[offset][None, :] * window, 0.0
        )
    mixed_rows = jax.nn.silu(preact).astype(jnp.bfloat16)
    values = (
        step_row[:, :, None] * mixed_rows.reshape(length, head_count, head_dim).astype(jnp.float32)
    ).astype(jnp.bfloat16)
    write_coeff = coeff[:, :nstate]
    read_coeff = coeff[:, nstate:]
    scores = jnp.dot(read_coeff, write_coeff.T, preferred_element_type=jnp.float32)
    log_decay = jnp.cumsum(-(decay_rate[None, :] * step_row), axis=0).T
    lower = jnp.arange(length)[:, None] >= jnp.arange(length)[None, :]
    allowed = lower & (seg_row[:, None] == seg_row[None, :])
    spread = log_decay[:, :, None] - log_decay[:, None, :]
    decays = jnp.where(allowed[None], jnp.exp(jnp.where(allowed[None], spread, 0.0)), 0.0)
    edge_weight = jnp.where(opening[None, :], jnp.exp(log_decay), 0.0)
    weighted = (decays * scores[None]).astype(jnp.bfloat16)
    grad_heads = grad_rows.reshape(length, head_count, head_dim)
    values_grad = jnp.einsum(
        "hts,thp->shp", weighted, grad_heads, preferred_element_type=jnp.float32
    )
    products = jnp.einsum("thp,shp->hts", grad_heads, values, preferred_element_type=jnp.float32)
    score_grad = jnp.sum(decays * products, axis=0)
    carried = jnp.einsum("thp,hpn->thn", grad_heads, state_zero, preferred_element_type=jnp.float32)
    read_grad = jnp.dot(
        score_grad, write_coeff.astype(jnp.float32), precision=lax.Precision.HIGHEST
    )
    read_grad = read_grad + jnp.sum(edge_weight.T[:, :, None] * carried, axis=1)
    write_grad = jnp.dot(
        score_grad.T, read_coeff.astype(jnp.float32), precision=lax.Precision.HIGHEST
    )
    scaled = edge_weight.T[:, :, None] * grad_heads.astype(jnp.float32)
    state_grad = jnp.einsum(
        "thp,tn->hpn", scaled, read_coeff.astype(jnp.float32), precision=lax.Precision.HIGHEST
    )
    mixed_grad = (values_grad * step_row[:, :, None]).reshape(length, channels)
    preact_grad = mixed_grad * silu_slope(preact)
    conv_rows = []
    for index_row in range(tap_count - 1):
        running = jnp.zeros((channels,), jnp.float32)
        for offset in range(tap_count - 1 - index_row, tap_count):
            position = index_row - (tap_count - 1) + offset
            running = running + jnp.where(
                opening[position], conv_weight[offset] * preact_grad[position], 0.0
            )
        conv_rows.append(running)
    conv_grad = jnp.stack(conv_rows)
    return (jnp.concatenate([write_grad, read_grad], axis=1), state_grad, conv_grad)


def shards(
    tokens_in,
    mix_in,
    step_size,
    doc_ids,
    out_grad,
    proj_weight,
    conv_weight,
    decay_rate,
    carried_state,
    carried_conv,
    carry_from,
):
    rows_dev, length, model_width = tokens_in.shape
    head_count = step_size.shape[2]
    slot_count = carried_state.shape[0]
    part_p = carried_state.shape[2]
    nstate = carried_state.shape[3]
    tap_count = conv_weight.shape[0]
    doc_count = lax.axis_size("doc")
    head_dim = part_p * doc_count
    channels = head_count * head_dim
    picker = (carry_from[:, None] == jnp.arange(slot_count, dtype=jnp.int32)[None, :]).astype(
        jnp.bfloat16
    )
    chosen_state = jnp.einsum(
        "rs,shpn->rhpn", picker, carried_state, preferred_element_type=jnp.float32
    ).astype(jnp.bfloat16)
    chosen_conv = jnp.einsum(
        "rs,skhp->rkhp", picker, carried_conv, preferred_element_type=jnp.float32
    ).astype(jnp.bfloat16)
    chosen_state = chosen_state.reshape(slot_count, head_count, part_p * nstate)
    chosen_conv = chosen_conv.reshape(slot_count, (tap_count - 1) * head_count, part_p)
    start_state, start_conv = (
        lax.all_to_all(chosen_state, "doc", split_axis=0, concat_axis=2, tiled=True),
        lax.all_to_all(chosen_conv, "doc", split_axis=0, concat_axis=2, tiled=True),
    )
    start_state = start_state.reshape(rows_dev, head_count, head_dim, nstate)
    start_conv = start_conv.reshape(rows_dev, tap_count - 1, channels)
    flattened = tokens_in.reshape(rows_dev * length, model_width)
    coeff_sum = jnp.dot(
        flattened,
        lax.all_gather(proj_weight, "fsdp", axis=0, tiled=True),
        preferred_element_type=jnp.float32,
    )
    coeff = coeff_sum.astype(jnp.bfloat16).reshape(rows_dev, length, proj_weight.shape[1])
    coeff_grad, state_grad, conv_grad = row_pass(
        coeff[0],
        mix_in[0],
        step_size[0],
        doc_ids[0],
        out_grad[0],
        start_state[0],
        start_conv[0],
        conv_weight,
        decay_rate,
    )
    coeff_grads = [coeff_grad]
    state_grads = [state_grad]
    conv_grads = [conv_grad]
    back_state = (
        jnp.stack(state_grads).astype(jnp.bfloat16).reshape(rows_dev, head_count, head_dim * nstate)
    )
    back_conv = (
        jnp.stack(conv_grads)
        .astype(jnp.bfloat16)
        .reshape(rows_dev, (tap_count - 1) * head_count, head_dim)
    )
    got_state, got_conv = (
        lax.all_to_all(back_state, "doc", split_axis=2, concat_axis=0, tiled=True),
        lax.all_to_all(back_conv, "doc", split_axis=2, concat_axis=0, tiled=True),
    )
    grad_state = jnp.einsum(
        "rs,rx->sx", picker, got_state.reshape(slot_count, -1), preferred_element_type=jnp.float32
    )
    grad_state = grad_state.astype(jnp.bfloat16).reshape(carried_state.shape)
    grad_conv = jnp.einsum(
        "rs,rx->sx", picker, got_conv.reshape(slot_count, -1), preferred_element_type=jnp.float32
    )
    grad_conv = grad_conv.astype(jnp.bfloat16).reshape(carried_conv.shape)
    coeff_flat = jnp.stack(coeff_grads).reshape(rows_dev * length, -1)
    share = lax.psum_scatter(coeff_flat, "fsdp", scatter_dimension=1, tiled=True)
    partial_cols = jnp.einsum(
        "tj,tn->jn", flattened.astype(jnp.float32), share, precision=lax.Precision.HIGHEST
    )
    summed_cols = lax.psum_scatter(partial_cols, "doc", scatter_dimension=0, tiled=True)
    grad_proj = lax.all_to_all(summed_cols, "fsdp", split_axis=0, concat_axis=1, tiled=True)
    return (grad_proj, grad_state, grad_conv)


F32 = jnp.float32
BF16 = jnp.bfloat16
MESH = pl.DeviceIdType.MESH


def dot_nn(a, b, precision=None):
    return lax.dot_general(
        a, b, (((1,), (0,)), ((), ())), precision=precision, preferred_element_type=F32
    )


def dot_nt(a, b):
    return lax.dot_general(a, b, (((1,), (1,)), ((), ())), preferred_element_type=F32)


def dot_tn(a, b):
    return lax.dot_general(a, b, (((0,), (0,)), ((), ())), preferred_element_type=F32)


def iota(shape, axis):
    return lax.broadcasted_iota(jnp.int32, shape, axis)


def layer_kernel(
    docs,
    parts,
    carry_hbm,
    tokens_hbm,
    mix_hbm,
    step_hbm,
    seg_hbm,
    grad_hbm,
    weight_hbm,
    taps_hbm,
    rate_hbm,
    state_hbm,
    conv_hbm,
    fin_own,
    fin_recv,
    sgrad_recv,
    cgrad_recv,
    carry_ref,
    mix_ref,
    step_ref,
    seg_ref,
    grad_ref,
    weight_ref,
    taps_ref,
    rate_ref,
    state_ref,
    conv_ref,
    tok_part,
    tok_cols,
    coeff_partial,
    coeff_recv,
    coeff,
    sum_partial,
    sum_send,
    sum_recv,
    sums_of,
    state_send,
    state_recv,
    conv_send,
    conv_recv,
    sgrad_send,
    cgrad_send,
    fin_part,
    fin_send,
    ext,
    seg_ext,
    og_scaled,
    val_scaled,
    first_scale,
    tap_mask,
    factors,
    load_sem,
    store_sem,
    part_send_sem,
    part_recv_sem,
    doc_send_sem,
    doc_recv_sem,
):
    d = lax.axis_index("doc")
    f = lax.axis_index("fsdp")
    length, channels = mix_ref.shape
    heads = step_ref.shape[0]
    head_dim = channels // heads
    part_p = head_dim // docs
    width = weight_ref.shape[1]
    nstate = width // 2
    slots = state_ref.shape[0]
    depth = weight_ref.shape[0]
    block = length // parts
    out_rows = fin_own.shape[0]
    taps = taps_ref.shape[0]

    own_columns = pl.ds(pl.multiple_of(f * depth, 128), depth)
    pairs = [
        (carry_hbm, carry_ref),
        (state_hbm, state_ref),
        (conv_hbm, conv_ref),
        (tokens_hbm.at[0, :, own_columns], tok_part),
        (weight_hbm, weight_ref),
        (step_hbm.at[0], step_ref),
        (rate_hbm, rate_ref),
        (seg_hbm, seg_ref),
        (taps_hbm, taps_ref),
        (mix_hbm.at[0], mix_ref),
        (grad_hbm.at[0], grad_ref),
    ]
    for q in range(docs):
        columns = pl.ds(pl.multiple_of((q * parts + f) * out_rows, 128), out_rows)
        pairs.append(
            (tokens_hbm.at[0, :, columns], tok_cols.at[:, pl.ds(q * out_rows, out_rows)])
        )
    loads = [
        pltpu.make_async_copy(src, dst, load_sem.at[i]) for i, (src, dst) in enumerate(pairs)
    ]
    for load in loads:
        load.start()

    barrier = pltpu.get_barrier_semaphore()
    for j in range(1, parts):
        pl.semaphore_signal(
            barrier, inc=1, device_id=(d, lax.rem(f + j, parts)), device_id_type=MESH
        )
    for j in range(1, docs):
        pl.semaphore_signal(
            barrier, inc=1, device_id=(lax.rem(d + j, docs), f), device_id_type=MESH
        )

    def part_copy(phase, j, src, dst):
        return pltpu.make_async_remote_copy(
            src_ref=src,
            dst_ref=dst,
            send_sem=part_send_sem.at[phase, j],
            recv_sem=part_recv_sem.at[phase, j],
            device_id=(d, lax.rem(f + j, parts)),
            device_id_type=MESH,
        )

    def doc_copy(phase, j, src, dst):
        return pltpu.make_async_remote_copy(
            src_ref=src,
            dst_ref=dst,
            send_sem=doc_send_sem.at[phase, j],
            recv_sem=doc_recv_sem.at[phase, j],
            device_id=(lax.rem(d + j, docs), f),
            device_id_type=MESH,
        )

    def rows_of(owner):
        return pl.ds(pl.multiple_of(owner * block, block), block)

    lane = iota((1, channels), 1)
    head_of_lane = lax.div(lane, head_dim)
    lane_in_head = lane - head_of_lane * head_dim
    place = jnp.where(
        jnp.broadcast_to(lane_in_head, (head_dim, channels)) == iota((head_dim, channels), 0),
        1.0,
        0.0,
    ).astype(BF16)
    head_rows = (taps - 1) * heads
    own_head = jnp.broadcast_to(head_of_lane, (heads, channels)) == iota((heads, channels), 0)

    for load in loads[:3]:
        load.wait()
    for r in range(slots):
        source = carry_ref[r]
        usable = jnp.where(source >= 0, 1.0, 0.0)
        index = jnp.maximum(source, 0)
        state_send[r] = (state_ref[index].astype(F32) * usable).astype(BF16)
        conv_send[r] = (conv_ref[index].astype(F32) * usable).astype(BF16)

    for load in loads[3:5]:
        load.wait()
    coeff_partial[...] = dot_nn(tok_part[...], weight_ref[...])

    pl.semaphore_wait(barrier, parts - 1 + docs - 1)

    conv_copies = [
        doc_copy(0, j, conv_send.at[lax.rem(d + j, docs)], conv_recv.at[d]) for j in range(1, docs)
    ]
    coeff_copies = [
        part_copy(0, j, coeff_partial.at[rows_of(lax.rem(f + j, parts))], coeff_recv.at[j])
        for j in range(1, parts)
    ]
    state_copies = [
        doc_copy(1, j, state_send.at[lax.rem(d + j, docs)], state_recv.at[:, d])
        for j in range(1, docs)
    ]
    for copy in conv_copies + coeff_copies + state_copies:
        copy.start()
    conv_recv[d] = conv_send[d]
    state_recv[:, d] = state_send[d]

    for load in loads[5:11]:
        load.wait()
    lower = iota((length, length), 0) >= iota((length, length), 1)
    rate = jnp.sum(
        jnp.where(iota((heads, heads), 0) == iota((heads, heads), 1), rate_ref[...], 0.0),
        axis=1,
        keepdims=True,
    )
    steps = step_ref[...]
    rest = -(rate * steps)
    pieces = []
    for _ in range(3):
        piece = rest.astype(BF16)
        pieces.append(piece)
        rest = rest - piece.astype(F32)
    sums = dot_nt(
        jnp.concatenate(pieces, axis=0), jnp.where(lower, 1.0, 0.0).astype(BF16)
    )
    log_decay = sums[:heads] + sums[heads : 2 * heads] + sums[2 * heads :]

    def halves(x):
        top = x.astype(BF16).astype(F32)
        both = jnp.concatenate([top, x - top, jnp.zeros((128 - 2 * heads, length), F32)], axis=0)
        return both.T.astype(BF16)

    grow = halves(jnp.exp(log_decay))
    shrink = halves(steps * jnp.exp(-log_decay))

    seg_row = seg_ref[...].astype(F32)
    seg_cols = jnp.broadcast_to(seg_row, (128, length)).T
    seg_ext[8:, :] = seg_cols
    seg_ext[:8, :] = jnp.broadcast_to(seg_cols[:1], (8, 128))
    opening = seg_cols == seg_cols[:1]

    for k in range(1, taps):
        tap_mask[k - 1] = jnp.where(seg_ext[8 - k : 8 - k + length, :] == seg_cols, 1.0, 0.0)

    def scaled_values(preact, factor):
        return (preact * (0.5 + 0.5 * jnp.tanh(0.5 * preact)) * factor).astype(BF16)

    ext[:8, :] = jnp.zeros((8, channels), F32)

    row = iota((128, channels), 0)
    head = jnp.broadcast_to(head_of_lane, (128, channels))
    expand = jnp.where((row == head) | (row == head + heads), 1.0, 0.0).astype(BF16)
    factors[0] = dot_nn(grow, expand)
    factors[1] = dot_nn(shrink, expand)
    first_scale[...] = factors[1, :16, :]

    def chunk(c):
        lanes = slice(c * 128, (c + 1) * 128)
        ext[8:, lanes] = mix_ref[:, lanes].astype(F32)
        for base in range(0, length, 64):
            rows = slice(base, base + 64)
            preact = taps_ref[0:1, lanes] * ext[8 + base : 72 + base, lanes]
            for k in range(1, taps):
                window = ext[8 - k + base : 72 - k + base, lanes]
                preact = preact + taps_ref[k : k + 1, lanes] * (tap_mask[k - 1, rows, :] * window)
            val_scaled[rows, lanes] = scaled_values(preact, factors[1, rows, lanes])
            og_scaled[rows, lanes] = (
                grad_ref[rows, lanes].astype(F32) * factors[0, rows, lanes]
            ).astype(BF16)

    chunks = channels // 128
    for c in range(chunks // 2):
        chunk(c)

    for copy in coeff_copies:
        copy.wait_recv()
    total = coeff_partial[rows_of(f)]
    for j in range(1, parts):
        total = total + coeff_recv[j]
    coeff[rows_of(f)] = total.astype(BF16)
    gather_copies = [
        part_copy(1, j, coeff.at[rows_of(f)], coeff.at[rows_of(f)]) for j in range(1, parts)
    ]
    for copy in gather_copies:
        copy.start()


    for c in range(chunks // 2, chunks):
        chunk(c)

    for copy in conv_copies:
        copy.wait_recv()

    spread = dot_nn(
        jnp.concatenate(
            [conv_recv[q].reshape(head_rows, part_p) for q in range(docs)], axis=1
        ),
        place,
    )
    carried_rows = jnp.sum(
        jnp.where(own_head[None], spread.reshape(taps - 1, heads, channels), 0.0), axis=1
    )
    ext[8 - (taps - 1) : 8, :] = carried_rows
    pre = jnp.zeros((16, channels), F32)
    for k in range(taps):
        same = seg_ext[8 - k : 24 - k, :1] == seg_cols[:16, :1]
        window = ext[8 - k : 24 - k, :]
        pre = pre + jnp.where(same, taps_ref[k : k + 1, :] * window, 0.0)
    val_scaled[:16, :] = scaled_values(pre, first_scale[...])

    same_doc = seg_cols[:, :1] == seg_row
    score_grad = jnp.where(lower & same_doc, dot_nt(og_scaled[...], val_scaled[...]), 0.0)
    sum_partial[:, :length] = score_grad
    sum_send[:, :length] = score_grad.astype(BF16)
    for copy in state_copies:
        copy.wait_recv()
    from_state = jnp.where(
        opening, dot_nn(og_scaled[...], state_recv[...].reshape(channels, nstate)), 0.0
    )
    sum_partial[:, length:] = from_state
    sum_send[:, length:] = from_state.astype(BF16)

    sum_copies = [
        part_copy(2, j, sum_send.at[rows_of(lax.rem(f + j, parts))], sum_recv.at[j])
        for j in range(1, parts)
    ]
    for copy in sum_copies:
        copy.start()

    for load in loads[11:]:
        load.wait()
    tok_rows = tok_cols[...].T

    for copy in sum_copies:
        copy.wait_recv()
    total = sum_partial[rows_of(f)]
    for j in range(1, parts):
        total = total + sum_recv[j].astype(F32)
    sums_of[rows_of(f)] = total.astype(BF16)
    total_copies = [
        part_copy(3, j, sums_of.at[rows_of(f)], sums_of.at[rows_of(f)]) for j in range(1, parts)
    ]
    for copy in total_copies:
        copy.start()

    for copy in gather_copies:
        copy.wait_recv()
    write_coeff = coeff[:, :nstate]
    read_coeff = coeff[:, nstate:]

    open_read = jnp.where(opening, read_coeff.astype(F32), 0.0).astype(BF16)
    sgrad_send[...] = (
        dot_tn(og_scaled[...], open_read).astype(BF16).reshape(heads, docs, part_p, nstate)
    )
    sgrad_copies = [
        doc_copy(2, j, sgrad_send.at[:, lax.rem(d + j, docs)], sgrad_recv.at[d])
        for j in range(1, docs)
    ]
    for copy in sgrad_copies:
        copy.start()
    stores = [
        pltpu.make_async_copy(sgrad_send.at[:, d], sgrad_recv.at[d], store_sem.at[0]),
    ]
    stores[0].start()
    first_scores = dot_nt(write_coeff[:16], read_coeff)
    first_seg = jnp.broadcast_to(seg_row, (16, length)) == seg_cols[:16, :1]
    first_allowed = first_seg & (iota((16, length), 1) >= iota((16, length), 0))
    first_scores = jnp.where(first_allowed, first_scores, 0.0).astype(BF16)
    first_grad = dot_nn(first_scores, og_scaled[...])[:8]
    pre = pre[:8]
    gate = 1.0 / (1.0 + jnp.exp(-pre))
    pre_grad = first_grad * first_scale[:8] * gate * (1.0 + pre * (1.0 - gate))
    pre_grad = jnp.where(seg_cols[:8, :1] == seg_cols[:1, :1], pre_grad, 0.0)
    conv_rows = []
    for row in range(taps - 1):
        running = jnp.zeros((1, channels), F32)
        for k in range(taps - 1 - row, taps):
            position = row - (taps - 1) + k
            running = running + taps_ref[k : k + 1, :] * pre_grad[position : position + 1]
        conv_rows.append(
            jnp.where(own_head, jnp.broadcast_to(running, (heads, channels)), 0.0).astype(BF16)
        )
    placed = dot_nt(jnp.concatenate(conv_rows, axis=0), place).astype(BF16)
    for q in range(docs):
        cgrad_send[q] = placed[:, q * part_p : (q + 1) * part_p].reshape(
            taps - 1, heads, part_p
        )
    cgrad_copies = [
        doc_copy(3, j, cgrad_send.at[lax.rem(d + j, docs)], cgrad_recv.at[d])
        for j in range(1, docs)
    ]
    for copy in cgrad_copies:
        copy.start()
    stores.append(pltpu.make_async_copy(cgrad_send.at[d], cgrad_recv.at[d], store_sem.at[1]))
    stores[1].start()

    for copy in total_copies:
        copy.wait_recv()
    score_total = sums_of[:, :length]
    write_grad = dot_tn(score_total, read_coeff)
    read_grad = dot_nn(score_total, write_coeff) + sums_of[:, length:].astype(F32)
    cg = jnp.concatenate([write_grad, read_grad], axis=1).astype(BF16)
    product = dot_nn(tok_rows, cg).reshape(docs, out_rows, width)
    fin_send[...] = product.astype(BF16)
    fin_copies = [
        doc_copy(4, j, fin_send.at[lax.rem(d + j, docs)], fin_recv.at[j - 1])
        for j in range(1, docs)
    ]
    for copy in fin_copies:
        copy.start()
    fin_part[...] = product
    stores.append(pltpu.make_async_copy(fin_part.at[d], fin_own, store_sem.at[2]))
    stores[2].start()
    for copy in sgrad_copies + cgrad_copies + fin_copies:
        copy.wait_recv()
    for store in stores:
        store.wait()

    for copies in (
        conv_copies,
        coeff_copies,
        state_copies,
        gather_copies,
        sum_copies,
        sgrad_copies,
        cgrad_copies,
        total_copies,
        fin_copies,
    ):
        for copy in copies:
            copy.wait_send()


def finish_kernel(
    carry_hbm,
    own_hbm,
    recv_hbm,
    sgrad_hbm,
    cgrad_hbm,
    proj_out,
    state_out,
    conv_out,
    carry_ref,
    own_ref,
    recv_ref,
    sgrad_ref,
    cgrad_ref,
    load_sem,
):
    pairs = (
        (carry_hbm, carry_ref),
        (sgrad_hbm, sgrad_ref),
        (cgrad_hbm, cgrad_ref),
        (own_hbm, own_ref),
        (recv_hbm, recv_ref),
    )
    loads = [
        pltpu.make_async_copy(src, dst, load_sem.at[i]) for i, (src, dst) in enumerate(pairs)
    ]
    for load in loads:
        load.start()
    for load in loads:
        load.wait()
    slots = state_out.shape[0]
    for s in range(slots):
        row_of = jnp.int32(0)
        found = jnp.float32(0.0)
        for r in range(slots):
            hit = carry_ref[r] == s
            row_of = jnp.where(hit, r, row_of)
            found = jnp.where(hit, 1.0, found)
        state_out[s] = (sgrad_ref[row_of].astype(F32) * found).astype(BF16)
        conv_out[s] = (cgrad_ref[row_of].astype(F32) * found).astype(BF16)
    result = own_ref[...]
    for j in range(recv_ref.shape[0]):
        result = result + recv_ref[j].astype(F32)
    proj_out[...] = result


def device_part(docs, parts, *args):
    (
        tokens_in,
        mix_in,
        step_size,
        doc_ids,
        out_grad,
        proj_weight,
        conv_weight,
        decay_rate,
        carried_state,
        carried_conv,
        carry_from,
    ) = args
    rows_dev, length, model_width = tokens_in.shape
    channels = mix_in.shape[2]
    heads = step_size.shape[2]
    depth, width = proj_weight.shape
    slots, _, part_p, nstate = carried_state.shape
    taps = conv_weight.shape[0]
    out_rows = model_width // (docs * parts)
    block = length // parts
    aligned = (
        rows_dev == 1
        and slots == docs
        and part_p % 16 == 0
        and heads % 16 == 0
        and 2 * heads <= 128
        and block % 16 == 0
        and length % 128 == 0
        and out_rows % 128 == 0
        and depth % 128 == 0
        and nstate == 128
        and channels % 128 == 0
        and taps <= 8
    )
    if not aligned:
        return shards(*args)
    vmem = pl.BlockSpec(memory_space=pltpu.VMEM)
    hbm = pl.BlockSpec(memory_space=pltpu.HBM)
    landed = (
        jax.ShapeDtypeStruct((out_rows, width), F32),
        jax.ShapeDtypeStruct((docs - 1, out_rows, width), BF16),
        jax.ShapeDtypeStruct(carried_state.shape, BF16),
        jax.ShapeDtypeStruct(carried_conv.shape, BF16),
    )
    buffers = pl.pallas_call(
        functools.partial(layer_kernel, docs, parts),
        out_shape=landed,
        in_specs=[hbm] * 11,
        out_specs=(hbm,) * 4,
        scratch_shapes=[
            pltpu.SMEM(carry_from.shape, jnp.int32),
            pltpu.VMEM((length, channels), BF16),
            pltpu.VMEM((heads, length), F32),
            pltpu.VMEM(doc_ids.shape, jnp.int32),
            pltpu.VMEM((length, channels), BF16),
            pltpu.VMEM(proj_weight.shape, BF16),
            pltpu.VMEM(conv_weight.shape, F32),
            pltpu.VMEM((1, heads), F32),
            pltpu.VMEM(carried_state.shape, BF16),
            pltpu.VMEM(carried_conv.shape, BF16),
            pltpu.VMEM((length, depth), BF16),
            pltpu.VMEM((length, docs * out_rows), BF16),
            pltpu.VMEM((length, width), F32),
            pltpu.VMEM((parts, block, width), F32),
            pltpu.VMEM((length, width), BF16),
            pltpu.VMEM((length, length + nstate), F32),
            pltpu.VMEM((length, length + nstate), BF16),
            pltpu.VMEM((parts, block, length + nstate), BF16),
            pltpu.VMEM((length, length + nstate), BF16),
            pltpu.VMEM((slots, heads, part_p, nstate), BF16),
            pltpu.VMEM((heads, docs, part_p, nstate), BF16),
            pltpu.VMEM((slots, taps - 1, heads, part_p), BF16),
            pltpu.VMEM((docs, taps - 1, heads, part_p), BF16),
            pltpu.VMEM((heads, docs, part_p, nstate), BF16),
            pltpu.VMEM((docs, taps - 1, heads, part_p), BF16),
            pltpu.VMEM((docs, out_rows, width), F32),
            pltpu.VMEM((docs, out_rows, width), BF16),
            pltpu.VMEM((length + 8, channels), F32),
            pltpu.VMEM((length + 8, 128), F32),
            pltpu.VMEM((length, channels), BF16),
            pltpu.VMEM((length, channels), BF16),
            pltpu.VMEM((16, channels), F32),
            pltpu.VMEM((taps - 1, length, 128), F32),
            pltpu.VMEM((2, length, channels), F32),
            pltpu.SemaphoreType.DMA((11 + docs,)),
            pltpu.SemaphoreType.DMA((3,)),
            pltpu.SemaphoreType.DMA((4, parts)),
            pltpu.SemaphoreType.DMA((4, parts)),
            pltpu.SemaphoreType.DMA((5, docs)),
            pltpu.SemaphoreType.DMA((5, docs)),
        ],
        compiler_params=pltpu.CompilerParams(
            collective_id=0, has_side_effects=True, vmem_limit_bytes=60 * 1024 * 1024
        ),
        cost_estimate=pl.CostEstimate(
            flops=2 * length * channels * length * 4, bytes_accessed=4 << 20, transcendentals=0
        ),
    )(
        carry_from,
        tokens_in,
        mix_in,
        jnp.swapaxes(step_size, 1, 2),
        doc_ids,
        out_grad,
        proj_weight,
        conv_weight,
        decay_rate.reshape(1, heads),
        carried_state,
        carried_conv,
    )
    return pl.pallas_call(
        finish_kernel,
        out_shape=(
            jax.ShapeDtypeStruct((out_rows, width), F32),
            jax.ShapeDtypeStruct(carried_state.shape, BF16),
            jax.ShapeDtypeStruct(carried_conv.shape, BF16),
        ),
        in_specs=[hbm] * 5,
        out_specs=(vmem,) * 3,
        scratch_shapes=[pltpu.SMEM(carry_from.shape, jnp.int32)]
        + [pltpu.VMEM(leaf.shape, leaf.dtype) for leaf in landed]
        + [pltpu.SemaphoreType.DMA((5,))],
        compiler_params=pltpu.CompilerParams(vmem_limit_bytes=60 * 1024 * 1024),
    )(carry_from, *buffers)


def solution(mesh):
    return jax.shard_map(
        functools.partial(device_part, mesh.shape["doc"], mesh.shape["fsdp"]),
        mesh=mesh,
        in_specs=(
            P("doc", None, None),
            P("doc", None, "fsdp"),
            P("doc", None, "fsdp"),
            P("doc", None),
            P("doc", None, "fsdp"),
            P("fsdp", None),
            P(None, "fsdp"),
            P("fsdp"),
            P(None, "fsdp", "doc", None),
            P(None, None, "fsdp", "doc"),
            P(),
        ),
        out_specs=(
            P(("doc", "fsdp"), None),
            P(None, "fsdp", "doc", None),
            P(None, None, "fsdp", "doc"),
        ),
        check_vma=False,
    )
```
